256 devices in a mesh: grp: 8 (over z), seg: 32 (over x, y, core).
Axes of the slice: x: 4, y: 4, z: 8, core: 2. Of those that a mesh axis runs over, the one named last changes fastest.
Arguments:
- tokens: bfloat16 [98304, 768], P(('grp', 'seg')), may hold values from -6 to 6
- doc_segments: int32 [8, 6], P('grp'), may hold values from 1 to 48, 96 in all within a row
- local_qkv: bfloat16 [768, 2304], P('seg'), may hold values from -0.21875 to 0.21875
- local_out: bfloat16 [768, 768], P('seg'), may hold values from -0.875 to 0.875
- local_up: bfloat16 [768, 3072], P('seg'), may hold values from -0.21875 to 0.21875
- local_down: bfloat16 [3072, 768], P('seg'), may hold values from -0.109375 to 0.109375
- local_bias: bfloat16 [6, 768], P(None, 'seg'), may hold values from -1.5 to 1.5
- local_upbias: bfloat16 [3072], P('seg'), may hold values from -1.5 to 1.5
- local_gains: bfloat16 [2, 768], P(None, 'seg'), may hold values from 0.5 to 1.5
- cross_qkv: bfloat16 [768, 2304], P('seg'), may hold values from -0.21875 to 0.21875
- cross_out: bfloat16 [768, 768], P('seg'), may hold values from -0.625 to 0.625
- cross_up: bfloat16 [768, 3072], P('seg'), may hold values from -0.21875 to 0.21875
- cross_down: bfloat16 [3072, 768], P('seg'), may hold values from -0.109375 to 0.109375
- cross_bias: bfloat16 [6, 768], P(None, 'seg'), may hold values from -1.5 to 1.5
- cross_upbias: bfloat16 [3072], P('seg'), may hold values from -1.5 to 1.5
- cross_gains: bfloat16 [2, 768], P(None, 'seg'), may hold values from 0.5 to 1.5
- pos_table: bfloat16 [64, 768], P('seg'), may hold values from -3 to 3
- cotangent: bfloat16 [98304, 768], P(('grp', 'seg')), may hold values from -6 to 6
Outputs:
- layer_out: bfloat16 [98304, 768], P(('grp', 'seg'))
- tokens_grad: float32 [98304, 768], P(('grp', 'seg'))
- local_qkv_grad: float32 [768, 2304], P('seg')
- local_out_grad: float32 [768, 768], P('seg')
- local_up_grad: float32 [768, 3072], P('seg')
- local_down_grad: float32 [3072, 768], P('seg')
- local_bias_grad: float32 [6, 768], P(None, 'seg')
- local_upbias_grad: float32 [3072], P('seg')
- local_gains_grad: float32 [2, 768], P(None, 'seg')
- cross_qkv_grad: float32 [768, 2304], P('seg')
- cross_out_grad: float32 [768, 768], P('seg')
- cross_up_grad: float32 [768, 3072], P('seg')
- cross_down_grad: float32 [3072, 768], P('seg')
- cross_bias_grad: float32 [6, 768], P(None, 'seg')
- cross_upbias_grad: float32 [3072], P('seg')
- cross_gains_grad: float32 [2, 768], P(None, 'seg')
- pos_table_grad: float32 [64, 768], P('seg')
The draws below stay inside these ranges and needn't reach their ends.
Inputs may be any that keep to these rules, and one draw needn't show every extreme that they name: `doc_segments`: each row lists the segment counts of a group's 6 documents in document order; a row sums to 96 and its largest count is exactly 48.
All inputs are finite; a program needn't handle non-finite values.
Results may differ from the reference program's by a relative error of at most 0.029.
Values may be sent and summed in bfloat16 or wider, within the bound.
A program may use at most 128 MiB of HBM per device.

```python
import math
import jax
import jax.numpy as jnp
import numpy as np
from jax import lax

D = 768
H = 12
HD = 64
FF = 3072
SEG_LEN = 128
POSN = 64
S_DEV = 3
SEGS = 96
MOST = 48
DOCS = 6
TOKENS = 98304
N_GRP = 8
N_SEG = 32


def block_levels(rng, dims, shards, smallest, top_value):
    gain, own = 1.0, jax.random.fold_in(rng, 6)
    for dim, shards_of in shards:
        draws = jnp.exp(jax.random.uniform(jax.random.fold_in(own, dim), (shards_of,), jnp.float32, smallest / len(shards), top_value / len(shards)))
        gain = gain * jnp.repeat(draws, dims[dim] // shards_of).reshape([-1 if axis == dim else 1 for axis in range(len(dims))])
    return gain


def profile(count, total, reach, skew):
    loads = [(1 << 20) // math.isqrt(standing ** skew) + 1 for standing in range(2, count + 1)]
    surplus, counts = total - reach - (count - 1), [1] * (count - 1)
    while surplus > 0:
        movable = [i for i in range(count - 1) if counts[i] < reach]
        mass, remaining = sum([loads[i] for i in movable]), surplus
        for i in movable:
            addition = min(reach - counts[i], max(1, remaining * loads[i] // mass), surplus)
            counts[i] = counts[i] + addition
            surplus = surplus - addition
    return np.array([reach] + counts)


def uneven(key, number_of, total, bound, lean):
    if number_of == 2:
        one = jax.random.randint(key, (), max(1, total - bound), min(bound, total - 1) + 1)
        return jnp.stack([one, total - one])
    tallies = jnp.asarray(profile(number_of, total, bound, lean), jnp.int32)
    pairs = (number_of - 1) // 2
    source_of, sink = tallies[1:1 + 2 * pairs:2], tallies[2:2 + 2 * pairs:2]
    margin = jnp.minimum(source_of - 1, bound - sink)
    passed = jax.random.randint(jax.random.fold_in(key, 1), (pairs,), 0, 1 << 20) % (margin + 1)
    tallies = tallies.at[1:1 + 2 * pairs:2].set(source_of - passed).at[2:2 + 2 * pairs:2].set(sink + passed)
    return tallies[jax.random.permutation(jax.random.fold_in(key, 2), number_of)]


def normal_values(own_key, shape, deviation, limit, split=(), kind=jnp.bfloat16):
    level = block_levels(own_key, shape, split, -0.22, 0.18) if split else 1.0
    drawn = jax.random.normal(own_key, shape, jnp.float32) * deviation * level
    return jnp.minimum(jnp.maximum(drawn, -limit), limit).astype(kind)


def setup_inputs(seed: int = 0) -> dict:
    streams_of = jax.random.split(jax.random.key(seed), 19)
    return {
        "tokens": normal_values(streams_of[0], (TOKENS, D), 1.0, 6.0, ((0, 256),)),
        "doc_segments": jax.vmap(lambda own: uneven(own, DOCS, SEGS, MOST, 2))(jax.random.split(streams_of[1], N_GRP)).reshape((N_GRP, DOCS)).astype(jnp.int32),
        "local_qkv": normal_values(streams_of[2], (D, 3 * D), D ** -0.5, 0.21875, ((0, 32),)),
        "local_out": normal_values(streams_of[3], (D, D), (D // 16) ** -0.5, 0.875, ((0, 32),)),
        "local_up": normal_values(streams_of[4], (D, FF), D ** -0.5, 0.21875, ((0, 32),)),
        "local_down": normal_values(streams_of[5], (FF, D), FF ** -0.5, 0.109375, ((0, 32),)),
        "local_bias": normal_values(streams_of[6], (6, D), 0.3, 1.5, ((1, 32),)),
        "local_upbias": normal_values(streams_of[7], (FF,), 0.3, 1.5, ((0, 32),)),
        "local_gains": jnp.clip(1.0 + 0.1 * jax.random.normal(streams_of[8], (2, D), jnp.float32), 0.5, 1.5).astype(jnp.bfloat16),
        "cross_qkv": normal_values(streams_of[9], (D, 3 * D), D ** -0.5, 0.21875, ((0, 32),)),
        "cross_out": normal_values(streams_of[10], (D, D), (D // 8) ** -0.5, 0.625, ((0, 32),)),
        "cross_up": normal_values(streams_of[11], (D, FF), D ** -0.5, 0.21875, ((0, 32),)),
        "cross_down": normal_values(streams_of[12], (FF, D), FF ** -0.5, 0.109375, ((0, 32),)),
        "cross_bias": normal_values(streams_of[13], (6, D), 0.3, 1.5, ((1, 32),)),
        "cross_upbias": normal_values(streams_of[14], (FF,), 0.3, 1.5, ((0, 32),)),
        "cross_gains": jnp.clip(1.0 + 0.1 * jax.random.normal(streams_of[15], (2, D), jnp.float32), 0.5, 1.5).astype(jnp.bfloat16),
        "pos_table": normal_values(streams_of[16], (POSN, D), 0.5, 3.0, ((0, 32),)),
        "cotangent": normal_values(streams_of[17], (TOKENS, D), 1.0, 6.0, ((0, 256),)),
    }


HIGHEST = lax.Precision.HIGHEST

@jax.custom_vjp
def low(v):
    return lax.optimization_barrier(v.astype(jnp.bfloat16)).astype(jnp.float32)

@jax.custom_vjp
def low_back(v):
    return v

def low_keep(v):
    return (low(v), None)

def low_pass(kept, grad):
    return (grad,)

def back_keep(v):
    return (v, None)

def back_low(kept, grad):
    return (low(grad),)
low.defvjp(low_keep, low_pass)
low_back.defvjp(back_keep, back_low)

def layer_norm(values, gain_vec, shift_vec):
    center = values - lax.optimization_barrier(jnp.mean(values, axis=-1, keepdims=True))
    spread = lax.optimization_barrier(jnp.mean(center * center, axis=-1, keepdims=True))
    return center * lax.rsqrt(spread + 1e-05) * gain_vec + shift_vec

def product(left_side, right_side):
    return jnp.matmul(left_side, right_side, precision=HIGHEST)

def block_forward(inputs, params, allowed):
    w_qkv, w_out, w_up, w_down, biases, up_bias, gains = params
    lead, height = (inputs.shape[0], inputs.shape[1])
    joined = product(inputs, w_qkv)
    queries = low_back(low(joined[..., :D] + biases[0]))
    key_rows = low_back(low(joined[..., D:2 * D]))
    value_rows = low_back(low(joined[..., 2 * D:] + biases[1]))
    four_shape = (lead, height, H, HD)
    scores = jnp.einsum('bqhe,bkhe->bhqk', queries.reshape(four_shape), key_rows.reshape(four_shape), precision=HIGHEST) * (1.0 / math.sqrt(HD))
    scores = low_back(scores)
    if allowed is not None:
        scores = jnp.where(allowed[:, None, :, :], scores, -1e+30)
    row_max = lax.optimization_barrier(jnp.max(scores, axis=-1, keepdims=True))
    exp_scores = jnp.exp(scores - row_max)
    weights_f = low(exp_scores / lax.optimization_barrier(jnp.sum(exp_scores, axis=-1, keepdims=True)))
    mixed_rows = jnp.einsum('bhqk,bkhe->bqhe', weights_f, value_rows.reshape(four_shape), precision=HIGHEST)
    mixed_rows = low_back(low(mixed_rows.reshape(lead, height, D)))
    attn_out = low_back(product(mixed_rows, w_out) + biases[2])
    first_norm = low(layer_norm(inputs + attn_out, gains[0], biases[3]))
    up_pre = low_back(product(first_norm, w_up) + up_bias)
    active = low(jax.nn.gelu(up_pre, approximate=False))
    down_out = low_back(product(active, w_down) + biases[4])
    return layer_norm(first_norm + down_out, gains[1], biases[5])

def segment_block(seg_block, params):
    return block_forward(seg_block, params, None)

def slot_layout(doc_segments):
    slot_ids = jnp.arange(SEGS, dtype=jnp.int32)
    doc_order = slot_ids % S_DEV * N_SEG + slot_ids // S_DEV
    doc_ends = jnp.cumsum(doc_segments, axis=1).astype(jnp.int32)
    doc_starts = doc_ends - doc_segments
    member_of = (doc_order[None, :, None] >= doc_starts[:, None, :]) & (doc_order[None, :, None] < doc_ends[:, None, :])
    numbers = jnp.arange(DOCS, dtype=jnp.int32)
    doc_ids = lax.optimization_barrier(jnp.sum(jnp.where(member_of, numbers[None, None, :], 0), axis=2)).astype(jnp.int32)
    seg_place = doc_order[None, :] - lax.optimization_barrier(jnp.sum(jnp.where(member_of, doc_starts[:, None, :], 0), axis=2))
    return (doc_ids, seg_place.astype(jnp.int32))

def forward(inputs, local_set, cross_set, table, doc_ids, seg_place):
    per_step = math.gcd(N_GRP * SEGS, max(1, 4096 // SEG_LEN))
    blocks = inputs.reshape(N_GRP * SEGS // per_step, per_step, SEG_LEN, D)
    checked = jax.checkpoint(segment_block)
    outputs = lax.map(lambda seg_block: checked(seg_block, local_set), blocks)
    outputs = outputs.reshape(N_GRP, SEGS, SEG_LEN, D)
    cross_in = low(outputs[:, :, 0, :] + table[seg_place])
    allowed = doc_ids[:, :, None] == doc_ids[:, None, :]
    cross_result = block_forward(cross_in, cross_set, allowed)
    outputs = outputs.at[:, :, 0, :].set(cross_result)
    return outputs.reshape(TOKENS, D)

def to_float(argument):
    return argument.astype(jnp.float32)

def reference(tokens, doc_segments, local_qkv, local_out, local_up, local_down, local_bias, local_upbias, local_gains, cross_qkv, cross_out, cross_up, cross_down, cross_bias, cross_upbias, cross_gains, pos_table, cotangent):
    doc_ids, seg_place = slot_layout(doc_segments)
    local_set = tuple((to_float(argument) for argument in (local_qkv, local_out, local_up, local_down, local_bias, local_upbias, local_gains)))
    cross_set = tuple((to_float(argument) for argument in (cross_qkv, cross_out, cross_up, cross_down, cross_bias, cross_upbias, cross_gains)))

    def closed_forward(inputs, local_arg, cross_arg, table):
        return forward(inputs, local_arg, cross_arg, table, doc_ids, seg_place)
    result, pullback = jax.vjp(closed_forward, to_float(tokens), local_set, cross_set, to_float(pos_table))
    grad_tokens, grad_local, grad_cross, grad_table = pullback(to_float(cotangent))
    return (result.astype(jnp.bfloat16), grad_tokens, grad_local[0], grad_local[1], grad_local[2], grad_local[3], grad_local[4], grad_local[5], grad_local[6], grad_cross[0], grad_cross[1], grad_cross[2], grad_cross[3], grad_cross[4], grad_cross[5], grad_cross[6], grad_table)
```

```python
import functools
import math

import jax
import jax.numpy as jnp
from jax import lax
from jax.experimental import pallas as pl
from jax.experimental.pallas import tpu as pltpu
from jax.sharding import PartitionSpec as P

H = 12
HD = 64
SEG_LEN = 128
POSN = 64
HIGHEST = lax.Precision.HIGHEST
MESH = pl.DeviceIdType.MESH
F32, BF16 = jnp.float32, jnp.bfloat16
D = 768
N_OWN, N_PAIR, N_SEG = 12, 6, 32
RSQ2 = 1.0 / math.sqrt(2.0)
RS2PI = 1.0 / math.sqrt(2.0 * math.pi)


def dot(a, b):
    return lax.dot_general(a, b, (((1,), (0,)), ((), ())), preferred_element_type=F32)
def dot_bt(a, b):
    return lax.dot_general(a, b, (((1,), (1,)), ((), ())), preferred_element_type=F32)
def dot_at(a, b):
    return lax.dot_general(a, b, (((0,), (0,)), ((), ())), preferred_element_type=F32)

def rcopy(src, dst, ssem, rsem, seg):
    return pltpu.make_async_remote_copy(src_ref=src, dst_ref=dst, send_sem=ssem, recv_sem=rsem,
                                        device_id={"seg": seg}, device_id_type=MESH)

def take(ref, sem):
    pltpu.make_async_copy(ref, ref, sem).wait()

def send_to(me, target, src, dst, ssem, rsem):
    @pl.when(target != me)
    def _():
        rcopy(src, dst, ssem, rsem, target).start()
    @pl.when(target == me)
    def _():
        pltpu.make_async_copy(src, dst, rsem).start()

def norm(v):
    center = v - jnp.mean(v, axis=-1, keepdims=True)
    rstd = lax.rsqrt(jnp.mean(center * center, axis=-1, keepdims=True) + 1e-05)
    return center * rstd, rstd

def norm_back(grad, n, rstd, gain):
    dn = grad * gain
    return rstd * (dn - jnp.mean(dn, axis=-1, keepdims=True) - n * jnp.mean(dn * n, axis=-1, keepdims=True))

def gelu(u):
    return u * (0.5 + 0.5 * lax.erf(u * RSQ2))

def gelu_grad(u):
    return 0.5 + 0.5 * lax.erf(u * RSQ2) + u * (RS2PI * jnp.exp(-0.5 * u * u))

def rows8(value):
    return value.reshape(value.shape[0] // 8, 8, value.shape[1])

def flat8(value):
    v = value.astype(F32)
    return v.reshape(v.shape[0] * v.shape[1], v.shape[2])

def owner_seg(k):
    return 2 * k
def pair_seg(p):
    return 4 * p + 1
def pair_first(p):
    return 5 * (p % 3) + 16 * (p // 3)

dma = pltpu.SemaphoreType.DMA
SCRATCH = dict(
    xup=pltpu.VMEM((32, 24, 128), BF16), xqkv=pltpu.VMEM((32, 3, 24, 128), BF16), xout=pltpu.VMEM((6, 24, 768), BF16),
    wup=pltpu.VMEM((768, 128), BF16), wqkv=pltpu.VMEM((768, 384), BF16), wout=pltpu.VMEM((128, 768), BF16),
    wout_f=pltpu.VMEM((144, 768), F32), wdn=pltpu.VMEM((128, 768), BF16),
    msg=pltpu.VMEM((8, 768), BF16), x1=pltpu.VMEM((32, 8, 768), BF16),
    own=pltpu.VMEM((8, 8, 768), F32),
    rst=pltpu.VMEM((2, 8, 128), F32),
    xall=pltpu.VMEM((96, 768), BF16), q=pltpu.VMEM((3, 96, 128), BF16), o=pltpu.VMEM((96, 128), BF16),
    af=pltpu.VMEM((2, 96, 96), F32),
    p2=pltpu.VMEM((12, 8, 768), BF16), g2=pltpu.VMEM((6, 8, 768), BF16),
    p3=pltpu.VMEM((8, 768), BF16), g3=pltpu.VMEM((12, 8, 768), BF16),
    p4=pltpu.VMEM((12, 8, 768), BF16), g46=pltpu.VMEM((64, 8, 768), BF16),
    p5=pltpu.VMEM((2, 8, 768), BF16), g5=pltpu.VMEM((12, 2, 8, 768), BF16),
    p6=pltpu.VMEM((12, 8, 768), BF16),
    p7=pltpu.VMEM((8, 768), BF16), g7=pltpu.VMEM((12, 8, 768), BF16),
    p7f=pltpu.VMEM((8, 768), F32), g7f=pltpu.VMEM((2, 8, 768), F32),
    p8=pltpu.VMEM((12, 8, 768), BF16), g8=pltpu.VMEM((6, 2, 8, 768), BF16),
    u=pltpu.VMEM((96, 128), F32), gact=pltpu.VMEM((96, 128), BF16),
    fall=pltpu.VMEM((96, 768), BF16), dd=pltpu.VMEM((96, 768), BF16), du=pltpu.VMEM((96, 128), BF16),
    dq=pltpu.VMEM((96, 384), BF16), de=pltpu.VMEM((96, 768), BF16),
    pu=pltpu.VMEM((32, 24, 128), BF16), pq=pltpu.VMEM((32, 24, 384), BF16), po=pltpu.VMEM((6, 24, 768), BF16),
    po_f=pltpu.VMEM((144, 768), F32), go=pltpu.VMEM((2, 24, 768), BF16),
    cs=dma((16,)), cr=dma((16,)), c7=dma((32,)),
)


class Cross:
    def __init__(self, r, args):
        self.r, self.a = r, args
        self.me = lax.axis_index("seg")
        self.is_owner = (self.me % 2 == 0) & (self.me < 24)
        self.k = self.me // 2
        self.is_pair = (self.me % 4 == 1) & (self.me < 24)
        self.p = self.me // 4

    def sem(self, e):
        return self.r["cs"].at[e], self.r["cr"].at[e]

    def loop(self, n, fn):
        def body(i, _):
            fn(i)
            return 0
        lax.fori_loop(0, n, body, 0)

    def reshard(self):
        r, a, me = self.r, self.a, self.me
        s0, r0 = self.sem(0)
        s1, r1 = self.sem(1)
        s2, r2 = self.sem(2)
        self.loop(32, lambda t: send_to(me, t, a["cup"].at[t], r["xup"].at[me], s0, r0))
        def to_pair(p):
            for j in range(3):
                col = pl.ds(pl.multiple_of(768 * j + 128 * p, 128), 128)
                send_to(me, pair_seg(p), a["cqkv"].at[:, col], r["xqkv"].at[me, j], s1, r1)
            first = pair_first(p)
            @pl.when((me >= first) & (me < first + 6))
            def _():
                send_to(me, pair_seg(p), a["cout"], r["xout"].at[me - first], s2, r2)
        self.loop(6, to_pair)
        r["wdn"][0:96, :] = a["cdown"][...]
        r["wdn"][96:128, :] = jnp.zeros((32, 768), BF16)

    def reshard_end(self):
        r = self.r
        take(r["xup"], self.r["cr"].at[0])
        r["wup"][...] = r["xup"][...].astype(F32).reshape(768, 128).astype(BF16)
        @pl.when(self.is_pair)
        def _():
            take(r["xqkv"], self.r["cr"].at[1])
            for j in range(3):
                r["wqkv"][:, 128 * j:128 * (j + 1)] = r["xqkv"][:, j].astype(F32).reshape(768, 128).astype(BF16)
            take(r["xout"], self.r["cr"].at[2])
            r["wout_f"][...] = r["xout"][...].astype(F32).reshape(144, 768)
            off = pl.multiple_of(8 * (self.p % 3), 8)
            r["wout"][...] = r["wout_f"][pl.ds(off, 128), :].astype(BF16)

    def layout(self, shape, axis, slots):
        pos = (slots % 3) * 32 + slots // 3
        doc = jnp.zeros(shape, jnp.int32)
        begin = jnp.zeros(shape, jnp.int32)
        end = jnp.int32(0)
        for d in range(6):
            count = self.a["doc"][0, d]
            begin = jnp.where(pos >= end, end, begin)
            doc = jnp.where(pos >= end, d, doc)
            end = end + count
        return doc, pos - begin

    def start(self, z0, dy0):
        r, a, me = self.r, self.a, self.me
        slots = me * 3 + lax.broadcasted_iota(jnp.int32, (8, 64), 0)
        _, place = self.layout((8, 64), 0, jnp.minimum(slots, 95))
        row = lax.broadcasted_iota(jnp.int32, (8, 64), 0)
        hot = ((place == lax.broadcasted_iota(jnp.int32, (8, 64), 1)) & (row < 3)).astype(BF16)
        cross_in = z0 + dot(hot, a["pos"][...])
        rowd = lax.broadcasted_iota(jnp.int32, (8, 768), 0)
        both = jnp.where(rowd < 3, cross_in, pltpu.roll(dy0, 3, 0))
        r["msg"][...] = jnp.where(rowd < 6, both, 0.0).astype(BF16)
        ss, rs = self.sem(3)
        self.loop(6, lambda p: send_to(me, pair_seg(p), r["msg"], r["x1"].at[me], ss, rs))
        self.loop(12, lambda k: send_to(me, owner_seg(k), r["msg"], r["x1"].at[me], ss, rs))

    def pick(self, n, first, base):
        row = lax.broadcasted_iota(jnp.int32, (n, 256), 0) + first
        col = lax.broadcasted_iota(jnp.int32, (n, 256), 1)
        return (col == (row // 3) * 8 + row % 3 + base).astype(BF16)

    def attention(self):
        r, a, me = self.r, self.a, self.me
        ss, rs = self.sem(4)
        @pl.when(self.is_pair)
        def _():
            take(r["x1"], self.r["cr"].at[3])
            msgs = flat8(r["x1"][...]).astype(BF16)
            xall = dot(self.pick(96, 0, 0), msgs).astype(BF16)
            r["xall"][...] = xall
            col = pl.ds(pl.multiple_of(128 * self.p, 128), 128)
            joined = dot(xall, r["wqkv"][...])
            q = (joined[:, 0:128] + a["cb"][0:1, col]).astype(BF16)
            k = joined[:, 128:256].astype(BF16)
            v = (joined[:, 256:384] + a["cb"][1:2, col]).astype(BF16)
            r["q"][0], r["q"][1], r["q"][2] = q, k, v
            doc_r, _ = self.layout((96, 96), 0, lax.broadcasted_iota(jnp.int32, (96, 96), 0))
            doc_c, _ = self.layout((96, 96), 0, lax.broadcasted_iota(jnp.int32, (96, 96), 1))
            allowed = doc_r == doc_c
            lane = lax.broadcasted_iota(jnp.int32, (96, 128), 1)
            outs = []
            for h in range(2):
                mine = (lane < 64) if h == 0 else (lane >= 64)
                qh = jnp.where(mine, q, jnp.zeros_like(q))
                s = jnp.where(allowed, dot_bt(qh, k) * 0.125, -1e30)
                e = jnp.exp(s - jnp.max(s, axis=-1, keepdims=True))
                w = e / jnp.sum(e, axis=-1, keepdims=True)
                r["af"][h] = w
                outs.append(dot(w.astype(BF16), v))
            o = jnp.where(lane < 64, outs[0], outs[1]).astype(BF16)
            r["o"][...] = o
            r["p2"][...] = rows8(dot(o, r["wout"][...])).astype(BF16)
            self.loop(12, lambda k: send_to(me, owner_seg(k), r["p2"].at[k], r["g2"].at[self.p], ss, rs))

    def first_norm(self):
        r, a, me = self.r, self.a, self.me
        ss, rs = self.sem(5)
        @pl.when(self.is_owner)
        def _():
            take(r["x1"], self.r["cr"].at[3])
            msgs = flat8(r["x1"][...]).astype(BF16)
            x = dot(self.pick(8, 8 * self.k, 0), msgs)
            r["own"][1] = dot(self.pick(8, 8 * self.k, 3), msgs)
            take(r["g2"], self.r["cr"].at[4])
            total = jnp.sum(r["g2"][...].astype(F32), axis=0)
            n, rstd = norm(x + (total + a["cb"][2:3, :]))
            r["own"][2] = n
            r["rst"][0] = jnp.broadcast_to(rstd, (8, 128))
            f = (n * a["cb"][6:7, :] + a["cb"][3:4, :]).astype(BF16)
            r["p3"][...] = f
            self.loop(32, lambda t: send_to(me, t, r["p3"], r["g3"].at[self.k], ss, rs))

    def mlp(self):
        r, a, me = self.r, self.a, self.me
        ss, rs = self.sem(6)
        take(r["g3"], self.r["cr"].at[5])
        f = flat8(r["g3"][...]).astype(BF16)
        r["fall"][...] = f
        u = dot(f, r["wup"][...]) + a["cupb"][0:1, :]
        r["u"][...] = u
        g = gelu(u).astype(BF16)
        r["gact"][...] = g
        r["p4"][...] = rows8(dot(g, r["wdn"][...])).astype(BF16)
        self.loop(12, lambda k: send_to(me, owner_seg(k), r["p4"].at[k], r["g46"].at[me], ss, rs))

    def second_norm(self):
        r, a, me = self.r, self.a, self.me
        ss, rs = self.sem(7)
        @pl.when(self.is_owner)
        def _():
            take(r["g46"].at[pl.ds(0, 32)], self.r["cr"].at[6])
            total = jnp.sum(r["g46"][0:32].astype(F32), axis=0)
            n, rstd = norm(r["p3"][...].astype(F32) + (total + a["cb"][4:5, :]))
            y = n * a["cb"][7:8, :] + a["cb"][5:6, :]
            dy = r["own"][1]
            dr2 = norm_back(dy, n, rstd, a["cb"][7:8, :])
            r["own"][3] = n
            r["own"][4] = dr2
            r["p5"][0] = dr2.astype(BF16)
            r["p5"][1] = y.astype(BF16)
            self.loop(32, lambda t: send_to(me, t, r["p5"], r["g5"].at[self.k], ss, rs))

    def mlp_back(self):
        r, a, me = self.r, self.a, self.me
        ss, rs = self.sem(8)
        take(r["g5"], self.r["cr"].at[7])
        dd = flat8(r["g5"][:, 0]).astype(BF16)
        r["dd"][...] = dd
        du = (dot_bt(dd, r["wdn"][...]) * gelu_grad(r["u"][...])).astype(BF16)
        r["du"][...] = du
        r["p6"][...] = rows8(dot_bt(du, r["wup"][...])).astype(BF16)
        self.loop(12, lambda k: send_to(me, owner_seg(k), r["p6"].at[k], r["g46"].at[32 + me], ss, rs))

    def window(self, seg):
        return jnp.minimum((3 * seg) // 8, 10)

    def first_norm_back(self):
        r, a, me = self.r, self.a, self.me
        ss, rs = self.sem(9)
        fs, fr = self.sem(10)
        @pl.when(self.is_owner)
        def _():
            take(r["g46"].at[pl.ds(32, 32)], self.r["cr"].at[8])
            df = jnp.sum(r["g46"][32:64].astype(F32), axis=0) + r["own"][4]
            r["own"][5] = df
            dr1 = norm_back(df, r["own"][2], r["rst"][0][:, 0:1], a["cb"][6:7, :])
            r["p7"][...] = dr1.astype(BF16)
            self.loop(6, lambda p: send_to(me, pair_seg(p), r["p7"], r["g7"].at[self.k], ss, rs))
            r["p7f"][...] = dr1
            def one(t):
                w = self.window(t)
                @pl.when((w == self.k) | (w + 1 == self.k))
                def _():
                    send_to(me, t, r["p7f"], r["g7f"].at[self.k - w], r["c7"].at[t], fr)
            self.loop(32, one)

    def attention_back(self):
        r, a, me = self.r, self.a, self.me
        ss, rs = self.sem(11)
        @pl.when(self.is_pair)
        def _():
            take(r["g7"], self.r["cr"].at[9])
            de = flat8(r["g7"][...]).astype(BF16)
            r["de"][...] = de
            do = dot_bt(de, r["wout"][...]).astype(BF16)
            q, k, v = r["q"][0], r["q"][1], r["q"][2]
            lane = lax.broadcasted_iota(jnp.int32, (96, 128), 1)
            dqs, dks, dvs = [], [], []
            for h in range(2):
                mine = (lane < 64) if h == 0 else (lane >= 64)
                doh = jnp.where(mine, do, jnp.zeros_like(do))
                w = r["af"][h]
                da = dot_bt(doh, v)
                ds = (w * (da - jnp.sum(w * da, axis=-1, keepdims=True))).astype(BF16)
                dqs.append(dot(ds, k) * 0.125)
                dks.append(dot_at(ds, q) * 0.125)
                dvs.append(dot_at(w.astype(BF16), do))
            first = lane < 64
            r["dq"][:, 0:128] = jnp.where(first, dqs[0], dqs[1]).astype(BF16)
            r["dq"][:, 128:256] = jnp.where(first, dks[0], dks[1]).astype(BF16)
            r["dq"][:, 256:384] = jnp.where(first, dvs[0], dvs[1]).astype(BF16)
            r["p8"][...] = rows8(dot_bt(r["dq"][...], r["wqkv"][...])).astype(BF16)
            def one(t):
                send_to(me, t, r["p8"].at[pl.ds(self.window(t), 2)], r["g8"].at[self.p], ss, rs)
            self.loop(32, one)

    def finish(self):
        r = self.r
        take(r["g7f"], self.r["cr"].at[10])
        take(r["g8"], self.r["cr"].at[11])
        total = r["g7f"][...] + jnp.sum(r["g8"][...].astype(F32), axis=0)
        total = total.reshape(16, 768)
        shift = 3 * self.me - 8 * self.window(self.me)
        return pltpu.roll(total, 16 - shift, 0)[0:8]

    def output_rows(self):
        r = self.r
        w = self.window(self.me)
        y = r["g5"][pl.ds(w, 2), 1].astype(F32).reshape(16, 768)
        return pltpu.roll(y, 16 - (3 * self.me - 8 * w), 0)[0:8]

    def grads(self):
        r, a, me = self.r, self.a, self.me
        s0, r0 = self.sem(12)
        s1, r1 = self.sem(13)
        s2, r2 = self.sem(14)
        r["pu"][...] = dot_at(r["fall"][...], r["du"][...]).reshape(32, 24, 128).astype(BF16)
        self.loop(32, lambda t: send_to(me, t, r["pu"].at[t], a["gup"].at[me], s0, r0))
        a["gdn"][...] = dot_at(r["gact"][...], r["dd"][...])[0:96].astype(a["gdn"].dtype)
        @pl.when(self.is_pair)
        def _():
            r["pq"][...] = dot_at(r["xall"][...], r["dq"][...]).reshape(32, 24, 384).astype(BF16)
            self.loop(32, lambda t: send_to(me, t, r["pq"].at[t], a["gqkv"].at[self.p], s1, r1))
            r["po_f"][...] = jnp.zeros((144, 768), F32)
            off = pl.multiple_of(8 * (self.p % 3), 8)
            r["po_f"][pl.ds(off, 128), :] = dot_at(r["o"][...], r["de"][...])
            r["po"][...] = r["po_f"][...].reshape(6, 24, 768).astype(BF16)
            self.loop(6, lambda i: send_to(me, pair_first(self.p) + i, r["po"].at[i], r["go"].at[self.p % 2], s2, r2))
        sm = a["small"]
        sm[...] = jnp.zeros(sm.shape, F32)
        @pl.when(self.is_owner)
        def _():
            dr1, df, dr2, dy = r["p7"][...].astype(F32), r["own"][5], r["own"][4], r["own"][1]
            dd = r["p5"][0].astype(F32)
            for row, v in ((2, dr1), (3, df), (4, dd), (5, dy), (6, df * r["own"][2]), (7, dy * r["own"][3])):
                sm[row:row + 1, :] = jnp.sum(v, axis=0, keepdims=True)
        @pl.when(self.is_pair)
        def _():
            col = pl.ds(pl.multiple_of(128 * self.p, 128), 128)
            sm[0:1, col] = jnp.sum(r["dq"][:, 0:128].astype(F32), axis=0, keepdims=True)
            sm[1:2, col] = jnp.sum(r["dq"][:, 256:384].astype(F32), axis=0, keepdims=True)
        a["dc"][...] = jnp.broadcast_to(jnp.sum(r["du"][...].astype(F32), axis=0, keepdims=True), (8, 128))

    def grads_end(self):
        r, a, me = self.r, self.a, self.me
        take(a["gup"], r["cr"].at[12])
        take(a["gqkv"], r["cr"].at[13])
        seam = (me % 16 == 5) | (me % 16 == 10)
        m = me % 16
        p0 = 3 * (me // 16) + jnp.where(m > 10, 2, jnp.where(m > 5, 1, 0))
        @pl.when(seam)
        def _():
            take(r["go"], r["cr"].at[14])
            a["gout"][...] = (r["go"][0].astype(F32) + r["go"][1].astype(F32)).astype(a["gout"].dtype)
        @pl.when(jnp.logical_not(seam))
        def _():
            take(r["go"].at[0], r["cr"].at[14])
            a["gout"][...] = r["go"][p0 % 2]

    def drain_all(self):
        r, me = self.r, self.me
        cs = r["cs"]
        def some(e, ref, count, fewer):
            @pl.when(fewer)
            def _():
                take(ref.at[pl.ds(0, count - 1)], cs.at[e])
            @pl.when(jnp.logical_not(fewer))
            def _():
                take(ref.at[pl.ds(0, count)], cs.at[e])
        take(r["xup"].at[pl.ds(0, 31)], cs.at[0])
        some(1, r["xqkv"], 6, self.is_pair)
        m = me % 16
        seam = (m == 5) | (m == 10)
        p0 = 3 * (me // 16) + jnp.where(m > 10, 2, jnp.where(m > 5, 1, 0))
        hits = jnp.where(me == pair_seg(p0), 1, 0) + jnp.where(seam & (me == pair_seg(p0 + 1)), 1, 0)
        count = jnp.where(seam, 2, 1) - hits
        for n in (1, 2):
            @pl.when(count == n)
            def _():
                take(r["xout"].at[pl.ds(0, n)], cs.at[2])
        some(3, r["g46"], 18, self.is_pair | self.is_owner)
        some(6, r["g46"], 12, self.is_owner)
        some(8, r["g46"], 12, self.is_owner)
        take(r["xup"].at[pl.ds(0, 31)], cs.at[12])
        @pl.when(self.is_pair)
        def _():
            take(r["g46"].at[pl.ds(0, 12)], cs.at[4])
            take(r["g46"].at[pl.ds(0, 62)], cs.at[11])
            take(r["pq"].at[pl.ds(0, 31)], cs.at[13])
            first = pair_first(self.p)
            some(14, r["po"], 6, (me >= first) & (me < first + 6))
        @pl.when(self.is_owner)
        def _():
            take(r["g46"].at[pl.ds(0, 31)], cs.at[5])
            take(r["g46"].at[pl.ds(0, 62)], cs.at[7])
            take(r["g46"].at[pl.ds(0, 6)], cs.at[9])
            def one(t):
                w = self.window(t)
                @pl.when(((w == self.k) | (w + 1 == self.k)) & (t != me))
                def _():
                    take(r["p7f"], r["c7"].at[t])
            self.loop(32, one)


def cross_kernel(names, *refs):
    a = dict(zip(names[0], refs[:len(names[0])]))
    r = dict(zip(names[1], refs[len(names[0]):]))
    me = lax.axis_index("seg")
    bar = pltpu.get_barrier_semaphore()
    def greet(i, _):
        t = (me + 1 + i) % 32
        pl.semaphore_signal(bar, inc=1, device_id={"seg": t}, device_id_type=MESH)
        return 0
    lax.fori_loop(0, 31, greet, 0)
    pl.semaphore_wait(bar, 31)
    c = Cross(r, a)
    c.reshard()
    c.reshard_end()
    c.start(a["z0"][...], a["dy0"][...].astype(F32))
    c.attention()
    c.first_norm()
    c.mlp()
    c.second_norm()
    c.mlp_back()
    c.first_norm_back()
    c.attention_back()
    c.grads()
    a["y"][...] = c.output_rows()
    a["dx"][...] = c.finish()
    c.grads_end()
    c.drain_all()


INS = ["z0", "dy0", "cqkv", "cout", "cup", "cdown", "cb", "cupb", "pos", "doc"]
OUTS = dict(y=((8, 768), F32), dx=((8, 768), F32), gup=((32, 24, 128), BF16), gqkv=((6, 24, 384), BF16),
            gout=((24, 768), BF16), gdn=((96, 768), BF16), small=((8, 768), F32), dc=((8, 128), F32))

def cross(*args):
    names = (INS + list(OUTS), list(SCRATCH))
    vm = pl.BlockSpec(memory_space=pltpu.VMEM)
    return pl.pallas_call(
        functools.partial(cross_kernel, names),
        out_shape=tuple(jax.ShapeDtypeStruct(s, t) for s, t in OUTS.values()),
        in_specs=[vm] * 9 + [pl.BlockSpec(memory_space=pltpu.SMEM)],
        out_specs=tuple([vm] * len(OUTS)),
        scratch_shapes=list(SCRATCH.values()),
        compiler_params=pltpu.CompilerParams(collective_id=1, has_side_effects=True, vmem_limit_bytes=60 << 20),
        name="cross",
    )(*args)


def coords():
    s = lax.axis_index("seg")
    return s // 8, (s // 2) % 4, s % 2

def seg_of(x, y, c):
    return (x * 4 + y) * 2 + c

W = 384
def gather_kernel(a_ref, d_ref, sm_ref, wa, wd, smg, sm_s, sm_r, sib, stage, sib_s, sib_r, own_sem, s1, r1, s2, r2, s3, r3):
    x, y, c = coords()
    me = lax.axis_index("seg")
    xr, xl, yr, yl = (x + 1) % 4, (x + 3) % 4, (y + 1) % 4, (y + 3) % 4
    xo, yo = (x + 2) % 4, (y + 2) % 4
    other = seg_of(x, y, 1 - c)
    bar = pltpu.get_barrier_semaphore()
    def greet(i, _):
        pl.semaphore_signal(bar, inc=1, device_id={"seg": (me + 1 + i) % 32}, device_id_type=MESH)
        return 0
    lax.fori_loop(0, 31, greet, 0)
    pl.semaphore_wait(bar, 31)

    cp = rcopy(a_ref, sib, sib_s, sib_r, other)
    cp.start()
    def small(t, _):
        send_to(me, t, sm_ref, smg.at[me], sm_s, sm_r)
        return 0
    lax.fori_loop(0, 32, small, 0)

    def view(u, px, py):
        if isinstance(u, tuple):
            j = u[1]
            return wd.at[px, py, pl.ds(c * 96 + (j % 2) * 48, 48), pl.ds((j // 2) * W, W)]
        return wa.at[px, py, :, pl.ds((2 * u + c) * W, W)]

    def nbr(part, ring, step):
        if (part == 0) == (ring == 1):
            return seg_of((x + step) % 4, y, c)
        return seg_of(x, (y + step) % 4, c)

    full = pl.ds(0, 4)
    def v1(u, part, off):
        return view(u, (x + off) % 4, y) if part == 0 else view(u, x, (y + off) % 4)
    def v2(u, part, off):
        return view(u, full, (y + off) % 4) if part == 0 else view(u, (x + off) % 4, full)

    def phase1_start(u, k, part, src):
        own = v1(u, part, 0)
        rcopy(src, own, s1.at[k, 0], r1.at[k, 0], nbr(part, 1, 1)).start()
        rcopy(src, own, s1.at[k, 1], r1.at[k, 1], nbr(part, 1, 3)).start()
    def recv1(u, k, part, which):
        off = (3, 1, 2)[which]
        take(v1(u, part, off), r1.at[k, which])
    def fwd(ring, u, k, part, dirn):
        v, s, r = (v1, s1, r1) if ring == 1 else (v2, s2, r2)
        off, step = ((3, 1), (1, 3))[dirn]
        b = v(u, part, off)
        rcopy(b, b, s.at[k, 2], r.at[k, 2], nbr(part, ring, step)).start()
    def phase2_start(u, k, part):
        b = v2(u, part, 0)
        rcopy(b, b, s2.at[k, 0], r2.at[k, 0], nbr(part, 2, 1)).start()
        rcopy(b, b, s2.at[k, 1], r2.at[k, 1], nbr(part, 2, 3)).start()
    def recv2(u, k, part, which):
        off = (3, 1, 2)[which]
        take(v2(u, part, off), r2.at[k, which])
    def sibsend(u, k, part, n, off):
        b = v2(u, part, off)
        rcopy(b, b, s3.at[k, n], r3.at[k, n], other).start()

    def each(fn):
        def body_a(m, _):
            dirn = None
            for q in range(4):
                k = 4 * m + q
                fn(k, k, q % 2, q // 2)
            return 0
        lax.fori_loop(0, 2, body_a, 0)
        for q in range(4):
            fn(("d", q), 8 + q, q % 2, q // 2)

    def start_d(q):
        u = ("d", q)
        src = d_ref.at[pl.ds((q % 2) * 48, 48), pl.ds((q // 2) * W, W)]
        pltpu.make_async_copy(src, v1(u, q % 2, 0), own_sem.at[8 + q]).start()
        phase1_start(u, 8 + q, q % 2, src)
    cp.wait()
    def compose(k, kk, part, dirn):
        if isinstance(k, tuple):
            return
        col = pl.ds(pl.multiple_of((2 * k + c) * W, W), W)
        own = a_ref[:, col].astype(jnp.float32)
        oth = sib[:, col].astype(jnp.float32)
        lo = jnp.where(c == 0, own, oth)
        hi = jnp.where(c == 0, oth, own)
        stage[k] = jnp.concatenate([lo, hi], axis=0).astype(jnp.bfloat16)
        pltpu.make_async_copy(stage.at[k], v1(k, part, 0), own_sem.at[k]).start()
        phase1_start(k, k, part, stage.at[k])
    each(compose)
    for q in range(4):
        start_d(q)
    def step1(u, k, part, dirn):
        recv1(u, k, part, dirn)
        fwd(1, u, k, part, dirn)
    each(step1)
    def step2(u, k, part, dirn):
        recv1(u, k, part, 1 - dirn)
        recv1(u, k, part, 2)
        take(v1(u, part, 0), own_sem.at[k])
        phase2_start(u, k, part)
        sibsend(u, k, part, 0, 0)
    each(step2)
    def step3(u, k, part, dirn):
        recv2(u, k, part, dirn)
        fwd(2, u, k, part, dirn)
        recv2(u, k, part, 1 - dirn)
        sibsend(u, k, part, 1, 3)
        sibsend(u, k, part, 2, 1)
    each(step3)
    def step4(u, k, part, dirn):
        recv2(u, k, part, 2)
        sibsend(u, k, part, 3, 2)
    each(step4)
    def step5(u, k, part, dirn):
        for n in range(4):
            take(v2(u, part, 0), r3.at[k, n])
            take(v2(u, part, 0), s3.at[k, n])
        for n in range(3):
            take(v1(u, part, 0), s1.at[k, n])
            take(v2(u, part, 0), s2.at[k, n])
    each(step5)
    take(smg, sm_r)
    take(smg.at[pl.ds(0, 31)], sm_s)

def gather(a, d, sm):
    return pl.pallas_call(
        gather_kernel,
        out_shape=(jax.ShapeDtypeStruct((4, 4, 48, 6144), jnp.bfloat16),
                   jax.ShapeDtypeStruct((4, 4, 192, 768), jnp.bfloat16),
                   jax.ShapeDtypeStruct((32, 16, 384), jnp.bfloat16)),
        in_specs=[pl.BlockSpec(memory_space=pltpu.VMEM)] * 3,
        out_specs=[pl.BlockSpec(memory_space=pl.ANY)] * 3,
        scratch_shapes=[dma, dma, pltpu.VMEM((24, 6144), jnp.bfloat16), pltpu.VMEM((8, 48, W), jnp.bfloat16),
                        dma, dma, dma((12,)), dma((12, 3)), dma((12, 3)), dma((12, 3)), dma((12, 3)), dma((12, 4)), dma((12, 4))],
        compiler_params=pltpu.CompilerParams(collective_id=0, has_side_effects=True, vmem_limit_bytes=60 << 20),
        name="gather",
    )(a, d, sm)


def zcopy(src, dst, ssem, rsem, z, seg):
    return pltpu.make_async_remote_copy(src_ref=src, dst_ref=dst, send_sem=ssem, recv_sem=rsem,
                                        device_id={"grp": z, "seg": seg}, device_id_type=MESH)

SCR5 = dict(
    t0=pltpu.VMEM((12, 4, 4, 48, W), BF16), r0=pltpu.VMEM((12, 4, 4, 48, W), BF16),
    f2=pltpu.VMEM((12, 4, 48, W), BF16), a2=pltpu.VMEM((12, 4, 48, W), BF16), b2=pltpu.VMEM((12, 4, 48, W), BF16),
    t1=pltpu.VMEM((12, 4, 48, W), BF16),
    f1=pltpu.VMEM((12, 48, W), BF16), a1=pltpu.VMEM((12, 48, W), BF16), b1=pltpu.VMEM((12, 48, W), BF16),
    z0=pltpu.VMEM((24, 24, W), BF16), zr=pltpu.VMEM((8, 3, 24, W), BF16), zs=pltpu.VMEM((3, 24, W), BF16),
    fa=pltpu.VMEM((16, 24, W), BF16), fd=pltpu.VMEM((8, 24, W), BF16),
    c0=pltpu.VMEM((16, 24, W), BF16), cr=pltpu.VMEM((8, 2, 24, W), BF16), cs=pltpu.VMEM((2, 24, W), BF16), cf=pltpu.VMEM((8, 2, 24, W), BF16),
    ur=pltpu.VMEM((8, 4, 24, 128), BF16), us=pltpu.VMEM((4, 24, 128), BF16), uf=pltpu.VMEM((8, 4, 24, 128), BF16),
    s0=pltpu.VMEM((12, 8, 768), BF16), sg=pltpu.VMEM((32, 8, 768), BF16), s1=pltpu.VMEM((8, 768), F32), sz=pltpu.VMEM((31, 8, 768), F32),
    s2=pltpu.VMEM((8, 768), F32),
    mr=dma((12, 7)), ms=dma((12, 7)), lo=dma((12,)),
    xr=dma((9,)), xs=dma((9,)),
)

def reduce_kernel(names, *refs):
    a = dict(zip(names[0], refs[:len(names[0])]))
    r = dict(zip(names[1], refs[len(names[0]):]))
    me = lax.axis_index("seg")
    z = lax.axis_index("grp")
    x, y, c = me // 8, (me // 2) % 4, me % 2
    other = me + 1 - 2 * c
    k_own = me // 2
    is_owner = (c == 0) & (me < 24)
    bar = pltpu.get_barrier_semaphore()
    def greet(i, _):
        pl.semaphore_signal(bar, inc=1, device_id={"grp": z, "seg": (me + 1 + i) % 32}, device_id_type=MESH)
        return 0
    lax.fori_loop(0, 31, greet, 0)
    def greet_z(i, _):
        pl.semaphore_signal(bar, inc=1, device_id={"grp": (z + 1 + i) % 8, "seg": me}, device_id_type=MESH)
        pl.semaphore_signal(bar, inc=1, device_id={"grp": (z + 1 + i) % 8, "seg": other}, device_id_type=MESH)
        return 0
    lax.fori_loop(0, 7, greet_z, 0)
    pl.semaphore_wait(bar, 45)

    def loop(n, fn):
        def body(i, _):
            fn(i)
            return 0
        lax.fori_loop(0, n, body, 0)
    def units(fn):
        def body(m, _):
            for part in range(2):
                fn(2 * m + part, part, m % 2)
            return 0
        lax.fori_loop(0, 6, body, 0)
    def peers(fn):
        loop(7, lambda i: fn((z + 1 + i) % 8))

    def grad_a(u, cc):
        return a["ga"].at[:, :, :, pl.ds(pl.multiple_of((2 * u + cc) * W, W), W)]
    def grad_d(j, cc):
        return a["gd"].at[:, :, pl.ds(pl.multiple_of(cc * 96 + (j % 2) * 48, 16), 48), pl.ds(pl.multiple_of((j // 2) * W, W), W)]
    def first_a(u):
        rcopy(grad_a(u, 1 - c), r["r0"].at[u], r["ms"].at[u, 0], r["mr"].at[u, 0], other).start()
        pltpu.make_async_copy(grad_a(u, c), r["t0"].at[u], r["lo"].at[u]).start()
    def first_d(j):
        rcopy(grad_d(j, 1 - c), r["r0"].at[8 + j], r["ms"].at[8 + j, 0], r["mr"].at[8 + j, 0], other).start()
        pltpu.make_async_copy(grad_d(j, c), r["t0"].at[8 + j], r["lo"].at[8 + j]).start()
    loop(8, first_a)
    loop(4, first_d)

    xs, xr = r["xs"], r["xr"]
    r["s0"][...] = a["small"][...].reshape(12, 8, 768).astype(BF16)
    loop(12, lambda k: send_to(me, owner_seg(k), r["s0"].at[k], r["sg"].at[me], xs.at[0], xr.at[0]))
    for i in range(6):
        r["c0"][i] = a["gqkv"][i]
    for i in range(2):
        r["c0"][6 + i] = a["gout"][:, W * i:W * (i + 1)]
        for n in range(4):
            r["c0"][8 + 4 * i + n] = a["gdn"][...].astype(F32).reshape(4, 24, 768)[n, :, W * i:W * (i + 1)].astype(BF16)
    def cross_out(zz):
        zcopy(r["c0"].at[pl.ds(2 * zz, 2)], r["cr"].at[z], xs.at[1], xr.at[1], zz, me).start()
        zcopy(a["gup"].at[pl.ds(4 * zz, 4)], r["ur"].at[z], xs.at[2], xr.at[2], zz, me).start()
    peers(cross_out)
    pltpu.make_async_copy(r["c0"].at[pl.ds(2 * z, 2)], r["cr"].at[z], xr.at[1]).start()
    pltpu.make_async_copy(a["gup"].at[pl.ds(4 * z, 4)], r["ur"].at[z], xr.at[2]).start()

    def seg_on(axis_x, step):
        return (((x + step) % 4) * 4 + y) * 2 + c if axis_x else (x * 4 + (y + step) % 4) * 2 + c
    def ring(part, which, step):
        axis_x = (part == 0) == (which == 1)
        return seg_on(axis_x, step)
    def pos(part, which):
        return x if (part == 0) == (which == 1) else y
    def msg(k, part, q):
        return r["t0"].at[k, :, q] if part == 0 else r["t0"].at[k, q]

    def step_a(k, part, dirn):
        take(r["r0"].at[k], r["mr"].at[k, 0])
        take(r["t0"].at[k], r["lo"].at[k])
        def add(i):
            px, py = i // 4, i % 4
            r["t0"][k, px, py] = (r["t0"][k, px, py].astype(F32) + r["r0"][k, px, py].astype(F32)).astype(BF16)
        loop(16, add)
        q = pos(part, 2)
        fwd = 1 + 2 * dirn
        rcopy(msg(k, part, (q + 2) % 4), r["f2"].at[k], r["ms"].at[k, 1], r["mr"].at[k, 1], ring(part, 2, fwd)).start()
        rcopy(msg(k, part, (q + 4 - fwd) % 4), r["b2"].at[k], r["ms"].at[k, 2], r["mr"].at[k, 2], ring(part, 2, 4 - fwd)).start()
    units(step_a)

    def step_b(k, part, dirn):
        take(r["f2"].at[k], r["mr"].at[k, 1])
        q = pos(part, 2)
        fwd = 1 + 2 * dirn
        n = (q + fwd) % 4
        def add(i):
            v = msg(k, part, n).at[i]
            v[...] = (v[...].astype(F32) + r["f2"][k, i].astype(F32)).astype(BF16)
        loop(4, add)
        rcopy(msg(k, part, n), r["a2"].at[k], r["ms"].at[k, 3], r["mr"].at[k, 3], ring(part, 2, fwd)).start()
    units(step_b)

    @pl.when(is_owner)
    def _():
        take(r["sg"], xr.at[0])
        r["s1"][...] = jnp.sum(r["sg"][...].astype(F32), axis=0)
        peers(lambda zz: zcopy(r["s1"], r["sz"].at[z], xs.at[3], xr.at[3], zz, me).start())
        pltpu.make_async_copy(r["s1"], r["sz"].at[z], xr.at[3]).start()

    def step_c(k, part, dirn):
        take(r["a2"].at[k], r["mr"].at[k, 3])
        take(r["b2"].at[k], r["mr"].at[k, 2])
        q = pos(part, 2)
        def add(i):
            r["t1"][k, i] = (msg(k, part, q)[i].astype(F32) + r["a2"][k, i].astype(F32) + r["b2"][k, i].astype(F32)).astype(BF16)
        loop(4, add)
        q = pos(part, 1)
        fwd = 1 + 2 * dirn
        rcopy(r["t1"].at[k, (q + 2) % 4], r["f1"].at[k], r["ms"].at[k, 4], r["mr"].at[k, 4], ring(part, 1, fwd)).start()
        rcopy(r["t1"].at[k, (q + 4 - fwd) % 4], r["b1"].at[k], r["ms"].at[k, 5], r["mr"].at[k, 5], ring(part, 1, 4 - fwd)).start()
    units(step_c)

    take(r["cr"], xr.at[1])
    r["cs"][...] = jnp.sum(r["cr"][...].astype(F32), axis=0).astype(BF16)
    take(r["ur"], xr.at[2])
    r["us"][...] = jnp.sum(r["ur"][...].astype(F32), axis=0).astype(BF16)
    def cross_back(zz):
        zcopy(r["cs"], r["cf"].at[z], xs.at[4], xr.at[4], zz, me).start()
        zcopy(r["us"], r["uf"].at[z], xs.at[5], xr.at[5], zz, me).start()
    peers(cross_back)
    pltpu.make_async_copy(r["cs"], r["cf"].at[z], xr.at[4]).start()
    pltpu.make_async_copy(r["us"], r["uf"].at[z], xr.at[5]).start()

    def step_d(k, part, dirn):
        take(r["f1"].at[k], r["mr"].at[k, 4])
        q = pos(part, 1)
        fwd = 1 + 2 * dirn
        n = (q + fwd) % 4
        r["t1"][k, n] = (r["t1"][k, n].astype(F32) + r["f1"][k].astype(F32)).astype(BF16)
        rcopy(r["t1"].at[k, n], r["a1"].at[k], r["ms"].at[k, 6], r["mr"].at[k, 6], ring(part, 1, fwd)).start()
    units(step_d)

    @pl.when(is_owner)
    def _():
        take(r["sz"].at[pl.ds(0, 8)], xr.at[3])
        r["s2"][...] = jnp.sum(r["sz"][0:8], axis=0)
        loop(32, lambda t: send_to(me, t, r["s2"], a["osm"].at[k_own], xs.at[6], xr.at[6]))

    def step_e(k, part, dirn):
        take(r["a1"].at[k], r["mr"].at[k, 6])
        take(r["b1"].at[k], r["mr"].at[k, 5])
        q = pos(part, 1)
        t = r["t1"][k, q].astype(F32) + r["a1"][k].astype(F32) + r["b1"][k].astype(F32)
        r["z0"][pl.ds(2 * k, 2)] = t.reshape(2, 24, W).astype(BF16)
    units(step_e)
    peers(lambda zz: zcopy(r["z0"].at[pl.ds(3 * zz, 3)], r["zr"].at[z], xs.at[7], xr.at[7], zz, me).start())
    pltpu.make_async_copy(r["z0"].at[pl.ds(3 * z, 3)], r["zr"].at[z], xr.at[7]).start()
    take(r["zr"], xr.at[7])
    r["zs"][...] = jnp.sum(r["zr"][...].astype(F32), axis=0).astype(BF16)
    def piece(i):
        n = 3 * z + i
        u, h = n // 2, n % 2
        def one(dst, zz, seg):
            here = (zz == z) & (seg == me)
            @pl.when(here)
            def _():
                pltpu.make_async_copy(r["zs"].at[i], dst, xr.at[8]).start()
            @pl.when(jnp.logical_not(here))
            def _():
                zcopy(r["zs"].at[i], dst, xs.at[8], xr.at[8], zz, seg).start()
        @pl.when(n < 16)
        def _():
            dst = r["fa"].at[2 * u + c]
            seg = me - c + h
            loop(8, lambda zz: one(dst, zz, seg))
        @pl.when(n >= 16)
        def _():
            dst = r["fd"].at[n - 16]
            loop(8, lambda zz: one(dst, zz, me))
    loop(3, piece)

    take(r["cf"], xr.at[4])
    take(r["uf"], xr.at[5])
    for i in range(6):
        a["oxq"][i] = r["cf"][i // 2, i % 2].astype(F32)
    for i in range(2):
        a["oxo"][:, W * i:W * (i + 1)] = r["cf"][3, i].astype(F32)
        for n in range(4):
            m = 8 + 4 * i + n
            a["oxd"][24 * n:24 * (n + 1), W * i:W * (i + 1)] = r["cf"][m // 2, m % 2].astype(F32)
    a["oxu"][...] = r["uf"][...].reshape(32, 24, 128).astype(F32)
    take(r["z0"], xr.at[8])
    for u in range(16):
        if u < 6:
            a["oq"][:, W * u:W * (u + 1)] = r["fa"][u].astype(F32)
        elif u < 8:
            a["oo"][:, W * (u - 6):W * (u - 5)] = r["fa"][u].astype(F32)
        else:
            a["ou"][:, W * (u - 8):W * (u - 7)] = r["fa"][u].astype(F32)
    for n in range(8):
        j, h = n // 2, n % 2
        a["od"][(j % 2) * 48 + 24 * h:(j % 2) * 48 + 24 * h + 24, (j // 2) * W:(j // 2 + 1) * W] = r["fd"][n].astype(F32)
    take(a["osm"], xr.at[6])

    def sent(k, part, dirn):
        take(r["r0"].at[k], r["ms"].at[k, 0])
        for n in range(1, 4):
            take(r["f2"].at[k], r["ms"].at[k, n])
        for n in range(4, 7):
            take(r["f1"].at[k], r["ms"].at[k, n])
    units(sent)
    @pl.when(is_owner)
    def _():
        take(r["sg"].at[pl.ds(0, 11)], xs.at[0])
        take(r["sz"].at[pl.ds(0, 7)], xs.at[3])
        take(r["sz"], xs.at[6])
    @pl.when(jnp.logical_not(is_owner))
    def _():
        take(r["sg"].at[pl.ds(0, 12)], xs.at[0])
    take(r["cr"].at[pl.ds(0, 7)], xs.at[1])
    take(r["ur"].at[pl.ds(0, 7)], xs.at[2])
    take(r["cr"].at[pl.ds(0, 7)], xs.at[4])
    take(r["ur"].at[pl.ds(0, 7)], xs.at[5])
    take(r["zr"].at[pl.ds(0, 7)], xs.at[7])
    def here(i):
        n = 3 * z + i
        return jnp.where((n >= 16) | (n % 2 == c), 1, 0)
    stay = here(0) + here(1) + here(2)
    for n in range(4):
        @pl.when(stay == n)
        def _():
            take(r["z0"].at[pl.ds(0, 24 - n)], xs.at[8])

INS5 = ["ga", "gd", "gup", "gqkv", "gout", "gdn", "small"]
OUTS5 = dict(oq=((24, 2304), F32), oo=((24, 768), F32), ou=((24, 3072), F32), od=((96, 768), F32),
             oxq=((6, 24, W), F32), oxo=((24, 768), F32), oxu=((32, 24, 128), F32), oxd=((96, 768), F32), osm=((12, 8, 768), F32))

def reduce(*args):
    names = (INS5 + list(OUTS5), list(SCR5))
    vm = pl.BlockSpec(memory_space=pltpu.VMEM)
    return pl.pallas_call(
        functools.partial(reduce_kernel, names),
        out_shape=tuple(jax.ShapeDtypeStruct(s, t) for s, t in OUTS5.values()),
        in_specs=[pl.BlockSpec(memory_space=pl.ANY)] * 2 + [vm] * 5,
        out_specs=tuple([vm] * len(OUTS5)),
        scratch_shapes=list(SCR5.values()),
        compiler_params=pltpu.CompilerParams(collective_id=2, has_side_effects=True, vmem_limit_bytes=60 << 20),
        name="reduce",
    )(*args)


def layer_norm(values, gain_vec, shift_vec):
    center = values - jnp.mean(values, axis=-1, keepdims=True)
    spread = jnp.mean(center * center, axis=-1, keepdims=True)
    return center * lax.rsqrt(spread + 1e-05) * gain_vec + shift_vec


def gelu_exact(values):
    return jax.nn.gelu(values, approximate=False)


def project(inputs_b, weights):
    joined = jnp.dot(inputs_b, weights[0], preferred_element_type=jnp.float32)
    biases = weights[4]
    queries = (joined[:, :D] + biases[0]).astype(jnp.bfloat16)
    key_rows = joined[:, D : 2 * D].astype(jnp.bfloat16)
    value_rows = (joined[:, 2 * D :] + biases[1]).astype(jnp.bfloat16)
    return (queries, key_rows, value_rows)


def attend(queries, key_rows, value_rows, allowed):
    scores = jnp.einsum(
        "bqhe,bkhe->bhqk", queries, key_rows, preferred_element_type=jnp.float32
    ) * (1.0 / math.sqrt(HD))
    if allowed is not None:
        scores = jnp.where(allowed[:, None], scores, -1e30)
    row_max = jnp.max(scores, axis=-1, keepdims=True)
    exp_scores = jnp.exp(scores - row_max)
    row_sum = jnp.sum(exp_scores, axis=-1, keepdims=True)
    weights_b = (exp_scores / row_sum).astype(jnp.bfloat16)
    mixed_rows = jnp.einsum(
        "bhqk,bkhe->bqhe", weights_b, value_rows, preferred_element_type=jnp.float32
    )
    return (mixed_rows.astype(jnp.bfloat16), row_max + jnp.log(row_sum))


def attend_back(queries, key_rows, value_rows, allowed, log_total, grad_mixed):
    scale_f = 1.0 / math.sqrt(HD)
    scores = (
        jnp.einsum("bqhe,bkhe->bhqk", queries, key_rows, preferred_element_type=jnp.float32)
        * scale_f
    )
    if allowed is not None:
        scores = jnp.where(allowed[:, None], scores, -1e30)
    weights_f = jnp.exp(scores - log_total)
    grad_weights = jnp.einsum(
        "bqhe,bkhe->bhqk", grad_mixed, value_rows, preferred_element_type=jnp.float32
    )
    grad_scores = weights_f * (
        grad_weights - jnp.sum(weights_f * grad_weights, axis=-1, keepdims=True)
    )
    grad_scores = grad_scores.astype(jnp.bfloat16)
    grad_queries = (
        jnp.einsum("bhqk,bkhe->bqhe", grad_scores, key_rows, preferred_element_type=jnp.float32)
        * scale_f
    )
    grad_keys = (
        jnp.einsum("bhqk,bqhe->bkhe", grad_scores, queries, preferred_element_type=jnp.float32)
        * scale_f
    )
    grad_values = jnp.einsum(
        "bhqk,bqhe->bkhe",
        weights_f.astype(jnp.bfloat16),
        grad_mixed,
        preferred_element_type=jnp.float32,
    )
    return (grad_queries, grad_keys, grad_values)


def tail_ahead(inputs_f, mixed_rows, weights):
    w_qkv, w_out, w_up, w_down, biases, up_bias, gains = weights
    first_sum = (
        inputs_f + jnp.dot(mixed_rows, w_out, preferred_element_type=jnp.float32) + biases[2]
    )
    first_norm = layer_norm(first_sum, gains[0], biases[3]).astype(jnp.bfloat16)
    up_pre = jnp.dot(first_norm, w_up, preferred_element_type=jnp.float32) + up_bias
    active = gelu_exact(up_pre).astype(jnp.bfloat16)
    second_sum = (
        first_norm.astype(jnp.float32)
        + jnp.dot(active, w_down, preferred_element_type=jnp.float32)
        + biases[4]
    )
    output = layer_norm(second_sum, gains[1], biases[5])
    return (output, (first_sum, first_norm, up_pre, active, second_sum))


def tail_back(grad_out, mixed_rows, weights, saved):
    w_qkv, w_out, w_up, w_down, biases, up_bias, gains = weights
    first_sum, first_norm, up_pre, active, second_sum = saved
    _, second_pull = jax.vjp(
        layer_norm, second_sum, gains[1].astype(jnp.float32), biases[5].astype(jnp.float32)
    )
    grad_second, gain_two, shift_two = second_pull(grad_out)
    down_grad = grad_second.astype(jnp.bfloat16)
    grad_wdown = jnp.einsum("rf,rd->fd", active, down_grad, preferred_element_type=jnp.float32)
    grad_active = jnp.einsum("rd,fd->rf", down_grad, w_down, preferred_element_type=jnp.float32)
    _, gelu_pull = jax.vjp(gelu_exact, up_pre)
    up_grad = gelu_pull(grad_active)[0].astype(jnp.bfloat16)
    grad_wup = jnp.einsum("rd,rf->df", first_norm, up_grad, preferred_element_type=jnp.float32)
    grad_first = (
        jnp.einsum("rf,df->rd", up_grad, w_up, preferred_element_type=jnp.float32) + grad_second
    )
    _, first_pull = jax.vjp(
        layer_norm, first_sum, gains[0].astype(jnp.float32), biases[3].astype(jnp.float32)
    )
    grad_fsum, gain_one, shift_one = first_pull(grad_first)
    attn_grad = grad_fsum.astype(jnp.bfloat16)
    grad_wout = jnp.einsum("re,rd->ed", mixed_rows, attn_grad, preferred_element_type=jnp.float32)
    grad_mixed = jnp.einsum(
        "rd,ed->re", attn_grad, w_out, preferred_element_type=jnp.float32
    ).astype(jnp.bfloat16)
    small_grads = (
        jnp.sum(attn_grad.astype(jnp.float32), axis=0),
        shift_one,
        jnp.sum(down_grad.astype(jnp.float32), axis=0),
        shift_two,
        jnp.sum(up_grad.astype(jnp.float32), axis=0),
        gain_one,
        gain_two,
    )
    return (grad_mixed, grad_fsum, grad_wout, grad_wup, grad_wdown, small_grads)


def head_back(inputs_b, w_qkv, grad_queries, grad_keys, grad_values, grad_resid):
    grad_joined = jnp.concatenate([grad_queries, grad_keys, grad_values], axis=1)
    grad_inputs = (
        jnp.einsum("rc,dc->rd", grad_joined, w_qkv, preferred_element_type=jnp.float32) + grad_resid
    )
    grad_wqkv = jnp.einsum("rd,rc->dc", inputs_b, grad_joined, preferred_element_type=jnp.float32)
    sum_queries = jnp.sum(grad_queries.astype(jnp.float32), axis=0)
    sum_values = jnp.sum(grad_values.astype(jnp.float32), axis=0)
    return (grad_inputs, grad_wqkv, sum_queries, sum_values)


def pack_grads(grad_wqkv, sum_queries, sum_values, tail_parts):
    grad_mixed, grad_fsum, grad_wout, grad_wup, grad_wdown, small_grads = tail_parts
    out_bias, shift_one, down_bias, shift_two, up_bias, gain_one, gain_two = small_grads
    bias_grad = jnp.stack([sum_queries, sum_values, out_bias, shift_one, down_bias, shift_two])
    gains_grad = jnp.stack([gain_one, gain_two])
    return (grad_wqkv, grad_wout, grad_wup, grad_wdown, bias_grad, up_bias, gains_grad)


def local_ahead(tokens, weights):
    queries, key_rows, value_rows = project(tokens, weights)
    four_shape = (-1, SEG_LEN, H, HD)
    queries = queries.reshape(four_shape)
    key_rows = key_rows.reshape(four_shape)
    value_rows = value_rows.reshape(four_shape)
    mixed_rows, log_total = attend(queries, key_rows, value_rows, None)
    mixed_rows = mixed_rows.reshape(-1, D)
    output, saved = tail_ahead(tokens.astype(jnp.float32), mixed_rows, weights)
    return (output, (queries, key_rows, value_rows, mixed_rows, log_total, saved))


def shards(
    tokens,
    doc_segments,
    local_qkv,
    local_out,
    local_up,
    local_down,
    local_bias,
    local_upbias,
    local_gains,
    cross_qkv,
    cross_out,
    cross_up,
    cross_down,
    cross_bias,
    cross_upbias,
    cross_gains,
    pos_table,
    cotangent,
):
    me = lax.axis_index("seg")
    wide = jnp.concatenate([local_qkv, local_out, local_up], axis=1)
    def small_rows(bias, gains):
        return jnp.pad(jnp.concatenate([bias, gains], axis=0), ((0, 0), (0, 104)))
    ups = jnp.pad(jnp.stack([local_upbias, cross_upbias]), ((0, 6), (0, 32)))
    sm = jnp.concatenate(
        [
            jnp.concatenate([small_rows(local_bias, local_gains), small_rows(cross_bias, cross_gains), ups], axis=1),
            jnp.pad(pos_table.reshape(4, 384), ((0, 4), (0, 0))),
        ],
        axis=0,
    )
    wa, wd, smg = gather(wide, local_down, sm)
    wa = wa.reshape(D, 6144)
    def spread(lane):
        return smg[:, 0:8, lane : lane + 24].transpose(1, 0, 2).reshape(8, D)
    lsm, csm = spread(0), spread(128)
    local_full = (
        wa[:, : 3 * D],
        wa[:, 3 * D : 4 * D],
        wa[:, 4 * D :],
        wd.reshape(4 * D, D),
        lsm[:6],
        smg[:, 0, 256:352].reshape(4 * D),
        lsm[6:],
    )
    pos_full = smg[:, 8:12, :].reshape(POSN, D)
    local_result, local_saved = local_ahead(tokens, local_full)
    layer_rows = local_result.reshape(3, SEG_LEN, D)
    grad_layer = cotangent.astype(F32).reshape(3, SEG_LEN, D)
    cup = jnp.pad(cross_up.reshape(24, 32, 96).transpose(1, 0, 2), ((0, 0), (0, 0), (0, 32)))
    cupb = jnp.pad(cross_upbias.astype(F32)[None], ((0, 7), (0, 32)))
    y, dx, gup, gqkv, gout, gdn, small, dc = cross(
        jnp.pad(layer_rows[:, 0, :], ((0, 5), (0, 0))),
        jnp.pad(grad_layer[:, 0, :], ((0, 5), (0, 0))),
        cross_qkv,
        cross_out,
        cup,
        cross_down,
        csm.astype(F32),
        cupb,
        pos_full,
        doc_segments,
    )
    layer_out = layer_rows.at[:, 0, :].set(y[:3]).reshape(-1, D).astype(BF16)
    grad_layer = grad_layer.at[:, 0, :].set(dx[:3])

    seg_queries, seg_keys, seg_values, seg_mixed, seg_total, seg_saved = local_saved
    local_tail = tail_back(grad_layer.reshape(-1, D), seg_mixed, local_full, seg_saved)
    grad_sq, grad_sk, grad_sv = attend_back(
        seg_queries, seg_keys, seg_values, None, seg_total, local_tail[0].reshape(-1, SEG_LEN, H, HD)
    )
    grad_tokens, local_wqkv, local_sum_q, local_sum_v = head_back(
        tokens,
        local_full[0],
        grad_sq.reshape(-1, D).astype(BF16),
        grad_sk.reshape(-1, D).astype(BF16),
        grad_sv.reshape(-1, D).astype(BF16),
        local_tail[1],
    )
    wqkv, wout, wup, wdown, lbias, lup, lgains = pack_grads(local_wqkv, local_sum_q, local_sum_v, local_tail)
    ga = jnp.concatenate([wqkv.astype(BF16), wout.astype(BF16), wup.astype(BF16)], axis=1).reshape(4, 4, 48, 6144)
    gd = wdown.astype(BF16).reshape(4, 4, 192, D)

    counts = doc_segments[0]
    ends = jnp.cumsum(counts)
    slots = me * 3 + jnp.arange(3, dtype=jnp.int32)
    order = slots % 3 * 32 + slots // 3
    begins = jnp.sum(jnp.where(order[:, None] >= ends[None, :], counts[None, :], 0), axis=1)
    onehot = ((order - begins)[:, None] == jnp.arange(POSN, dtype=jnp.int32)[None, :]).astype(F32)
    grad_pos = jnp.einsum("rp,rd->pd", onehot, dx[:3], precision=HIGHEST)
    cross_dc = lax.dynamic_update_slice(jnp.zeros((4 * D,), F32), dc[0, :96], (me * 96,)).reshape(4, D)
    packed = jnp.concatenate(
        [lbias, lgains, small, lup.reshape(4, D), cross_dc, grad_pos, jnp.zeros((8, D), F32)], axis=0
    )
    oq, oo, ou, od, oxq, oxo, oxu, oxd, osm = reduce(ga, gd, gup, gqkv, gout, gdn, packed)
    osm = osm.reshape(96, D)
    col = lax.dynamic_slice(osm[:16], (0, me * 24), (16, 24))
    ups = lax.dynamic_slice(osm[16:24].reshape(2, 4 * D), (0, me * 96), (2, 96))
    return (
        layer_out,
        grad_tokens,
        oq,
        oo,
        ou,
        od,
        col[0:6],
        ups[0],
        col[6:8],
        oxq.reshape(6, 24, 3, 128).transpose(1, 2, 0, 3).reshape(24, 3 * D),
        oxo,
        oxu[:, :, :96].transpose(1, 0, 2).reshape(24, 4 * D),
        oxd,
        col[8:14],
        ups[1],
        col[14:16],
        lax.dynamic_slice(osm[24:88], (me * 2, 0), (2, D)),
    )


def solution(mesh):
    in_specs = (
        P(("grp", "seg"), None),
        P("grp", None),
        P("seg", None),
        P("seg", None),
        P("seg", None),
        P("seg", None),
        P(None, "seg"),
        P("seg"),
        P(None, "seg"),
        P("seg", None),
        P("seg", None),
        P("seg", None),
        P("seg", None),
        P(None, "seg"),
        P("seg"),
        P(None, "seg"),
        P("seg", None),
        P(("grp", "seg"), None),
    )
    out_specs = (
        P(("grp", "seg"), None),
        P(("grp", "seg"), None),
        P("seg", None),
        P("seg", None),
        P("seg", None),
        P("seg", None),
        P(None, "seg"),
        P("seg"),
        P(None, "seg"),
        P("seg", None),
        P("seg", None),
        P("seg", None),
        P("seg", None),
        P(None, "seg"),
        P("seg"),
        P(None, "seg"),
        P("seg", None),
    )
    return jax.shard_map(shards, mesh=mesh, in_specs=in_specs, out_specs=out_specs, check_vma=False)
```

```python
import functools
import math
import types

import jax
import jax.numpy as jnp
from jax import lax
from jax.experimental import pallas as pl
from jax.experimental.pallas import tpu as pltpu
from jax.sharding import PartitionSpec as P

D = 768
FF = 3072
ROWS = 384
SEG_LEN = 128
W = 384
F32, BF16 = jnp.float32, jnp.bfloat16
MESH = pl.DeviceIdType.MESH
DMA = pltpu.SemaphoreType.DMA
RSQ2 = 1.0 / math.sqrt(2.0)
RS2PI = 1.0 / math.sqrt(2.0 * math.pi)
VM = pltpu.VMEM


def dot(a, b):
    return lax.dot_general(a, b, (((1,), (0,)), ((), ())), preferred_element_type=F32)


def dot_bt(a, b):
    return lax.dot_general(a, b, (((1,), (1,)), ((), ())), preferred_element_type=F32)


def dot_at(a, b):
    return lax.dot_general(a, b, (((0,), (0,)), ((), ())), preferred_element_type=F32)


def rcopy(src, dst, ssem, rsem, seg):
    return pltpu.make_async_remote_copy(
        src_ref=src, dst_ref=dst, send_sem=ssem, recv_sem=rsem, device_id={"seg": seg}, device_id_type=MESH
    )


def zcopy(src, dst, ssem, rsem, z, seg):
    return pltpu.make_async_remote_copy(
        src_ref=src, dst_ref=dst, send_sem=ssem, recv_sem=rsem, device_id={"grp": z, "seg": seg}, device_id_type=MESH
    )


def take(ref, sem):
    pltpu.make_async_copy(ref, ref, sem).wait()


def send_to(me, target, src, dst, ssem, rsem):
    @pl.when(target != me)
    def _():
        rcopy(src, dst, ssem, rsem, target).start()

    @pl.when(target == me)
    def _():
        pltpu.make_async_copy(src, dst, rsem).start()


def loop(n, fn, first=0):
    def body(i, _):
        fn(i)
        return 0

    lax.fori_loop(first, n, body, 0)


def col(u, width=W):
    return pl.ds(pl.multiple_of(u * width, 128), width)


def norm(v):
    center = v - jnp.mean(v, axis=-1, keepdims=True)
    rstd = lax.rsqrt(jnp.mean(center * center, axis=-1, keepdims=True) + 1e-05)
    return center * rstd, rstd


def norm_back(grad, n, rstd, gain):
    dn = grad * gain
    return rstd * (dn - jnp.mean(dn, axis=-1, keepdims=True) - n * jnp.mean(dn * n, axis=-1, keepdims=True))


def gelu_both(u):
    e = jnp.exp(-0.5 * u * u)
    t = 1.0 / (1.0 + (0.3275911 * RSQ2) * jnp.abs(u))
    poly = t * (0.127414796 + t * (-0.142248368 + t * (0.7107068705 + t * (-0.7265760135 + t * 0.5307027145))))
    tail = poly * e
    cdf = jnp.where(u < 0.0, tail, 1.0 - tail)
    return u * cdf, cdf + u * (RS2PI * e)


def two_heads(v):
    lane = lax.broadcasted_iota(jnp.int32, v.shape, 1)
    none = jnp.zeros_like(v)
    return jnp.concatenate([jnp.where(lane < 64, v, none), jnp.where(lane >= 64, v, none)], axis=0)


def side_by_side(v):
    n = v.shape[0] // 2
    lane = lax.broadcasted_iota(jnp.int32, (n, 128), 1)
    return jnp.where(lane < 64, v[:n], v[n:])


def softmax(s):
    e = jnp.exp(s - jnp.max(s, axis=-1, keepdims=True))
    return e / jnp.sum(e, axis=-1, keepdims=True)


def softmax_back(w, dw):
    return w * (dw - jnp.sum(w * dw, axis=-1, keepdims=True))


def rows8(value):
    return value.reshape(value.shape[0] // 8, 8, value.shape[1])


def flat8(value):
    v = value.astype(F32)
    return v.reshape(v.shape[0] * v.shape[1], v.shape[2])


def sum0(v):
    return jnp.sum(v, axis=0, keepdims=True)


def owner_seg(k):
    return 2 * k


def pair_seg(p):
    return 4 * p + 1


def pair_first(p):
    return 5 * (p % 3) + 16 * (p // 3)


def fields(spec, refs):
    return types.SimpleNamespace(**dict(zip(spec, refs)))


CROSS = dict(
    pup=VM((32, 24, 128), BF16),
    xup=VM((32, 24, 128), BF16),
    xqkv=VM((32, 3, 24, 128), BF16),
    xout=VM((6, 24, D), BF16),
    wup=VM((D, 128), BF16),
    wqkv=VM((D, 384), BF16),
    wout=VM((128, D), BF16),
    wout_f=VM((144, D), F32),
    wdn=VM((128, D), BF16),
    msg=VM((8, D), BF16),
    x1=VM((32, 8, D), BF16),
    own=VM((8, 8, D), F32),
    rst=VM((8, 128), F32),
    xall=VM((96, D), BF16),
    q=VM((3, 96, 128), BF16),
    o=VM((96, 128), BF16),
    af=VM((192, 96), F32),
    p2=VM((12, 8, D), BF16),
    g2=VM((6, 8, D), BF16),
    p3=VM((8, D), BF16),
    g3=VM((12, 8, D), BF16),
    p4=VM((12, 8, D), BF16),
    g46=VM((64, 8, D), BF16),
    p5=VM((2, 8, D), BF16),
    g5=VM((12, 2, 8, D), BF16),
    p6=VM((12, 8, D), BF16),
    p7=VM((8, D), BF16),
    g7=VM((12, 8, D), BF16),
    p7f=VM((8, D), F32),
    g7f=VM((2, 8, D), F32),
    p8=VM((12, 8, D), BF16),
    g8=VM((6, 2, 8, D), BF16),
    gp=VM((96, 128), F32),
    gact=VM((96, 128), BF16),
    fall=VM((96, D), BF16),
    dd=VM((96, D), BF16),
    du=VM((96, 128), BF16),
    dq=VM((96, 384), BF16),
    de=VM((96, D), BF16),
    po_f=VM((144, D), F32),
    cs=DMA((16,)),
    cr=DMA((16,)),
    c7=DMA((32,)),
)


def slot_layout(doc, shape, slots):
    pos = (slots % 3) * 32 + slots // 3
    number = jnp.zeros(shape, jnp.int32)
    begin = jnp.zeros(shape, jnp.int32)
    end = jnp.int32(0)
    for d in range(6):
        begin = jnp.where(pos >= end, end, begin)
        number = jnp.where(pos >= end, d, number)
        end = end + doc[0, d]
    return number, pos - begin


class Cross:
    def __init__(self, r, a):
        self.r, self.a = r, a
        self.me = lax.axis_index("seg")
        self.is_owner = (self.me % 2 == 0) & (self.me < 24)
        self.k = self.me // 2
        self.is_pair = (self.me % 4 == 1) & (self.me < 24)
        self.p = self.me // 4

    def sem(self, e):
        return self.r.cs.at[e], self.r.cr.at[e]

    def seams(self):
        m = self.me % 16
        seam = (m == 5) | (m == 10)
        p0 = 3 * (self.me // 16) + jnp.where(m > 10, 2, jnp.where(m > 5, 1, 0))
        return seam, p0

    def reshard(self):
        r, a, me = self.r, self.a, self.me
        s0, r0 = self.sem(0)
        s1, r1 = self.sem(1)
        s2, r2 = self.sem(2)
        r.pup[...] = jnp.zeros((32, 24, 128), BF16)
        up = a.cup[...].astype(F32)
        for t in range(32):
            r.pup[t, :, 0:96] = up[:, 96 * t : 96 * t + 96].astype(BF16)
        loop(32, lambda t: send_to(me, t, r.pup.at[t], r.xup.at[me], s0, r0))

        def to_pair(p):
            for j in range(3):
                part = pl.ds(pl.multiple_of(D * j + 128 * p, 128), 128)
                send_to(me, pair_seg(p), a.cqkv.at[:, part], r.xqkv.at[me, j], s1, r1)
            first = pair_first(p)

            @pl.when((me >= first) & (me < first + 6))
            def _():
                send_to(me, pair_seg(p), a.cout, r.xout.at[me - first], s2, r2)

        loop(6, to_pair)
        r.wdn[0:96, :] = a.cdown[...]
        r.wdn[96:128, :] = jnp.zeros((32, D), BF16)

    def reshard_end(self):
        r = self.r
        take(r.xup, r.cr.at[0])
        r.wup[...] = r.xup[...].astype(F32).reshape(D, 128).astype(BF16)

        @pl.when(self.is_pair)
        def _():
            take(r.xqkv, r.cr.at[1])
            for j in range(3):
                r.wqkv[:, 128 * j : 128 * (j + 1)] = r.xqkv[:, j].astype(F32).reshape(D, 128).astype(BF16)
            take(r.xout, r.cr.at[2])
            r.wout_f[...] = r.xout[...].astype(F32).reshape(144, D)
            off = pl.multiple_of(8 * (self.p % 3), 8)
            r.wout[...] = r.wout_f[pl.ds(off, 128), :].astype(BF16)

    def start(self, z0, dy0):
        r, a, me = self.r, self.a, self.me
        row = lax.broadcasted_iota(jnp.int32, (8, 512), 0)
        lane = lax.broadcasted_iota(jnp.int32, (8, 512), 1)
        _, place = slot_layout(a.doc, (8, 512), jnp.minimum(me * 3 + row, 95))
        table = a.smg[...].astype(F32).reshape(512, W)[:, 256:384].astype(BF16)
        parts = []
        for i in range(6):
            hot = (lane == (place // 2) * 16 + (place % 2) * 6 + i) & (row < 3)
            parts.append(dot(hot.astype(BF16), table))
        cross_in = z0 + jnp.concatenate(parts, axis=1)
        rowd = lax.broadcasted_iota(jnp.int32, (8, D), 0)
        both = jnp.where(rowd < 3, cross_in, pltpu.roll(dy0, 3, 0))
        r.msg[...] = jnp.where(rowd < 6, both, 0.0).astype(BF16)
        ss, rs = self.sem(3)
        loop(6, lambda p: send_to(me, pair_seg(p), r.msg, r.x1.at[me], ss, rs))
        loop(12, lambda k: send_to(me, owner_seg(k), r.msg, r.x1.at[me], ss, rs))

    def pick(self, n, first, base):
        row = lax.broadcasted_iota(jnp.int32, (n, 256), 0) + first
        lane = lax.broadcasted_iota(jnp.int32, (n, 256), 1)
        return (lane == (row // 3) * 8 + row % 3 + base).astype(BF16)

    def attention(self):
        r, a, me = self.r, self.a, self.me
        ss, rs = self.sem(4)

        @pl.when(self.is_pair)
        def _():
            take(r.x1, r.cr.at[3])
            msgs = flat8(r.x1[...]).astype(BF16)
            xall = dot(self.pick(96, 0, 0), msgs).astype(BF16)
            r.xall[...] = xall
            part = col(self.p, 128)
            joined = dot(xall, r.wqkv[...])
            q = (joined[:, 0:128] + a.cb[0:1, part]).astype(BF16)
            k = joined[:, 128:256].astype(BF16)
            v = (joined[:, 256:384] + a.cb[1:2, part]).astype(BF16)
            r.q[0], r.q[1], r.q[2] = q, k, v
            line = lax.broadcasted_iota(jnp.int32, (192, 96), 0)
            doc_r, _ = slot_layout(a.doc, (192, 96), jnp.where(line < 96, line, line - 96))
            doc_c, _ = slot_layout(a.doc, (192, 96), lax.broadcasted_iota(jnp.int32, (192, 96), 1))
            w = softmax(jnp.where(doc_r == doc_c, dot_bt(two_heads(q), k) * 0.125, -1e30))
            r.af[...] = w
            o = side_by_side(dot(w.astype(BF16), v)).astype(BF16)
            r.o[...] = o
            r.p2[...] = rows8(dot(o, r.wout[...])).astype(BF16)
            loop(12, lambda k: send_to(me, owner_seg(k), r.p2.at[k], r.g2.at[self.p], ss, rs))

    def first_norm(self):
        r, a, me = self.r, self.a, self.me
        ss, rs = self.sem(5)

        @pl.when(self.is_owner)
        def _():
            take(r.x1, r.cr.at[3])
            msgs = flat8(r.x1[...]).astype(BF16)
            x = dot(self.pick(8, 8 * self.k, 0), msgs)
            r.own[1] = dot(self.pick(8, 8 * self.k, 3), msgs)
            take(r.g2, r.cr.at[4])
            total = jnp.sum(r.g2[...].astype(F32), axis=0)
            n, rstd = norm(x + (total + a.cb[2:3, :]))
            r.own[2] = n
            r.rst[...] = jnp.broadcast_to(rstd, (8, 128))
            r.p3[...] = (n * a.cb[6:7, :] + a.cb[3:4, :]).astype(BF16)
            loop(32, lambda t: send_to(me, t, r.p3, r.g3.at[self.k], ss, rs))

    def mlp(self):
        r, a, me = self.r, self.a, self.me
        ss, rs = self.sem(6)
        take(r.g3, r.cr.at[5])
        f = flat8(r.g3[...]).astype(BF16)
        r.fall[...] = f
        g, gp = gelu_both(dot(f, r.wup[...]) + a.cub[0:1, :])
        r.gp[...] = gp
        g = g.astype(BF16)
        r.gact[...] = g
        r.p4[...] = rows8(dot(g, r.wdn[...])).astype(BF16)
        loop(12, lambda k: send_to(me, owner_seg(k), r.p4.at[k], r.g46.at[me], ss, rs))

    def second_norm(self):
        r, a, me = self.r, self.a, self.me
        ss, rs = self.sem(7)

        @pl.when(self.is_owner)
        def _():
            take(r.g46.at[pl.ds(0, 32)], r.cr.at[6])
            total = jnp.sum(r.g46[0:32].astype(F32), axis=0)
            n, rstd = norm(r.p3[...].astype(F32) + (total + a.cb[4:5, :]))
            y = n * a.cb[7:8, :] + a.cb[5:6, :]
            dr2 = norm_back(r.own[1], n, rstd, a.cb[7:8, :])
            r.own[3] = n
            r.own[4] = dr2
            r.p5[0] = dr2.astype(BF16)
            r.p5[1] = y.astype(BF16)
            loop(32, lambda t: send_to(me, t, r.p5, r.g5.at[self.k], ss, rs))

    def mlp_back(self):
        r, me = self.r, self.me
        ss, rs = self.sem(8)
        take(r.g5, r.cr.at[7])
        dd = flat8(r.g5[:, 0]).astype(BF16)
        r.dd[...] = dd
        du = (dot_bt(dd, r.wdn[...]) * r.gp[...]).astype(BF16)
        r.du[...] = du
        r.p6[...] = rows8(dot_bt(du, r.wup[...])).astype(BF16)
        loop(12, lambda k: send_to(me, owner_seg(k), r.p6.at[k], r.g46.at[32 + me], ss, rs))

    def window(self, seg):
        return jnp.minimum((3 * seg) // 8, 10)

    def first_norm_back(self):
        r, a, me = self.r, self.a, self.me
        ss, rs = self.sem(9)
        fr = r.cr.at[10]

        @pl.when(self.is_owner)
        def _():
            take(r.g46.at[pl.ds(32, 32)], r.cr.at[8])
            df = jnp.sum(r.g46[32:64].astype(F32), axis=0) + r.own[4]
            r.own[5] = df
            dr1 = norm_back(df, r.own[2], r.rst[:, 0:1], a.cb[6:7, :])
            r.p7[...] = dr1.astype(BF16)
            loop(6, lambda p: send_to(me, pair_seg(p), r.p7, r.g7.at[self.k], ss, rs))
            r.p7f[...] = dr1

            def one(t):
                w = self.window(t)

                @pl.when((w == self.k) | (w + 1 == self.k))
                def _():
                    send_to(me, t, r.p7f, r.g7f.at[self.k - w], r.c7.at[t], fr)

            loop(32, one)

    def attention_back(self):
        r, me = self.r, self.me
        ss, rs = self.sem(11)

        @pl.when(self.is_pair)
        def _():
            take(r.g7, r.cr.at[9])
            de = flat8(r.g7[...]).astype(BF16)
            r.de[...] = de
            do = dot_bt(de, r.wout[...]).astype(BF16)
            q, k, v = r.q[0], r.q[1], r.q[2]
            do2, w = two_heads(do), r.af[...]
            ds = softmax_back(w, dot_bt(do2, v)).astype(BF16)
            r.dq[:, 0:128] = (side_by_side(dot(ds, k)) * 0.125).astype(BF16)
            r.dq[:, 128:256] = (dot_at(ds, two_heads(q)) * 0.125).astype(BF16)
            r.dq[:, 256:384] = dot_at(w.astype(BF16), do2).astype(BF16)
            r.p8[...] = rows8(dot_bt(r.dq[...], r.wqkv[...])).astype(BF16)
            loop(32, lambda t: send_to(me, t, r.p8.at[pl.ds(self.window(t), 2)], r.g8.at[self.p], ss, rs))

    def finish(self):
        r = self.r
        take(r.g7f, r.cr.at[10])
        take(r.g8, r.cr.at[11])
        total = r.g7f[...] + jnp.sum(r.g8[...].astype(F32), axis=0)
        shift = 3 * self.me - 8 * self.window(self.me)
        return pltpu.roll(total.reshape(16, D), 16 - shift, 0)[0:8]

    def output_rows(self):
        w = self.window(self.me)
        y = self.r.g5[pl.ds(w, 2), 1].astype(F32).reshape(16, D)
        return pltpu.roll(y, 16 - (3 * self.me - 8 * w), 0)[0:8]

    def grads(self):
        r, a = self.r, self.a
        a.pu[...] = dot_at(r.fall[...], r.du[...]).reshape(32, 24, 128).astype(BF16)
        a.gdn[...] = dot_at(r.gact[...], r.dd[...])[0:96].astype(BF16)

        @pl.when(self.is_pair)
        def _():
            a.pq[...] = dot_at(r.xall[...], r.dq[...]).reshape(32, 24, 384).astype(BF16)
            r.po_f[...] = jnp.zeros((144, D), F32)
            off = pl.multiple_of(8 * (self.p % 3), 8)
            r.po_f[pl.ds(off, 128), :] = dot_at(r.o[...], r.de[...])
            a.po[...] = r.po_f[...].reshape(6, 24, D).astype(BF16)

        a.small[...] = jnp.zeros((8, D), F32)

        @pl.when(self.is_owner)
        def _():
            dr1, df, dr2, dy = r.p7[...].astype(F32), r.own[5], r.own[4], r.own[1]
            dd = r.p5[0].astype(F32)
            for row, v in ((2, dr1), (3, df), (4, dd), (5, dy), (6, df * r.own[2]), (7, dy * r.own[3])):
                a.small[row : row + 1, :] = sum0(v)

        @pl.when(self.is_pair)
        def _():
            part = col(self.p, 128)
            a.small[0:1, part] = sum0(r.dq[:, 0:128].astype(F32))
            a.small[1:2, part] = sum0(r.dq[:, 256:384].astype(F32))

        a.dc[...] = jnp.broadcast_to(sum0(r.du[...].astype(F32)), (8, 128))

    def drain(self):
        r, me = self.r, self.me
        cs = r.cs

        def some(e, ref, count, fewer):
            @pl.when(fewer)
            def _():
                take(ref.at[pl.ds(0, count - 1)], cs.at[e])

            @pl.when(jnp.logical_not(fewer))
            def _():
                take(ref.at[pl.ds(0, count)], cs.at[e])

        take(r.xup.at[pl.ds(0, 31)], cs.at[0])
        some(1, r.xqkv, 6, self.is_pair)
        seam, p0 = self.seams()
        hits = jnp.where(me == pair_seg(p0), 1, 0) + jnp.where(seam & (me == pair_seg(p0 + 1)), 1, 0)
        count = jnp.where(seam, 2, 1) - hits
        for n in (1, 2):

            @pl.when(count == n)
            def _():
                take(r.xout.at[pl.ds(0, n)], cs.at[2])

        some(3, r.g46, 18, self.is_pair | self.is_owner)
        some(6, r.g46, 12, self.is_owner)
        some(8, r.g46, 12, self.is_owner)

        @pl.when(self.is_pair)
        def _():
            take(r.g46.at[pl.ds(0, 12)], cs.at[4])
            take(r.g46.at[pl.ds(0, 62)], cs.at[11])

        @pl.when(self.is_owner)
        def _():
            take(r.g46.at[pl.ds(0, 31)], cs.at[5])
            take(r.g46.at[pl.ds(0, 62)], cs.at[7])
            take(r.g46.at[pl.ds(0, 6)], cs.at[9])

            def one(t):
                w = self.window(t)

                @pl.when(((w == self.k) | (w + 1 == self.k)) & (t != me))
                def _():
                    take(r.p7f, r.c7.at[t])

            loop(32, one)


class CrossGrads(Cross):
    def scatter(self):
        r, a, me = self.r, self.a, self.me
        loop(32, lambda t: send_to(me, t, a.pu.at[t], r.gup.at[me], r.ks.at[0], r.kr.at[0]))

        @pl.when(self.is_pair)
        def _():
            loop(32, lambda t: send_to(me, t, a.pq.at[t], r.gqkv.at[self.p], r.ks.at[1], r.kr.at[1]))
            loop(
                6,
                lambda i: send_to(
                    me, pair_first(self.p) + i, a.po.at[i], r.go.at[self.p % 2], r.ks.at[2], r.kr.at[2]
                ),
            )

    def planes(self, red):
        r, a, me, z = self.r, self.a, self.me, red.z
        take(r.gup, r.kr.at[0])
        take(r.gqkv, r.kr.at[1])
        for i in range(6):
            r.c0[i] = r.gqkv[i]
        seam, p0 = self.seams()

        @pl.when(seam)
        def _():
            take(r.go, r.kr.at[2])
            both = (r.go[0].astype(F32) + r.go[1].astype(F32)).astype(BF16)
            for i in range(2):
                r.c0[6 + i] = both[:, W * i : W * (i + 1)]

        @pl.when(jnp.logical_not(seam))
        def _():
            take(r.go.at[0], r.kr.at[2])
            for i in range(2):
                r.c0[6 + i] = r.go[p0 % 2, :, W * i : W * (i + 1)]

        gdn = a.gdn[...].astype(F32).reshape(4, 24, D)
        for i in range(2):
            for n in range(4):
                r.c0[8 + 4 * i + n] = gdn[n, :, W * i : W * (i + 1)].astype(BF16)

        def out(zz):
            zcopy(r.c0.at[pl.ds(2 * zz, 2)], r.cr.at[z], r.xs.at[1], r.xr.at[1], zz, me).start()
            zcopy(r.gup.at[pl.ds(4 * zz, 4)], r.ur.at[z], r.xs.at[2], r.xr.at[2], zz, me).start()

        red.peers(out)
        pltpu.make_async_copy(r.c0.at[pl.ds(2 * z, 2)], r.cr.at[z], r.xr.at[1]).start()
        pltpu.make_async_copy(r.gup.at[pl.ds(4 * z, 4)], r.ur.at[z], r.xr.at[2]).start()

    def planes_sum(self, red):
        r, me, z = self.r, self.me, red.z
        take(r.cr, r.xr.at[1])
        r.cs[...] = jnp.sum(r.cr[...].astype(F32), axis=0).astype(BF16)
        take(r.ur, r.xr.at[2])
        r.us[...] = jnp.sum(r.ur[...].astype(F32), axis=0).astype(BF16)

        def back(zz):
            zcopy(r.cs, r.cf.at[z], r.xs.at[4], r.xr.at[4], zz, me).start()
            zcopy(r.us, r.uf.at[z], r.xs.at[5], r.xr.at[5], zz, me).start()

        red.peers(back)
        pltpu.make_async_copy(r.cs, r.cf.at[z], r.xr.at[4]).start()
        pltpu.make_async_copy(r.us, r.uf.at[z], r.xr.at[5]).start()

    def end(self):
        r, me = self.r, self.me
        take(r.cf, r.xr.at[4])
        take(r.uf, r.xr.at[5])
        take(r.gup.at[pl.ds(0, 31)], r.ks.at[0])

        @pl.when(self.is_pair)
        def _():
            take(r.pq.at[pl.ds(0, 31)], r.ks.at[1])
            first = pair_first(self.p)
            inside = (me >= first) & (me < first + 6)

            @pl.when(inside)
            def _():
                take(r.po.at[pl.ds(0, 5)], r.ks.at[2])

            @pl.when(jnp.logical_not(inside))
            def _():
                take(r.po, r.ks.at[2])

        for n, buf in ((1, r.cr), (2, r.ur), (4, r.cr), (5, r.ur)):
            take(buf.at[pl.ds(0, 7)], r.xs.at[n])


class Plane:
    def __init__(self):
        self.me = lax.axis_index("seg")
        self.x, self.y, self.c = self.me // 8, (self.me // 2) % 4, self.me % 2
        self.other = self.me + 1 - 2 * self.c

    def seg(self, on_x, step):
        if on_x:
            return (((self.x + step) % 4) * 4 + self.y) * 2 + self.c
        return (self.x * 4 + (self.y + step) % 4) * 2 + self.c

    def ring(self, part, which, step):
        return self.seg((part == 0) == (which == 1), step)

    def pos(self, part, which):
        return self.x if (part == 0) == (which == 1) else self.y

    def by_part(self, k, fn):
        for part in range(2):
            pl.when(k % 2 == part)(functools.partial(fn, part))

    @staticmethod
    def ahead(k):
        return 1 + 2 * ((k // 2) % 2)


class Gather(Plane):
    def __init__(self, r):
        super().__init__()
        self.r = r

    def v1(self, k, part, off):
        mine = self.r.ws.at[self.c, k]
        return mine.at[(self.x + off) % 4, self.y] if part == 0 else mine.at[self.x, (self.y + off) % 4]

    def v2(self, k, part, off):
        mine = self.r.ws.at[self.c, k]
        return mine.at[:, (self.y + off) % 4] if part == 0 else mine.at[(self.x + off) % 4]

    def first(self, k):
        r = self.r

        def go(part):
            own = self.v1(k, part, 0)
            src = r.stage.at[k]
            pltpu.make_async_copy(src, own, r.own_sem.at[k]).start()
            rcopy(src, own, r.s1.at[k, 0], r.r1.at[k, 0], self.ring(part, 1, 1)).start()
            rcopy(src, own, r.s1.at[k, 1], r.r1.at[k, 1], self.ring(part, 1, 3)).start()

        self.by_part(k, go)

    def first_on(self, k):
        r, ahead = self.r, self.ahead(k)

        def go(part):
            block = self.v1(k, part, 4 - ahead)
            take(block, r.r1.at[k, ahead // 2])
            rcopy(block, block, r.s1.at[k, 2], r.r1.at[k, 2], self.ring(part, 1, ahead)).start()

        self.by_part(k, go)

    def second(self, k):
        r, ahead = self.r, self.ahead(k)

        def go(part):
            take(self.v1(k, part, ahead), r.r1.at[k, 1 - ahead // 2])
            take(self.v1(k, part, 2), r.r1.at[k, 2])
            own = self.v1(k, part, 0)
            take(own, r.own_sem.at[k])
            row = self.v2(k, part, 0)
            rcopy(row, row, r.s2.at[k, 0], r.r2.at[k, 0], self.ring(part, 2, 1)).start()
            rcopy(row, row, r.s2.at[k, 1], r.r2.at[k, 1], self.ring(part, 2, 3)).start()
            rcopy(row, row, r.s3.at[k, 0], r.r3.at[k, 0], self.other).start()

        self.by_part(k, go)

    def second_on(self, k):
        r, ahead = self.r, self.ahead(k)

        def go(part):
            row = self.v2(k, part, 4 - ahead)
            take(row, r.r2.at[k, ahead // 2])
            rcopy(row, row, r.s2.at[k, 2], r.r2.at[k, 2], self.ring(part, 2, ahead)).start()
            rcopy(row, row, r.s3.at[k, 1], r.r3.at[k, 1], self.other).start()
            row = self.v2(k, part, ahead)
            take(row, r.r2.at[k, 1 - ahead // 2])
            rcopy(row, row, r.s3.at[k, 2], r.r3.at[k, 2], self.other).start()

        self.by_part(k, go)

    def last(self, k):
        r = self.r

        def go(part):
            row = self.v2(k, part, 2)
            take(row, r.r2.at[k, 2])
            rcopy(row, row, r.s3.at[k, 3], r.r3.at[k, 3], self.other).start()

        self.by_part(k, go)

    def arrived(self, k):
        r = self.r
        for n in range(4):
            take(r.ws.at[1 - self.c, k, 0], r.r3.at[k, n])

    def drain(self):
        r = self.r

        def one(k):
            for n in range(4):
                take(r.ws.at[0, 0, 0], r.s3.at[k, n])
            for n in range(3):
                take(r.ws.at[0, 0, 0, 0], r.s1.at[k, n])
                take(r.ws.at[0, 0, 0], r.s2.at[k, n])

        loop(12, one)


F_IN = list(dict(tok=0, cot=0, qkv=0, out=0, up=0, down=0, bias=0, upbias=0, gains=0, cqkv=0, cout=0, cup=0, cdown=0, cbias=0, cupbias=0, cgains=0, pos=0, doc=0))
F_OUT = dict(
    lo=((ROWS, D), BF16),
    ws_o=((2, 12, 4, 4, 48, W), BF16),
    qkv_o=((3, ROWS, D), BF16),
    mix_o=((ROWS, D), BF16),
    n1_o=((ROWS, D), F32),
    n2_o=((ROWS, D), F32),
    f_o=((ROWS, D), BF16),
    g_o=((ROWS, FF), BF16),
    gp_o=((ROWS, FF), BF16),
    rst_o=((2, ROWS, 128), F32),
    lb=((8, D), F32),
    dx=((8, D), F32),
    aw_o=((3, 6, 256, 128), BF16),
    pu=((32, 24, 128), BF16),
    pq=((32, 24, W), BF16),
    po=((6, 24, D), BF16),
    gdn=((96, D), BF16),
    small=((8, D), F32),
    dc=((8, 128), F32),
)
F_HBM = list(dict(aw_o=0, ws_o=0, qkv_o=0, mix_o=0, n1_o=0, n2_o=0, f_o=0, g_o=0, gp_o=0, rst_o=0))
F_SCR = dict(
    ws=VM((2, 12, 4, 4, 48, W), BF16),
    stage=VM((12, 48, W), BF16),
    sibq=VM((24, 3 * D), BF16),
    sibo=VM((24, D), BF16),
    sibu=VM((24, FF), BF16),
    smf=VM((16, W), F32),
    sm=VM((16, W), BF16),
    smg=VM((32, 16, W), BF16),
    both=VM((16, D), F32),
    lub=VM((1, FF), F32),
    cub=VM((8, 128), F32),
    cb=VM((8, D), F32),
    qkvv=VM((3, ROWS, D), BF16),
    mix=VM((ROWS, D), BF16),
    aw=VM((3, 6, 256, 128), BF16),
    n1=VM((ROWS, D), F32),
    n2=VM((ROWS, D), F32),
    f=VM((ROWS, D), BF16),
    g=VM((ROWS, FF), BF16),
    gpl=VM((ROWS, FF), BF16),
    rstl=VM((2, ROWS, 128), F32),
    sib_s=DMA((3,)),
    sib_r=DMA((3,)),
    sm_s=DMA,
    sm_r=DMA,
    own_sem=DMA((12,)),
    s1=DMA((12, 3)),
    r1=DMA((12, 3)),
    s2=DMA((12, 3)),
    r2=DMA((12, 3)),
    s3=DMA((12, 4)),
    r3=DMA((12, 4)),
    keep=DMA((10,)),
    **CROSS,
)


def forward_kernel(*refs):
    r = fields(F_IN + list(F_OUT) + list(F_SCR), refs)
    ring = Gather(r)
    cross = Cross(r, r)
    me, c = ring.me, ring.c
    bar = pltpu.get_barrier_semaphore()
    loop(31, lambda i: pl.semaphore_signal(bar, inc=1, device_id={"seg": (me + 1 + i) % 32}, device_id_type=MESH))
    r.smf[...] = jnp.zeros((16, W), F32)
    r.smf[0:6, 0:24] = r.bias[...].astype(F32)
    r.smf[6:8, 0:24] = r.gains[...].astype(F32)
    r.smf[8:14, 0:24] = r.cbias[...].astype(F32)
    r.smf[14:16, 0:24] = r.cgains[...].astype(F32)
    r.smf[0:1, 128:224] = r.upbias[...].astype(F32)
    table = r.pos[...].astype(F32)
    for t in range(2):
        for i in range(6):
            r.smf[6 * t + i : 6 * t + i + 1, 256:384] = table[t : t + 1, 128 * i : 128 * (i + 1)]
    r.sm[...] = r.smf[...].astype(BF16)
    r.cub[...] = jnp.zeros((8, 128), F32)
    r.cub[0:1, 0:96] = r.cupbias[...].astype(F32)
    pl.semaphore_wait(bar, 31)

    swaps = [(r.qkv, r.sibq), (r.out, r.sibo), (r.up, r.sibu)]
    for i, (src, dst) in enumerate(swaps):
        rcopy(src, dst, r.sib_s.at[i], r.sib_r.at[i], ring.other).start()
    for j in range(4):
        r.stage[8 + j] = r.down[(j % 2) * 48 : (j % 2) * 48 + 48, (j // 2) * W : (j // 2 + 1) * W]

    def compose(k, src, sib, block):
        own = src[:, col(block)].astype(F32)
        oth = sib[:, col(block)].astype(F32)
        lo, hi = jnp.where(c == 0, own, oth), jnp.where(c == 0, oth, own)
        r.stage[k] = jnp.concatenate([lo, hi], axis=0).astype(BF16)
        ring.first(k)

    def arrive(i):
        take(swaps[i][1], r.sib_r.at[i])

    arrive(0)
    loop(3, lambda k: compose(k, r.qkv, r.sibq, 2 * k + c))
    arrive(1)
    compose(3, r.out, r.sibo, c)
    arrive(2)
    loop(8, lambda k: compose(k, r.up, r.sibu, 2 * (k - 4) + c), 4)
    loop(12, ring.first, 8)
    loop(32, lambda t: send_to(me, t, r.sm, r.smg.at[me], r.sm_s, r.sm_r))
    loop(12, ring.first_on)
    loop(6, ring.second)
    cross.reshard()

    take(r.smg, r.sm_r)
    for t in range(32):
        block = r.smg[t].astype(F32)
        r.both[:, 24 * t : 24 * t + 24] = block[:, 0:24]
        r.lub[:, 96 * t : 96 * t + 96] = block[0:1, 128:224]
    r.lb[...] = r.both[0:8, :]
    r.cb[...] = r.both[8:16, :]

    def tick(k):
        ring.second_on(k)

        @pl.when(k < 6)
        def _():
            ring.second(k + 6)

        @pl.when(k >= 3)
        def _():
            ring.last(k - 3)

    def weight(cc, k):
        return r.ws[cc, k].reshape(D, W)

    loop(5, tick)

    def project(k):
        tick(k)
        i = k - 5
        ring.arrived(i)
        shift = jnp.where(i == 0, r.lb[0:1, :], jnp.where(i == 2, r.lb[1:2, :], 0.0))
        for cc in range(2):
            part = slice(cc * W, (cc + 1) * W)
            r.qkvv[i, :, part] = (dot(r.tok[...], weight(cc, i)) + shift[:, part]).astype(BF16)

    loop(8, project, 5)

    def attend(k):
        tick(k)
        s = k - 8
        rows = pl.ds(pl.multiple_of(s * 128, 128), 128)
        for p in range(6):
            part = slice(128 * p, 128 * (p + 1))
            w = softmax(dot_bt(two_heads(r.qkvv[0, rows, part]), r.qkvv[1, rows, part]) * 0.125).astype(BF16)
            r.aw[s, p] = w
            r.mix[rows, part] = side_by_side(dot(w, r.qkvv[2, rows, part])).astype(BF16)

    loop(11, attend, 8)
    tick(11)
    ring.arrived(3)
    for cc in range(2):
        part = slice(cc * W, (cc + 1) * W)
        r.n1[:, part] = dot(r.mix[...], weight(cc, 3)) + (r.tok[:, part].astype(F32) + r.lb[2:3, part])
    ring.last(9)

    def blocks(fn):
        loop(ROWS // 64, lambda i: fn(pl.ds(pl.multiple_of(i * 64, 64), 64)))

    def norm_one(rows):
        n, rstd = norm(r.n1[rows, :])
        r.n1[rows, :] = n
        r.rstl[0, rows, :] = jnp.broadcast_to(rstd, (64, 128))
        r.f[rows, :] = (n * r.lb[6:7, :] + r.lb[3:4, :]).astype(BF16)

    blocks(norm_one)

    def raise_up(i):
        ring.arrived(i)

        def half(cc):
            part = col(2 * (i - 4) + cc)
            u = dot(r.f[...], weight(cc, i)) + r.lub[0:1, part]
            g, gp = gelu_both(u)
            r.g[:, part] = g.astype(BF16)
            r.gpl[:, part] = gp.astype(BF16)

        loop(2, half)

        @pl.when(i < 6)
        def _():
            ring.last(i + 6)

    loop(8, raise_up, 4)

    def lower(kc):
        for j in range(2):
            ring.arrived(8 + 2 * kc + j)
        part = slice(kc * W, (kc + 1) * W)
        r.n2[:, part] = r.f[:, part].astype(F32) + r.lb[4:5, part]

        def quarter(x):
            pieces = [r.ws[cc, 8 + 2 * kc + j, x, y] for y in range(4) for cc in range(2) for j in range(2)]
            r.n2[:, part] += dot(r.g[:, col(x, D)], jnp.concatenate(pieces, axis=0))

        loop(4, quarter)

    lower(0)
    lower(1)

    def norm_two(rows):
        n, rstd = norm(r.n2[rows, :])
        r.n2[rows, :] = n
        r.rstl[1, rows, :] = jnp.broadcast_to(rstd, (64, 128))
        r.lo[rows, :] = (n * r.lb[7:8, :] + r.lb[5:6, :]).astype(BF16)

    blocks(norm_two)

    row = lax.broadcasted_iota(jnp.int32, (8, D), 0)
    z0 = jnp.zeros((8, D), F32)
    dy0 = jnp.zeros((8, D), F32)
    for s in range(3):
        z0 = jnp.where(row == s, r.n2[128 * s : 128 * s + 1, :] * r.lb[7:8, :] + r.lb[5:6, :], z0)
        dy0 = jnp.where(row == s, r.cot[128 * s : 128 * s + 16, :].astype(F32)[0:1, :], dy0)
    cross.reshard_end()
    cross.start(z0, dy0)
    kept = [
        (r.ws, r.ws_o), (r.qkvv, r.qkv_o), (r.mix, r.mix_o), (r.n1, r.n1_o), (r.n2, r.n2_o), (r.f, r.f_o),
        (r.g, r.g_o), (r.gpl, r.gp_o), (r.rstl, r.rst_o), (r.aw, r.aw_o),
    ]
    for i, (src, dst) in enumerate(kept):
        pltpu.make_async_copy(src, dst, r.keep.at[i]).start()
    cross.attention()
    cross.first_norm()
    cross.mlp()
    cross.second_norm()
    cross.mlp_back()
    cross.first_norm_back()
    cross.attention_back()
    y = cross.output_rows()
    row16 = lax.broadcasted_iota(jnp.int32, (16, D), 0)
    for s in range(3):
        old = r.lo[128 * s : 128 * s + 16, :].astype(F32)
        r.lo[128 * s : 128 * s + 16, :] = jnp.where(row16 == 0, y[s : s + 1, :], old).astype(BF16)
    cross.grads()
    r.dx[...] = cross.finish()
    cross.drain()
    ring.drain()
    for i, (src, dst) in enumerate(swaps):
        take(src, r.sib_s.at[i])
    take(r.smg.at[pl.ds(0, 31)], r.sm_s)
    for i, (src, dst) in enumerate(kept):
        take(dst, r.keep.at[i])


B_IN = list(dict(tok=0, cot=0, ws_o=0, qkv_o=0, mix_o=0, n1_o=0, n2_o=0, f_o=0, g_o=0, gp_o=0, rst_o=0, aw_o=0, lb=0, dx=0, pu=0, pq=0, po=0, gdn=0, small=0, dc=0, doc=0))
B_OUT = dict(
    tg=((ROWS, D), F32),
    fa=((16, 24, W), BF16),
    fd=((8, 24, W), BF16),
    cf=((8, 2, 24, W), BF16),
    uf=((8, 4, 24, 128), BF16),
    osm=((12, 8, D), F32),
)
B_SCR = dict(
    qkv=VM((3, ROWS, D), BF16),
    mix=VM((ROWS, D), BF16),
    aw=VM((3, 6, 256, 128), BF16),
    gup=VM((32, 24, 128), BF16),
    gqkv=VM((6, 24, W), BF16),
    go=VM((2, 24, D), BF16),
    n1=VM((ROWS, D), F32),
    n2=VM((ROWS, D), F32),
    f=VM((ROWS, D), BF16),
    g=VM((ROWS, FF), BF16),
    gp=VM((ROWS, FF), BF16),
    rst=VM((2, ROWS, 128), F32),
    dd=VM((ROWS, D), BF16),
    de=VM((ROWS, D), BF16),
    dqkv=VM((3, ROWS, D), BF16),
    wdb=VM((2, 2, 4, 48, D), BF16),
    wub=VM((2, 4, 4, 48, W), BF16),
    wo=VM((2, 4, 4, 48, W), BF16),
    wq=VM((2, 3, 4, 4, 48, W), BF16),
    gb=VM((2, 12, 4, 4, 48, W), BF16),
    r0=VM((12, 4, 4, 48, W), BF16),
    f2=VM((12, 4, 48, W), BF16),
    a2=VM((12, 4, 48, W), BF16),
    b2=VM((12, 4, 48, W), BF16),
    t1=VM((12, 4, 48, W), BF16),
    f1=VM((12, 48, W), BF16),
    a1=VM((12, 48, W), BF16),
    b1=VM((12, 48, W), BF16),
    z0=VM((3, 8, 24, W), BF16),
    zr=VM((3, 8, 24, W), BF16),
    zs=VM((3, 24, W), BF16),
    c0=VM((16, 24, W), BF16),
    cr=VM((8, 2, 24, W), BF16),
    cs=VM((2, 24, W), BF16),
    ur=VM((8, 4, 24, 128), BF16),
    us=VM((4, 24, 128), BF16),
    sf=VM((96, D), F32),
    s0=VM((12, 8, D), BF16),
    sg=VM((32, 8, D), BF16),
    s1=VM((8, D), F32),
    sz=VM((31, 8, D), F32),
    s2=VM((8, D), F32),
    dcl=VM((1, FF), F32),
    mr=DMA((12, 7)),
    ms=DMA((12, 7)),
    xr=DMA((8,)),
    xs=DMA((8,)),
    zsr=DMA((3, 2)),
    zss=DMA((3, 2)),
    keep=DMA((9,)),
    ks=DMA((3,)),
    kr=DMA((3,)),
    wds=DMA((2, 8)),
    wus=DMA((2,)),
    wos=DMA((2,)),
    wqs=DMA((2,)),
)


class Reduce(Plane):
    def __init__(self, r):
        super().__init__()
        self.r = r
        self.z = lax.axis_index("grp")

    @staticmethod
    def unit(i):
        return jnp.where(i < 4, 8 + i, jnp.where(i < 8, i, jnp.where(i == 8, 3, i - 9)))

    def peers(self, fn):
        loop(7, lambda i: fn((self.z + 1 + i) % 8))

    def to_sibling(self, k):
        r = self.r
        rcopy(r.gb.at[1, k], r.r0.at[k], r.ms.at[k, 0], r.mr.at[k, 0], self.other).start()

    def msg(self, k, part, q):
        return self.r.gb.at[0, k, :, q] if part == 0 else self.r.gb.at[0, k, q]

    def step_a(self, k):
        r, ahead = self.r, self.ahead(k)
        take(r.r0.at[k], r.mr.at[k, 0])

        def add(i):
            px, py = i // 4, i % 4
            r.gb[0, k, px, py] = (r.gb[0, k, px, py].astype(F32) + r.r0[k, px, py].astype(F32)).astype(BF16)

        loop(16, add)

        def go(part):
            q = self.pos(part, 2)
            far, back = self.msg(k, part, (q + 2) % 4), self.msg(k, part, (q + 4 - ahead) % 4)
            rcopy(far, r.f2.at[k], r.ms.at[k, 1], r.mr.at[k, 1], self.ring(part, 2, ahead)).start()
            rcopy(back, r.b2.at[k], r.ms.at[k, 2], r.mr.at[k, 2], self.ring(part, 2, 4 - ahead)).start()

        self.by_part(k, go)

    def step_b(self, k):
        r, ahead = self.r, self.ahead(k)
        take(r.f2.at[k], r.mr.at[k, 1])

        def go(part):
            block = self.msg(k, part, (self.pos(part, 2) + ahead) % 4)

            def add(i):
                block[i] = (block[i].astype(F32) + r.f2[k, i].astype(F32)).astype(BF16)

            loop(4, add)
            rcopy(block, r.a2.at[k], r.ms.at[k, 3], r.mr.at[k, 3], self.ring(part, 2, ahead)).start()

        self.by_part(k, go)

    def step_c(self, k):
        r, ahead = self.r, self.ahead(k)
        take(r.a2.at[k], r.mr.at[k, 3])
        take(r.b2.at[k], r.mr.at[k, 2])

        def go(part):
            block = self.msg(k, part, self.pos(part, 2))

            def add(i):
                r.t1[k, i] = (block[i].astype(F32) + r.a2[k, i].astype(F32) + r.b2[k, i].astype(F32)).astype(BF16)

            loop(4, add)
            q = self.pos(part, 1)
            far, back = r.t1.at[k, (q + 2) % 4], r.t1.at[k, (q + 4 - ahead) % 4]
            rcopy(far, r.f1.at[k], r.ms.at[k, 4], r.mr.at[k, 4], self.ring(part, 1, ahead)).start()
            rcopy(back, r.b1.at[k], r.ms.at[k, 5], r.mr.at[k, 5], self.ring(part, 1, 4 - ahead)).start()

        self.by_part(k, go)

    def step_d(self, k):
        r, ahead = self.r, self.ahead(k)
        take(r.f1.at[k], r.mr.at[k, 4])

        def go(part):
            n = (self.pos(part, 1) + ahead) % 4
            r.t1[k, n] = (r.t1[k, n].astype(F32) + r.f1[k].astype(F32)).astype(BF16)
            rcopy(r.t1.at[k, n], r.a1.at[k], r.ms.at[k, 6], r.mr.at[k, 6], self.ring(part, 1, ahead)).start()

        self.by_part(k, go)

    def step_e(self, i):
        r = self.r
        k = self.unit(i)
        take(r.a1.at[k], r.mr.at[k, 6])
        take(r.b1.at[k], r.mr.at[k, 5])

        def go(part):
            t = r.t1[k, self.pos(part, 1)].astype(F32) + r.a1[k].astype(F32) + r.b1[k].astype(F32)
            r.z0[i // 4, pl.ds(2 * (i % 4), 2)] = t.reshape(2, 24, W).astype(BF16)

        self.by_part(k, go)

    def z_send(self, g):
        r, z, me = self.r, self.z, self.me
        self.peers(lambda zz: zcopy(r.z0.at[g, zz], r.zr.at[g, z], r.zss.at[g, 0], r.zsr.at[g, 0], zz, me).start())
        pltpu.make_async_copy(r.z0.at[g, z], r.zr.at[g, z], r.zsr.at[g, 0]).start()

    def z_sum(self, g):
        r, z, me, c = self.r, self.z, self.me, self.c
        take(r.zr.at[g], r.zsr.at[g, 0])
        r.zs[g] = jnp.sum(r.zr[g].astype(F32), axis=0).astype(BF16)
        m, h = z // 2, z % 2

        def out(dst, sem, seg):
            def one(zz):
                here = (zz == z) & (seg == me)

                @pl.when(here)
                def _():
                    pltpu.make_async_copy(r.zs.at[g], dst, sem).start()

                @pl.when(jnp.logical_not(here))
                def _():
                    zcopy(r.zs.at[g], dst, r.zss.at[g, 1], sem, zz, seg).start()

            loop(8, one)

        if g == 0:
            out(r.fd.at[z], r.zsr.at[0, 1], me)
        elif g == 1:
            out(r.fa.at[8 + 2 * m + c], r.zsr.at[1, 1], me - c + h)
        else:
            out(r.fa.at[2 * ((m + 3) % 4) + c], r.zsr.at[2, 1], me - c + h)

    def drain(self):
        r, z, c = self.r, self.z, self.c

        def one(k):
            take(r.r0.at[k], r.ms.at[k, 0])
            for n in range(1, 4):
                take(r.f2.at[k], r.ms.at[k, n])
            for n in range(4, 7):
                take(r.f1.at[k], r.ms.at[k, n])

        loop(12, one)
        for g in range(3):
            take(r.zr.at[g, pl.ds(0, 7)], r.zss.at[g, 0])
            stays = (z % 2 == c) if g > 0 else (z >= 0)

            @pl.when(stays)
            def _():
                take(r.zr.at[g, pl.ds(0, 7)], r.zss.at[g, 1])

            @pl.when(jnp.logical_not(stays))
            def _():
                take(r.zr.at[g], r.zss.at[g, 1])


def backward_kernel(*refs):
    r = fields(B_IN + list(B_OUT) + list(B_SCR), refs)
    red = Reduce(r)
    me, c, z = red.me, red.c, red.z
    is_owner = (c == 0) & (me < 24)
    cross = CrossGrads(r, r)
    loads = [
        (r.n2_o, r.n2), (r.rst_o, r.rst), (r.g_o, r.g), (r.gp_o, r.gp), (r.f_o, r.f), (r.n1_o, r.n1),
        (r.mix_o, r.mix), (r.qkv_o, r.qkv), (r.aw_o, r.aw),
    ]
    for i, (src, dst) in enumerate(loads):
        pltpu.make_async_copy(src, dst, r.keep.at[i]).start()

    def have(i):
        take(loads[i][1], r.keep.at[i])

    bar = pltpu.get_barrier_semaphore()
    loop(31, lambda i: pl.semaphore_signal(bar, inc=1, device_id={"grp": z, "seg": (me + 1 + i) % 32}, device_id_type=MESH))

    def greet_z(zz):
        for seg in (me, red.other):
            pl.semaphore_signal(bar, inc=1, device_id={"grp": zz, "seg": seg}, device_id_type=MESH)

    red.peers(greet_z)

    def down_block(b, start):
        for cc in range(2):
            for j in range(4):
                cp = pltpu.make_async_copy(
                    r.ws_o.at[cc, 8 + j, b // 2, pl.ds(2 * (b % 2), 2)],
                    r.wdb.at[b % 2, :, 2 * cc + j % 2, :, pl.ds((j // 2) * W, W)],
                    r.wds.at[b % 2, 4 * cc + j],
                )
                cp.start() if start else cp.wait()

    def up_block(b, start):
        cp = pltpu.make_async_copy(r.ws_o.at[b % 2, 4 + b // 2], r.wub.at[b % 2], r.wus.at[b % 2])
        cp.start() if start else cp.wait()

    down_block(0, True)
    up_block(0, True)
    for cc in range(2):
        pltpu.make_async_copy(r.ws_o.at[cc, 3], r.wo.at[cc], r.wos.at[cc]).start()
        pltpu.make_async_copy(r.ws_o.at[cc, pl.ds(0, 3)], r.wq.at[cc], r.wqs.at[cc]).start()

    def blocks(fn):
        loop(ROWS // 64, lambda i: fn(pl.ds(pl.multiple_of(i * 64, 64), 64)))

    sf = r.sf
    sf[...] = jnp.zeros((96, D), F32)
    have(0)
    have(1)
    row = lax.broadcasted_iota(jnp.int32, (64, D), 0)

    def norm_two(i):
        rows = pl.ds(pl.multiple_of(i * 64, 64), 64)
        first = r.dx[pl.ds(i // 2, 1), :]
        dy = jnp.where((row == 0) & (i % 2 == 0), first, r.cot[rows, :].astype(F32))
        n = r.n2[rows, :]
        dr2 = norm_back(dy, n, r.rst[1, rows, 0:1], r.lb[7:8, :])
        dd = dr2.astype(BF16)
        r.n2[rows, :] = dr2
        r.dd[rows, :] = dd
        sf[5:6, :] += sum0(dy)
        sf[7:8, :] += sum0(dy * n)
        sf[4:5, :] += sum0(dd.astype(F32))

    loop(6, norm_two)
    have(2)

    def down_grad(b):
        v = dot_at(r.g[:, col(b)], r.dd[...]).astype(BF16).reshape(2, 2, 2, 48, D)
        for chip in range(2):
            for cc in range(2):
                for j in range(4):
                    r.gb[(cc + c) % 2, 8 + j, b // 2, 2 * (b % 2) + chip] = v[chip, cc, j % 2, :, (j // 2) * W : (j // 2 + 1) * W]

    loop(8, down_grad)
    pl.semaphore_wait(bar, 45)
    loop(12, red.to_sibling, 8)

    cross.scatter()

    def tick(t):
        def run(lag, fn):
            @pl.when((t >= lag) & (t < lag + 12))
            def _():
                fn(t - lag)

        run(0, lambda i: red.step_a(red.unit(i)))
        run(2, lambda i: red.step_b(red.unit(i)))
        run(4, lambda i: red.step_c(red.unit(i)))
        run(5, lambda i: red.step_d(red.unit(i)))
        run(6, red.step_e)

    have(3)
    have(4)

    def middle(b):
        @pl.when(b < 7)
        def _():
            down_block(b + 1, True)
            up_block(b + 1, True)

        part = col(b)
        down_block(b, False)
        dg = dot_bt(r.dd[...], r.wdb[b % 2].reshape(W, D))
        du = (dg * r.gp[:, part].astype(F32)).astype(BF16)
        r.dcl[:, part] = sum0(du.astype(F32))
        up_block(b, False)
        r.n2[...] += dot_bt(du, r.wub[b % 2].reshape(D, W))
        r.gb[(b + c) % 2, 4 + b // 2] = dot_at(r.f[...], du).astype(BF16).reshape(4, 4, 48, W)

        @pl.when(b % 2 == 1)
        def _():
            red.to_sibling(4 + b // 2)
            tick(b // 2)

        @pl.when(b == 4)
        def _():
            cross.planes(red)

    loop(8, middle)
    have(5)

    def norm_one(rows):
        df, n = r.n2[rows, :], r.n1[rows, :]
        dr1 = norm_back(df, n, r.rst[0, rows, 0:1], r.lb[6:7, :])
        de = dr1.astype(BF16)
        r.n2[rows, :] = dr1
        r.de[rows, :] = de
        sf[3:4, :] += sum0(df)
        sf[6:7, :] += sum0(df * n)
        sf[2:3, :] += sum0(de.astype(F32))

    blocks(norm_one)
    have(6)
    for cc in range(2):
        r.gb[(cc + c) % 2, 3] = dot_at(r.mix[...], r.de[:, cc * W : (cc + 1) * W]).astype(BF16).reshape(4, 4, 48, W)
    red.to_sibling(3)
    for cc in range(2):
        take(r.wo.at[cc], r.wos.at[cc])
        part = dot_bt(r.de[:, cc * W : (cc + 1) * W], r.wo[cc].reshape(D, W))
        if cc == 0:
            r.n1[...] = part
        else:
            r.dd[...] = (r.n1[...] + part).astype(BF16)
    tick(4)
    have(7)
    have(8)

    def attend_back(s):
        rows = pl.ds(pl.multiple_of(s * 128, 128), 128)
        for p in range(6):
            part = slice(128 * p, 128 * (p + 1))
            q, k, v = r.qkv[0, rows, part], r.qkv[1, rows, part], r.qkv[2, rows, part]
            do = two_heads(r.dd[rows, part])
            w = r.aw[s, p]
            ds = softmax_back(w.astype(F32), dot_bt(do, v)).astype(BF16)
            r.dqkv[0, rows, part] = (side_by_side(dot(ds, k)) * 0.125).astype(BF16)
            r.dqkv[1, rows, part] = (dot_at(ds, two_heads(q)) * 0.125).astype(BF16)
            r.dqkv[2, rows, part] = dot_at(w, do).astype(BF16)
        tick(5 + s)

    loop(3, attend_back)
    cross.planes_sum(red)

    sf[0:1, :] = sum0(r.dqkv[0].astype(F32))
    sf[1:2, :] = sum0(r.dqkv[2].astype(F32))
    sf[8:16, :] = r.small[...]
    for i in range(4):
        sf[16 + i : 17 + i, :] = r.dcl[:, D * i : D * (i + 1)]
    own = jnp.concatenate([r.dc[0:1, :], jnp.zeros((1, D - 128), F32)], axis=1)
    own = pltpu.roll(own, 96 * (me % 8), 1)
    sf[pl.ds(20 + me // 8, 1), :] = own
    line = lax.broadcasted_iota(jnp.int32, (64, D), 0)
    for s in range(3):
        _, place = slot_layout(r.doc, (64, D), jnp.full((64, D), me * 3 + s, jnp.int32))
        sf[24:88, :] += jnp.where(line == place, r.dx[s : s + 1, :], 0.0)
    r.s0[...] = sf[...].reshape(12, 8, D).astype(BF16)
    xs, xr = r.xs, r.xr
    loop(12, lambda k: send_to(me, owner_seg(k), r.s0.at[k], r.sg.at[me], xs.at[0], xr.at[0]))

    def qkv_grad(i):
        for cc in range(2):
            part = slice(cc * W, (cc + 1) * W)
            r.gb[(cc + c) % 2, i] = dot_at(r.tok[...], r.dqkv[i, :, part]).astype(BF16).reshape(4, 4, 48, W)
        red.to_sibling(i)
        tick(8 + i)

    loop(3, qkv_grad)
    red.z_send(0)

    @pl.when(is_owner)
    def _():
        take(r.sg, xr.at[0])
        r.s1[...] = jnp.sum(r.sg[...].astype(F32), axis=0)
        red.peers(lambda zz: zcopy(r.s1, r.sz.at[z], xs.at[3], xr.at[3], zz, me).start())
        pltpu.make_async_copy(r.s1, r.sz.at[z], xr.at[3]).start()

    tick(11)
    for cc in range(2):
        take(r.wq.at[cc], r.wqs.at[cc])
    r.tg[...] = r.n2[...]

    def token_grad(i):
        acc = dot_bt(r.dqkv[i, :, 0:W], r.wq[0, i].reshape(D, W))
        r.tg[...] += acc + dot_bt(r.dqkv[i, :, W : 2 * W], r.wq[1, i].reshape(D, W))

    token_grad(0)
    tick(12)
    token_grad(1)
    red.z_sum(0)
    tick(13)
    red.z_send(1)
    token_grad(2)
    tick(14)

    @pl.when(is_owner)
    def _():
        take(r.sz.at[pl.ds(0, 8)], xr.at[3])
        r.s2[...] = jnp.sum(r.sz[0:8], axis=0)
        loop(32, lambda t: send_to(me, t, r.s2, r.osm.at[me // 2], xs.at[6], xr.at[6]))

    tick(15)
    red.z_sum(1)
    tick(16)
    tick(17)
    red.z_send(2)
    red.z_sum(2)
    for g, ref in ((0, r.fd), (1, r.fa.at[pl.ds(8, 8)]), (2, r.fa.at[pl.ds(0, 8)])):
        take(ref, r.zsr.at[g, 1])
    take(r.osm, xr.at[6])
    cross.end()
    red.drain()

    @pl.when(is_owner)
    def _():
        take(r.sg.at[pl.ds(0, 11)], xs.at[0])
        take(r.sz.at[pl.ds(0, 7)], xs.at[3])
        take(r.sz, xs.at[6])

    @pl.when(jnp.logical_not(is_owner))
    def _():
        take(r.sg.at[pl.ds(0, 12)], xs.at[0])


FORMAT_IN = list(dict(lo=0, tg=0, fa=0, fd=0, cf=0, uf=0, osm=0))
FORMAT_OUT = dict(
    lo_o=((ROWS, D), BF16),
    tg_o=((ROWS, D), F32),
    oq=((24, 3 * D), F32),
    oo=((24, D), F32),
    ou=((24, FF), F32),
    od=((96, D), F32),
    ob=((6, 24), F32),
    ouv=((1, 96), F32),
    og=((2, 24), F32),
    xoq=((24, 3 * D), F32),
    xoo=((24, D), F32),
    xou=((24, FF), F32),
    xod=((96, D), F32),
    xob=((6, 24), F32),
    xouv=((1, 96), F32),
    xog=((2, 24), F32),
    opos=((2, D), F32),
)


def format_kernel(*refs):
    r = fields(FORMAT_IN + list(FORMAT_OUT), refs)
    me = lax.axis_index("seg")
    r.lo_o[...] = r.lo[...]
    r.tg_o[...] = r.tg[...]
    for p in range(6):
        for j in range(3):
            r.xoq[:, D * j + 128 * p : D * j + 128 * (p + 1)] = r.cf[p // 2, p % 2, :, 128 * j : 128 * (j + 1)].astype(F32)
    for i in range(2):
        r.xoo[:, W * i : W * (i + 1)] = r.cf[3, i].astype(F32)
        for n in range(4):
            m = 8 + 4 * i + n
            r.xod[24 * n : 24 * (n + 1), W * i : W * (i + 1)] = r.cf[m // 2, m % 2].astype(F32)
    for t in range(32):
        r.xou[:, 96 * t : 96 * t + 96] = r.uf[t // 4, t % 4].astype(F32)[:, 0:96]
    for n in range(8):
        j, h = n // 2, n % 2
        top = (j % 2) * 48 + 24 * h
        r.od[top : top + 24, (j // 2) * W : (j // 2 + 1) * W] = r.fd[n].astype(F32)
    for u in range(8, 16):
        r.ou[:, W * (u - 8) : W * (u - 7)] = r.fa[u].astype(F32)
    ours = pltpu.roll(r.osm[0:2].reshape(16, D), (D - 24 * me) % D, 1)
    r.ob[...] = ours[0:6, 0:24]
    r.og[...] = ours[6:8, 0:24]
    r.xob[...] = ours[8:14, 0:24]
    r.xog[...] = ours[14:16, 0:24]
    ups = pltpu.roll(r.osm[2], (D - 96 * (me % 8)) % D, 1)
    line = lax.broadcasted_iota(jnp.int32, (8, D), 0)
    r.ouv[...] = sum0(jnp.where(line == me // 8, ups, 0.0))[:, 0:96]
    r.xouv[...] = sum0(jnp.where(line == 4 + me // 8, ups, 0.0))[:, 0:96]
    r.opos[...] = pltpu.roll(r.osm[3 + me // 4], (8 - 2 * (me % 4)) % 8, 0)[0:2]
    for u in range(8):
        if u < 6:
            r.oq[:, W * u : W * (u + 1)] = r.fa[u].astype(F32)
        else:
            r.oo[:, W * (u - 6) : W * (u - 5)] = r.fa[u].astype(F32)


def call(kernel, name, ins, outs, hbm_in, hbm_out, scratch, cid, args):
    vm, hbm = pl.BlockSpec(memory_space=pltpu.VMEM), pl.BlockSpec(memory_space=pl.ANY)
    smem = pl.BlockSpec(memory_space=pltpu.SMEM)
    return pl.pallas_call(
        kernel,
        out_shape=tuple(jax.ShapeDtypeStruct(s, t) for s, t in outs.values()),
        in_specs=[smem if n == "doc" else hbm if n in hbm_in else vm for n in ins],
        out_specs=tuple(hbm if n in hbm_out else vm for n in outs),
        scratch_shapes=list(scratch.values()),
        compiler_params=pltpu.CompilerParams(
            collective_id=cid, has_side_effects=cid is not None, vmem_limit_bytes=62 << 20
        ),
        name=name,
    )(*args)


def shards(tokens, doc, qkv, out, up, down, bias, upbias, gains, cqkv, cout, cup, cdown, cbias, cupbias, cgains, pos, cot):
    fwd = call(
        forward_kernel, "forward", F_IN, F_OUT, (), F_HBM, F_SCR, 0,
        (tokens, cot, qkv, out, up, down, bias, upbias.reshape(1, 96), gains, cqkv, cout, cup, cdown, cbias,
         cupbias.reshape(1, 96), cgains, pos, doc),
    )
    saved = dict(zip(F_OUT, fwd), tok=tokens, cot=cot, doc=doc)
    back = call(
        backward_kernel, "backward", B_IN, B_OUT, F_HBM, (), B_SCR, 1, [saved[n] for n in B_IN]
    )
    saved.update(zip(B_OUT, back))
    out = call(
        format_kernel, "format", FORMAT_IN, FORMAT_OUT, (), (), {}, None, [saved[n] for n in FORMAT_IN]
    )
    out = dict(zip(FORMAT_OUT, out))
    out["ouv"], out["xouv"] = out["ouv"].reshape(96), out["xouv"].reshape(96)
    return tuple(out.values())


def solution(mesh):
    both, seg, cols, flat = P(("grp", "seg"), None), P("seg", None), P(None, "seg"), P("seg")
    weights = (seg, seg, seg, seg, cols, flat, cols)
    in_specs = (both, P("grp", None)) + weights + weights + (seg, both)
    out_specs = (both, both) + weights + weights + (seg,)
    return jax.shard_map(shards, mesh=mesh, in_specs=in_specs, out_specs=out_specs, check_vma=False)
```

```python
import functools
import math
import types

import jax
import jax.numpy as jnp
from jax import lax
from jax.experimental import pallas as pl
from jax.experimental.pallas import tpu as pltpu
from jax.sharding import PartitionSpec as P

D = 768
FF = 3072
ROWS = 384
SEG_LEN = 128
W = 384
F32, BF16 = jnp.float32, jnp.bfloat16
MESH = pl.DeviceIdType.MESH
DMA = pltpu.SemaphoreType.DMA
RSQ2 = 1.0 / math.sqrt(2.0)
RS2PI = 1.0 / math.sqrt(2.0 * math.pi)
VM = pltpu.VMEM


def dot(a, b):
    return lax.dot_general(a, b, (((1,), (0,)), ((), ())), preferred_element_type=F32)


def dot_bt(a, b):
    return lax.dot_general(a, b, (((1,), (1,)), ((), ())), preferred_element_type=F32)


def dot_at(a, b):
    return lax.dot_general(a, b, (((0,), (0,)), ((), ())), preferred_element_type=F32)


def rcopy(src, dst, ssem, rsem, seg):
    return pltpu.make_async_remote_copy(
        src_ref=src, dst_ref=dst, send_sem=ssem, recv_sem=rsem, device_id={"seg": seg}, device_id_type=MESH
    )


def zcopy(src, dst, ssem, rsem, z, seg):
    return pltpu.make_async_remote_copy(
        src_ref=src, dst_ref=dst, send_sem=ssem, recv_sem=rsem, device_id={"grp": z, "seg": seg}, device_id_type=MESH
    )


def take(ref, sem):
    pltpu.make_async_copy(ref, ref, sem).wait()


def send_to(me, target, src, dst, ssem, rsem):
    @pl.when(target != me)
    def _():
        rcopy(src, dst, ssem, rsem, target).start()

    @pl.when(target == me)
    def _():
        pltpu.make_async_copy(src, dst, rsem).start()


def loop(n, fn, first=0):
    def body(i, _):
        fn(i)
        return 0

    lax.fori_loop(first, n, body, 0)


def col(u, width=W):
    return pl.ds(pl.multiple_of(u * width, 128), width)


def norm(v):
    center = v - jnp.mean(v, axis=-1, keepdims=True)
    rstd = lax.rsqrt(jnp.mean(center * center, axis=-1, keepdims=True) + 1e-05)
    return center * rstd, rstd


def norm_back(grad, n, rstd, gain):
    dn = grad * gain
    return rstd * (dn - jnp.mean(dn, axis=-1, keepdims=True) - n * jnp.mean(dn * n, axis=-1, keepdims=True))


def gelu_both(u):
    e = jnp.exp(-0.5 * u * u)
    t = 1.0 / (1.0 + (0.3275911 * RSQ2) * jnp.abs(u))
    poly = t * (0.127414796 + t * (-0.142248368 + t * (0.7107068705 + t * (-0.7265760135 + t * 0.5307027145))))
    tail = poly * e
    cdf = jnp.where(u < 0.0, tail, 1.0 - tail)
    return u * cdf, cdf + u * (RS2PI * e)


def two_heads(v):
    lane = lax.broadcasted_iota(jnp.int32, v.shape, 1)
    none = jnp.zeros_like(v)
    return jnp.concatenate([jnp.where(lane < 64, v, none), jnp.where(lane >= 64, v, none)], axis=0)


def side_by_side(v):
    n = v.shape[0] // 2
    lane = lax.broadcasted_iota(jnp.int32, (n, 128), 1)
    return jnp.where(lane < 64, v[:n], v[n:])


def softmax(s):
    e = jnp.exp(s - jnp.max(s, axis=-1, keepdims=True))
    return e / jnp.sum(e, axis=-1, keepdims=True)


def softmax_back(w, dw):
    return w * (dw - jnp.sum(w * dw, axis=-1, keepdims=True))


def rows8(value):
    return value.reshape(value.shape[0] // 8, 8, value.shape[1])


def flat8(value):
    v = value.astype(F32)
    return v.reshape(v.shape[0] * v.shape[1], v.shape[2])


def sum0(v):
    return jnp.sum(v, axis=0, keepdims=True)


def owner_seg(k):
    return 2 * k


def pair_seg(p):
    return 4 * p + 1


def pair_first(p):
    return 5 * (p % 3) + 16 * (p // 3)


def fields(spec, refs):
    return types.SimpleNamespace(**dict(zip(spec, refs)))


CROSS = dict(
    pup=VM((32, 24, 128), BF16),
    xup=VM((32, 24, 128), BF16),
    xqkv=VM((32, 3, 24, 128), BF16),
    xout=VM((6, 24, D), BF16),
    wup=VM((D, 128), BF16),
    wqkv=VM((D, 384), BF16),
    wout=VM((128, D), BF16),
    wout_f=VM((144, D), F32),
    wdn=VM((128, D), BF16),
    msg=VM((8, D), BF16),
    x1=VM((32, 8, D), BF16),
    own=VM((8, 8, D), F32),
    rst=VM((8, 128), F32),
    xall=VM((96, D), BF16),
    q=VM((3, 96, 128), BF16),
    o=VM((96, 128), BF16),
    af=VM((192, 96), F32),
    p2=VM((12, 8, D), BF16),
    g2=VM((6, 8, D), BF16),
    p3=VM((8, D), BF16),
    g3=VM((12, 8, D), BF16),
    p4=VM((12, 8, D), BF16),
    g46=VM((64, 8, D), BF16),
    p5=VM((2, 8, D), BF16),
    g5=VM((12, 2, 8, D), BF16),
    p6=VM((12, 8, D), BF16),
    p7=VM((8, D), BF16),
    g7=VM((12, 8, D), BF16),
    p7f=VM((8, D), F32),
    g7f=VM((2, 8, D), F32),
    p8=VM((12, 8, D), BF16),
    g8=VM((6, 2, 8, D), BF16),
    gp=VM((96, 128), F32),
    gact=VM((96, 128), BF16),
    fall=VM((96, D), BF16),
    dd=VM((96, D), BF16),
    du=VM((96, 128), BF16),
    dq=VM((96, 384), BF16),
    de=VM((96, D), BF16),
    cs=DMA((12,)),
    cr=DMA((12,)),
    c7=DMA,
)


def slot_layout(doc, shape, slots):
    pos = (slots % 3) * 32 + slots // 3
    number = jnp.zeros(shape, jnp.int32)
    begin = jnp.zeros(shape, jnp.int32)
    end = jnp.int32(0)
    for d in range(6):
        begin = jnp.where(pos >= end, end, begin)
        number = jnp.where(pos >= end, d, number)
        end = end + doc[0, d]
    return number, pos - begin


class Cross:
    def __init__(self, r, a):
        self.r, self.a = r, a
        self.me = lax.axis_index("seg")
        self.is_owner = (self.me % 2 == 0) & (self.me < 24)
        self.k = self.me // 2
        self.is_pair = (self.me % 4 == 1) & (self.me < 24)
        self.p = self.me // 4

    def sem(self, e):
        return self.r.xcs.at[e], self.r.xcr.at[e]

    def seams(self):
        m = self.me % 16
        seam = (m == 5) | (m == 10)
        p0 = 3 * (self.me // 16) + jnp.where(m > 10, 2, jnp.where(m > 5, 1, 0))
        return seam, p0

    def reshard(self):
        r, a, me = self.r, self.a, self.me
        s0, r0 = self.sem(0)
        s1, r1 = self.sem(1)
        s2, r2 = self.sem(2)
        r.pup[...] = jnp.zeros((32, 24, 128), BF16)
        up = a.cup[...].astype(F32)
        for t in range(32):
            r.pup[t, :, 0:96] = up[:, 96 * t : 96 * t + 96].astype(BF16)
        loop(32, lambda t: send_to(me, t, r.pup.at[t], r.xup.at[me], s0, r0))

        def to_pair(p):
            for j in range(3):
                part = pl.ds(pl.multiple_of(D * j + 128 * p, 128), 128)
                send_to(me, pair_seg(p), a.cqkv.at[:, part], r.xqkv.at[me, j], s1, r1)
            first = pair_first(p)

            @pl.when((me >= first) & (me < first + 6))
            def _():
                send_to(me, pair_seg(p), a.cout, r.xout.at[me - first], s2, r2)

        loop(6, to_pair)
        r.wdn[0:96, :] = a.cdown[...]
        r.wdn[96:128, :] = jnp.zeros((32, D), BF16)

    def reshard_end(self):
        r = self.r
        take(r.xup, r.xcr.at[0])
        self.reshard_sent()
        r.wup[...] = r.xup[...].astype(F32).reshape(D, 128).astype(BF16)

        @pl.when(self.is_pair)
        def _():
            take(r.xqkv, r.xcr.at[1])
            for j in range(3):
                r.wqkv[:, 128 * j : 128 * (j + 1)] = r.xqkv[:, j].astype(F32).reshape(D, 128).astype(BF16)
            take(r.xout, r.xcr.at[2])
            r.wout_f[...] = r.xout[...].astype(F32).reshape(144, D)
            off = pl.multiple_of(8 * (self.p % 3), 8)
            r.wout[...] = r.wout_f[pl.ds(off, 128), :].astype(BF16)

    def reshard_sent(self):
        r, me = self.r, self.me
        take(r.xup.at[pl.ds(0, 31)], r.xcs.at[0])

        @pl.when(self.is_pair)
        def _():
            take(r.xqkv.at[pl.ds(0, 5)], r.xcs.at[1])

        @pl.when(jnp.logical_not(self.is_pair))
        def _():
            take(r.xqkv.at[pl.ds(0, 6)], r.xcs.at[1])

        seam, p0 = self.seams()
        hits = jnp.where(me == pair_seg(p0), 1, 0) + jnp.where(seam & (me == pair_seg(p0 + 1)), 1, 0)
        count = jnp.where(seam, 2, 1) - hits
        for n in (1, 2):

            @pl.when(count == n)
            def _():
                take(r.xout.at[pl.ds(0, n)], r.xcs.at[2])

    def start(self, z0, dy0):
        r, a, me = self.r, self.a, self.me
        row = lax.broadcasted_iota(jnp.int32, (8, 512), 0)
        lane = lax.broadcasted_iota(jnp.int32, (8, 512), 1)
        _, place = slot_layout(a.doc, (8, 512), jnp.minimum(me * 3 + row, 95))
        table = a.smg[...].astype(F32).reshape(512, W)[:, 256:384].astype(BF16)
        parts = []
        for i in range(6):
            hot = (lane == (place // 2) * 16 + (place % 2) * 6 + i) & (row < 3)
            parts.append(dot(hot.astype(BF16), table))
        cross_in = z0 + jnp.concatenate(parts, axis=1)
        rowd = lax.broadcasted_iota(jnp.int32, (8, D), 0)
        both = jnp.where(rowd < 3, cross_in, pltpu.roll(dy0, 3, 0))
        r.msg[...] = jnp.where(rowd < 6, both, 0.0).astype(BF16)
        ss, rs = self.sem(3)
        loop(6, lambda p: send_to(me, pair_seg(p), r.msg, r.x1.at[me], ss, rs))
        loop(12, lambda k: send_to(me, owner_seg(k), r.msg, r.x1.at[me], ss, rs))

    def pick(self, n, first, base):
        row = lax.broadcasted_iota(jnp.int32, (n, 256), 0) + first
        lane = lax.broadcasted_iota(jnp.int32, (n, 256), 1)
        return (lane == (row // 3) * 8 + row % 3 + base).astype(BF16)

    def attention(self):
        r, a, me = self.r, self.a, self.me
        ss, rs = self.sem(4)

        @pl.when(self.is_pair)
        def _():
            take(r.x1, r.xcr.at[3])
            msgs = flat8(r.x1[...]).astype(BF16)
            xall = dot(self.pick(96, 0, 0), msgs).astype(BF16)
            r.xall[...] = xall
            part = col(self.p, 128)
            joined = dot(xall, r.wqkv[...])
            q = (joined[:, 0:128] + a.cb[0:1, part]).astype(BF16)
            k = joined[:, 128:256].astype(BF16)
            v = (joined[:, 256:384] + a.cb[1:2, part]).astype(BF16)
            r.q[0], r.q[1], r.q[2] = q, k, v
            line = lax.broadcasted_iota(jnp.int32, (192, 96), 0)
            doc_r, _ = slot_layout(a.doc, (192, 96), jnp.where(line < 96, line, line - 96))
            doc_c, _ = slot_layout(a.doc, (192, 96), lax.broadcasted_iota(jnp.int32, (192, 96), 1))
            w = softmax(jnp.where(doc_r == doc_c, dot_bt(two_heads(q), k) * 0.125, -1e30))
            r.af[...] = w
            o = side_by_side(dot(w.astype(BF16), v)).astype(BF16)
            r.o[...] = o
            r.p2[...] = rows8(dot(o, r.wout[...])).astype(BF16)
            loop(12, lambda k: send_to(me, owner_seg(k), r.p2.at[k], r.g2.at[self.p], ss, rs))

    def first_norm(self):
        r, a, me = self.r, self.a, self.me
        ss, rs = self.sem(5)

        @pl.when(self.is_owner)
        def _():
            take(r.x1, r.xcr.at[3])
            msgs = flat8(r.x1[...]).astype(BF16)
            x = dot(self.pick(8, 8 * self.k, 0), msgs)
            r.own[1] = dot(self.pick(8, 8 * self.k, 3), msgs)
            take(r.g2, r.xcr.at[4])
            total = jnp.sum(r.g2[...].astype(F32), axis=0)
            n, rstd = norm(x + (total + a.cb[2:3, :]))
            r.own[2] = n
            r.xrst[...] = jnp.broadcast_to(rstd, (8, 128))
            r.p3[...] = (n * a.cb[6:7, :] + a.cb[3:4, :]).astype(BF16)
            loop(32, lambda t: send_to(me, t, r.p3, r.g3.at[self.k], ss, rs))

    def mlp(self):
        r, a, me = self.r, self.a, self.me
        ss, rs = self.sem(6)
        take(r.g3, r.xcr.at[5])
        f = flat8(r.g3[...]).astype(BF16)
        r.fall[...] = f
        g, gp = gelu_both(dot(f, r.wup[...]) + a.cub[0:1, :])
        r.gp[...] = gp
        g = g.astype(BF16)
        r.gact[...] = g
        r.p4[...] = rows8(dot(g, r.wdn[...])).astype(BF16)
        loop(12, lambda k: send_to(me, owner_seg(k), r.p4.at[k], r.g46.at[me], ss, rs))

    def second_norm(self):
        r, a, me = self.r, self.a, self.me
        ss, rs = self.sem(7)

        @pl.when(self.is_owner)
        def _():
            take(r.g46.at[pl.ds(0, 32)], r.xcr.at[6])
            total = jnp.sum(r.g46[0:32].astype(F32), axis=0)
            n, rstd = norm(r.p3[...].astype(F32) + (total + a.cb[4:5, :]))
            y = n * a.cb[7:8, :] + a.cb[5:6, :]
            dr2 = norm_back(r.own[1], n, rstd, a.cb[7:8, :])
            r.own[3] = n
            r.own[4] = dr2
            r.p5[0] = dr2.astype(BF16)
            r.p5[1] = y.astype(BF16)
            loop(32, lambda t: send_to(me, t, r.p5, r.g5.at[self.k], ss, rs))

    def mlp_back(self):
        r, me = self.r, self.me
        ss, rs = self.sem(8)
        take(r.g5, r.xcr.at[7])
        dd = flat8(r.g5[:, 0]).astype(BF16)
        r.xdd[...] = dd
        du = (dot_bt(dd, r.wdn[...]) * r.gp[...]).astype(BF16)
        r.du[...] = du
        r.p6[...] = rows8(dot_bt(du, r.wup[...])).astype(BF16)
        loop(12, lambda k: send_to(me, owner_seg(k), r.p6.at[k], r.g46.at[32 + me], ss, rs))

    def window(self, seg):
        return jnp.minimum((3 * seg) // 8, 10)

    def first_norm_back(self):
        r, a, me = self.r, self.a, self.me
        ss, rs = self.sem(9)
        fr = r.xcr.at[10]

        @pl.when(self.is_owner)
        def _():
            take(r.g46.at[pl.ds(32, 32)], r.xcr.at[8])
            df = jnp.sum(r.g46[32:64].astype(F32), axis=0) + r.own[4]
            r.own[5] = df
            dr1 = norm_back(df, r.own[2], r.xrst[:, 0:1], a.cb[6:7, :])
            r.p7[...] = dr1.astype(BF16)
            loop(6, lambda p: send_to(me, pair_seg(p), r.p7, r.g7.at[self.k], ss, rs))
            r.p7f[...] = dr1

            def one(t):
                w = self.window(t)

                @pl.when((w == self.k) | (w + 1 == self.k))
                def _():
                    send_to(me, t, r.p7f, r.g7f.at[self.k - w], r.c7, fr)

            loop(32, one)

    def attention_back(self):
        r, me = self.r, self.me
        ss, rs = self.sem(11)

        @pl.when(self.is_pair)
        def _():
            take(r.g7, r.xcr.at[9])
            de = flat8(r.g7[...]).astype(BF16)
            r.xde[...] = de
            do = dot_bt(de, r.wout[...]).astype(BF16)
            q, k, v = r.q[0], r.q[1], r.q[2]
            do2, w = two_heads(do), r.af[...]
            ds = softmax_back(w, dot_bt(do2, v)).astype(BF16)
            r.dq[:, 0:128] = (side_by_side(dot(ds, k)) * 0.125).astype(BF16)
            r.dq[:, 128:256] = (dot_at(ds, two_heads(q)) * 0.125).astype(BF16)
            r.dq[:, 256:384] = dot_at(w.astype(BF16), do2).astype(BF16)
            r.p8[...] = rows8(dot_bt(r.dq[...], r.wqkv[...])).astype(BF16)
            loop(32, lambda t: send_to(me, t, r.p8.at[pl.ds(self.window(t), 2)], r.g8.at[self.p], ss, rs))

    def finish(self):
        r = self.r
        take(r.g7f, r.xcr.at[10])
        take(r.g8, r.xcr.at[11])
        total = r.g7f[...] + jnp.sum(r.g8[...].astype(F32), axis=0)
        shift = 3 * self.me - 8 * self.window(self.me)
        return pltpu.roll(total.reshape(16, D), 16 - shift, 0)[0:8]

    def output_rows(self):
        w = self.window(self.me)
        y = self.r.g5[pl.ds(w, 2), 1].astype(F32).reshape(16, D)
        return pltpu.roll(y, 16 - (3 * self.me - 8 * w), 0)[0:8]

    def grads(self):
        r, a = self.r, self.a
        a.pu[...] = dot_at(r.fall[...], r.du[...]).reshape(32, 24, 128).astype(BF16)
        a.gdn[...] = dot_at(r.gact[...], r.xdd[...])[0:96].astype(BF16)

        @pl.when(self.is_pair)
        def _():
            for j in range(3):
                part = dot_at(r.xall[...], r.dq[:, 128 * j : 128 * (j + 1)])
                a.pq[:, j] = part.reshape(32, 24, 128).astype(BF16)
            r.po_f[...] = jnp.zeros((144, D), F32)
            off = pl.multiple_of(8 * (self.p % 3), 8)
            r.po_f[pl.ds(off, 128), :] = dot_at(r.o[...], r.xde[...])
            a.po[...] = r.po_f[...].reshape(6, 24, D).astype(BF16)

        a.small[...] = jnp.zeros((8, D), F32)

        @pl.when(self.is_owner)
        def _():
            dr1, df, dr2, dy = r.p7[...].astype(F32), r.own[5], r.own[4], r.own[1]
            dd = r.p5[0].astype(F32)
            for row, v in ((2, dr1), (3, df), (4, dd), (5, dy), (6, df * r.own[2]), (7, dy * r.own[3])):
                a.small[row : row + 1, :] = sum0(v)

        @pl.when(self.is_pair)
        def _():
            part = col(self.p, 128)
            a.small[0:1, part] = sum0(r.dq[:, 0:128].astype(F32))
            a.small[1:2, part] = sum0(r.dq[:, 256:384].astype(F32))

        a.dc[...] = jnp.broadcast_to(sum0(r.du[...].astype(F32)), (8, 128))

    def drain(self):
        r, me = self.r, self.me
        cs = r.xcs

        def some(e, ref, count, fewer):
            @pl.when(fewer)
            def _():
                take(ref.at[pl.ds(0, count - 1)], cs.at[e])

            @pl.when(jnp.logical_not(fewer))
            def _():
                take(ref.at[pl.ds(0, count)], cs.at[e])

        some(3, r.g46, 18, self.is_pair | self.is_owner)
        some(6, r.g46, 12, self.is_owner)
        some(8, r.g46, 12, self.is_owner)

        @pl.when(self.is_pair)
        def _():
            take(r.g46.at[pl.ds(0, 12)], cs.at[4])
            take(r.g46.at[pl.ds(0, 62)], cs.at[11])

        @pl.when(self.is_owner)
        def _():
            take(r.g46.at[pl.ds(0, 31)], cs.at[5])
            take(r.g46.at[pl.ds(0, 62)], cs.at[7])
            take(r.g46.at[pl.ds(0, 6)], cs.at[9])

            count = jnp.int32(0)
            for t in range(32):
                w = min(3 * t // 8, 10)
                count += jnp.where(((self.k == w) | (self.k == w + 1)) & (me != t), 1, 0)
            for n in range(1, 10):

                @pl.when(count == n)
                def _():
                    take(r.g46.at[pl.ds(0, 2 * n)], r.c7)


class CrossGrads(Cross):
    def scatter(self):
        r, a, me = self.r, self.a, self.me
        loop(32, lambda t: send_to(me, t, a.pu.at[t], r.gup.at[me], r.ks.at[0], r.kr.at[0]))

        @pl.when(self.is_pair)
        def _():
            loop(32, lambda t: send_to(me, t, a.pq.at[t], r.gqkv.at[self.p], r.ks.at[1], r.kr.at[1]))
            loop(
                6,
                lambda i: send_to(
                    me, pair_first(self.p) + i, a.po.at[i], r.go.at[self.p % 2], r.ks.at[2], r.kr.at[2]
                ),
            )

    def planes(self, red):
        r, a, me, z = self.r, self.a, self.me, red.z
        take(r.gup, r.kr.at[0])
        take(r.gqkv, r.kr.at[1])
        for i in range(6):
            for j in range(3):
                r.c0[i, :, 128 * j : 128 * (j + 1)] = r.gqkv[i, j]
        seam, p0 = self.seams()

        @pl.when(seam)
        def _():
            take(r.go, r.kr.at[2])
            both = (r.go[0].astype(F32) + r.go[1].astype(F32)).astype(BF16)
            for i in range(2):
                r.c0[6 + i] = both[:, W * i : W * (i + 1)]

        @pl.when(jnp.logical_not(seam))
        def _():
            take(r.go.at[0], r.kr.at[2])
            for i in range(2):
                r.c0[6 + i] = r.go[p0 % 2, :, W * i : W * (i + 1)]

        gdn = a.gdn[...].astype(F32).reshape(4, 24, D)
        for i in range(2):
            for n in range(4):
                r.c0[8 + 4 * i + n] = gdn[n, :, W * i : W * (i + 1)].astype(BF16)

        def out(zz):
            zcopy(r.c0.at[pl.ds(2 * zz, 2)], r.cr.at[z], r.xs.at[1], r.xr.at[1], zz, me).start()
            zcopy(r.gup.at[pl.ds(4 * zz, 4)], r.ur.at[z], r.xs.at[2], r.xr.at[2], zz, me).start()

        red.peers(out)
        pltpu.make_async_copy(r.c0.at[pl.ds(2 * z, 2)], r.cr.at[z], r.xr.at[1]).start()
        pltpu.make_async_copy(r.gup.at[pl.ds(4 * z, 4)], r.ur.at[z], r.xr.at[2]).start()

    def planes_sum(self, red):
        r, me, z = self.r, self.me, red.z
        take(r.cr, r.xr.at[1])
        r.cs[...] = jnp.sum(r.cr[...].astype(F32), axis=0).astype(BF16)
        take(r.ur, r.xr.at[2])
        r.us[...] = jnp.sum(r.ur[...].astype(F32), axis=0).astype(BF16)

        def back(zz):
            zcopy(r.cs, r.cf.at[z], r.xs.at[4], r.xr.at[4], zz, me).start()
            zcopy(r.us, r.uf.at[z], r.xs.at[5], r.xr.at[5], zz, me).start()

        red.peers(back)
        pltpu.make_async_copy(r.cs, r.cf.at[z], r.xr.at[4]).start()
        pltpu.make_async_copy(r.us, r.uf.at[z], r.xr.at[5]).start()

    def end(self):
        r, me = self.r, self.me
        take(r.cf, r.xr.at[4])
        take(r.uf, r.xr.at[5])
        take(r.gup.at[pl.ds(0, 31)], r.ks.at[0])

        @pl.when(self.is_pair)
        def _():
            take(r.pq.at[pl.ds(0, 31)], r.ks.at[1])
            first = pair_first(self.p)
            inside = (me >= first) & (me < first + 6)

            @pl.when(inside)
            def _():
                take(r.po.at[pl.ds(0, 5)], r.ks.at[2])

            @pl.when(jnp.logical_not(inside))
            def _():
                take(r.po, r.ks.at[2])

        for n, buf in ((1, r.cr), (2, r.ur), (4, r.cr), (5, r.ur)):
            take(buf.at[pl.ds(0, 7)], r.xs.at[n])


class Plane:
    def __init__(self):
        self.me = lax.axis_index("seg")
        self.x, self.y, self.c = self.me // 8, (self.me // 2) % 4, self.me % 2
        self.other = self.me + 1 - 2 * self.c

    def seg(self, on_x, step):
        if on_x:
            return (((self.x + step) % 4) * 4 + self.y) * 2 + self.c
        return (self.x * 4 + (self.y + step) % 4) * 2 + self.c

    def ring(self, part, which, step):
        return self.seg((part == 0) == (which == 1), step)

    def pos(self, part, which):
        return self.x if (part == 0) == (which == 1) else self.y

    def by_part(self, k, fn):
        for part in range(2):
            pl.when(k % 2 == part)(functools.partial(fn, part))

    @staticmethod
    def ahead(k):
        return 1 + 2 * ((k // 2) % 2)


class Gather(Plane):
    def __init__(self, r):
        super().__init__()
        self.r = r

    def v1(self, k, part, off):
        mine = self.r.ws.at[self.c, k]
        return mine.at[(self.x + off) % 4, self.y] if part == 0 else mine.at[self.x, (self.y + off) % 4]

    def v2(self, k, part, off):
        mine = self.r.ws.at[self.c, k]
        return mine.at[:, (self.y + off) % 4] if part == 0 else mine.at[(self.x + off) % 4]

    def first(self, k):
        r = self.r

        def go(part):
            own = self.v1(k, part, 0)
            src = r.stage.at[k]
            pltpu.make_async_copy(src, own, r.own_sem.at[k]).start()
            rcopy(src, own, r.s1, r.r1.at[k, 0], self.ring(part, 1, 1)).start()
            rcopy(src, own, r.s1, r.r1.at[k, 1], self.ring(part, 1, 3)).start()

        self.by_part(k, go)

    def first_on(self, k):
        r, ahead = self.r, self.ahead(k)

        def go(part):
            block = self.v1(k, part, 4 - ahead)
            take(block, r.r1.at[k, ahead // 2])
            rcopy(block, block, r.s1, r.r1.at[k, 1 - ahead // 2], self.ring(part, 1, ahead)).start()

        self.by_part(k, go)

    def second(self, k):
        r, ahead = self.r, self.ahead(k)

        def go(part):
            take(r.ws.at[0, 0, 0, pl.ds(0, 2)], r.r1.at[k, 1 - ahead // 2])
            own = self.v1(k, part, 0)
            take(own, r.own_sem.at[k])
            row = self.v2(k, part, 0)
            rcopy(row, row, r.s2, r.r2.at[k, 0], self.ring(part, 2, 1)).start()
            rcopy(row, row, r.s2, r.r2.at[k, 1], self.ring(part, 2, 3)).start()
            rcopy(row, row, r.s3, r.r3.at[k], self.other).start()

        self.by_part(k, go)

    def second_on(self, k):
        r, ahead = self.r, self.ahead(k)

        def go(part):
            row = self.v2(k, part, 4 - ahead)
            take(row, r.r2.at[k, ahead // 2])
            rcopy(row, row, r.s2, r.r2.at[k, 2], self.ring(part, 2, ahead)).start()
            rcopy(row, row, r.s3, r.r3.at[k], self.other).start()
            row = self.v2(k, part, ahead)
            take(row, r.r2.at[k, 1 - ahead // 2])
            rcopy(row, row, r.s3, r.r3.at[k], self.other).start()

        self.by_part(k, go)

    def last(self, k):
        r = self.r

        def go(part):
            row = self.v2(k, part, 2)
            take(row, r.r2.at[k, 2])
            rcopy(row, row, r.s3, r.r3.at[k], self.other).start()

        self.by_part(k, go)

    def arrived(self, k):
        r = self.r
        take(r.ws.at[1 - self.c, k], r.r3.at[k])

    def drain(self):
        r = self.r

        take(r.ws.at[0, pl.ds(0, 9), 0], r.s1)
        take(r.ws.at[0, pl.ds(0, 9)], r.s2)
        take(r.ws.at[0], r.s3)


class Reduce(Plane):
    def __init__(self, r, pieces):
        super().__init__()
        self.r, self.pieces = r, pieces
        self.z = lax.axis_index("grp")

    def peers(self, fn):
        loop(7, lambda i: fn((self.z + 1 + i) % 8))

    def to_sibling(self, k):
        r = self.r
        rcopy(r.gb.at[1, k], r.r0.at[k], r.ms.at[0], r.mr.at[k, 0], self.other).start()

    def msg(self, k, part, q):
        return self.r.gb.at[0, k, :, q] if part == 0 else self.r.gb.at[0, k, q]

    def step_a(self, k):
        r, ahead = self.r, self.ahead(k)
        take(r.r0.at[k], r.mr.at[k, 0])

        def add(i):
            px, py = i // 4, i % 4
            r.gb[0, k, px, py] = (r.gb[0, k, px, py].astype(F32) + r.r0[k, px, py].astype(F32)).astype(BF16)

        loop(16, add)

        def go(part):
            q = self.pos(part, 2)
            far, back = self.msg(k, part, (q + 2) % 4), self.msg(k, part, (q + 4 - ahead) % 4)
            rcopy(far, r.f2.at[k], r.ms.at[1], r.mr.at[k, 1], self.ring(part, 2, ahead)).start()
            rcopy(back, r.b2.at[k], r.ms.at[1], r.mr.at[k, 2], self.ring(part, 2, 4 - ahead)).start()

        self.by_part(k, go)

    def step_b(self, k):
        r, ahead = self.r, self.ahead(k)
        take(r.f2.at[k], r.mr.at[k, 1])

        def go(part):
            block = self.msg(k, part, (self.pos(part, 2) + ahead) % 4)

            def add(i):
                block[i] = (block[i].astype(F32) + r.f2[k, i].astype(F32)).astype(BF16)

            loop(4, add)
            rcopy(block, r.a2.at[k], r.ms.at[1], r.mr.at[k, 2], self.ring(part, 2, ahead)).start()

        self.by_part(k, go)

    def step_c(self, k):
        r, ahead = self.r, self.ahead(k)
        take(r.r0.at[0, pl.ds(0, 2)], r.mr.at[k, 2])

        def go(part):
            block = self.msg(k, part, self.pos(part, 2))

            def add(i):
                r.t1[k, i] = (block[i].astype(F32) + r.a2[k, i].astype(F32) + r.b2[k, i].astype(F32)).astype(BF16)

            loop(4, add)
            q = self.pos(part, 1)
            far, back = r.t1.at[k, (q + 2) % 4], r.t1.at[k, (q + 4 - ahead) % 4]
            rcopy(far, r.f1.at[k], r.ms.at[2], r.mr.at[k, 3], self.ring(part, 1, ahead)).start()
            rcopy(back, r.b1.at[k], r.ms.at[2], r.mr.at[k, 4], self.ring(part, 1, 4 - ahead)).start()

        self.by_part(k, go)

    def step_d(self, k):
        r, ahead = self.r, self.ahead(k)
        take(r.f1.at[k], r.mr.at[k, 3])

        def go(part):
            n = (self.pos(part, 1) + ahead) % 4
            r.t1[k, n] = (r.t1[k, n].astype(F32) + r.f1[k].astype(F32)).astype(BF16)
            rcopy(r.t1.at[k, n], r.a1.at[k], r.ms.at[2], r.mr.at[k, 4], self.ring(part, 1, ahead)).start()

        self.by_part(k, go)

    def step_e(self, k):
        r = self.r
        take(r.r0.at[0, 0, pl.ds(0, 2)], r.mr.at[k, 4])

        def go(part):
            t = r.t1[k, self.pos(part, 1)].astype(F32) + r.a1[k].astype(F32) + r.b1[k].astype(F32)
            self.pieces[k // 4, pl.ds(2 * (k % 4), 2)] = t.reshape(2, 24, W).astype(BF16)

        self.by_part(k, go)

    def tick(self, t, slots):
        for lag, step in ((0, self.step_a), (3, self.step_b), (6, self.step_c), (8, self.step_d), (10, self.step_e)):

            @pl.when((t >= lag) & (t < lag + slots))
            def _():
                step(t - lag)

    def sent(self, slots):
        r = self.r
        some = pl.ds(0, slots * 3 // 4)
        take(r.r0, r.ms.at[0])
        take(r.r0.at[some], r.ms.at[1])
        take(r.r0.at[some, 0], r.ms.at[2])

    def z_send(self, g):
        r, z, me = self.r, self.z, self.me
        self.peers(lambda zz: zcopy(r.zp.at[g, zz], r.zr.at[g, z], r.zss.at[g, 0], r.zsr.at[g, 0], zz, me).start())
        pltpu.make_async_copy(r.zp.at[g, z], r.zr.at[g, z], r.zsr.at[g, 0]).start()

    def z_sum(self, g):
        r, z, me, c = self.r, self.z, self.me, self.c
        take(r.zr.at[g], r.zsr.at[g, 0])
        r.zs[g] = jnp.sum(r.zr[g].astype(F32), axis=0).astype(BF16)
        m, h = z // 2, z % 2

        def out(dst, sem, seg):
            def one(zz):
                here = (zz == z) & (seg == me)

                @pl.when(here)
                def _():
                    pltpu.make_async_copy(r.zs.at[g], dst, sem).start()

                @pl.when(jnp.logical_not(here))
                def _():
                    zcopy(r.zs.at[g], dst, r.zss.at[g, 1], sem, zz, seg).start()

            loop(8, one)

        if g == 0:
            out(r.fd.at[z], r.zsr.at[0, 1], me)
        elif g == 1:
            out(r.fa.at[8 + 2 * m + c], r.zsr.at[1, 1], me - c + h)
        else:
            out(r.fa.at[2 * ((m + 3) % 4) + c], r.zsr.at[2, 1], me - c + h)

    def z_sent(self):
        r, z, c = self.r, self.z, self.c
        for g in range(3):
            take(r.zr.at[g, pl.ds(0, 7)], r.zss.at[g, 0])
            stays = (z % 2 == c) if g > 0 else (z >= 0)

            @pl.when(stays)
            def _():
                take(r.zr.at[g, pl.ds(0, 7)], r.zss.at[g, 1])

            @pl.when(jnp.logical_not(stays))
            def _():
                take(r.zr.at[g], r.zss.at[g, 1])


F_IN = list(dict(tok=0, cot=0, qkv=0, out=0, up=0, down=0, bias=0, upbias=0, gains=0, cqkv=0, cout=0, cup=0, cdown=0, cbias=0, cupbias=0, cgains=0, pos=0, doc=0))
F_OUT = dict(
    lo_h=((ROWS, D), BF16),
    tg_h=((ROWS, D), F32),
    fa=((16, 24, W), BF16),
    fd=((8, 24, W), BF16),
    cf=((8, 2, 24, W), BF16),
    uf=((8, 4, 24, 128), BF16),
    osm=((12, 8, D), BF16),
)


def reduce_scratch(n):
    unit, line = (4, 4, 48, W), (n, 4, 48, W)
    return dict(
        gb=VM((2, n) + unit, BF16),
        r0=VM((n,) + unit, BF16),
        f2=VM(line, BF16),
        a2=VM(line, BF16),
        b2=VM(line, BF16),
        t1=VM(line, BF16),
        f1=VM((n, 48, W), BF16),
        a1=VM((n, 48, W), BF16),
        b1=VM((n, 48, W), BF16),
        mr=DMA((n, 5)),
        ms=DMA((3,)),
    )


F_SCR = dict(
    ws=VM((2, 12, 4, 4, 48, W), BF16),
    stage=VM((12, 48, W), BF16),
    sibq=VM((24, 3 * D), BF16),
    sibo=VM((24, D), BF16),
    sibu=VM((24, FF), BF16),
    smf=VM((16, W), F32),
    sm=VM((16, W), BF16),
    smg=VM((32, 16, W), BF16),
    both=VM((16, D), F32),
    lb=VM((8, D), F32),
    lub=VM((1, FF), F32),
    cub=VM((8, 128), F32),
    cb=VM((8, D), F32),
    qkvv=VM((3, ROWS, D), BF16),
    mix=VM((ROWS, D), BF16),
    aw=VM((3, 6, 256, 128), BF16),
    n1=VM((ROWS, D), F32),
    f=VM((ROWS, D), BF16),
    g=VM((ROWS, FF), BF16),
    gpl=VM((ROWS, FF), BF16),
    rst=VM((ROWS, 128), F32),
    dd=VM((ROWS, D), BF16),
    hf=VM((8, D), BF16),
    hg=VM((8, FF), BF16),
    hgp=VM((8, FF), F32),
    hn=VM((2, 8, D), F32),
    hrst=VM((2, 8, 128), F32),
    hgs=VM((32, 8, 128), BF16),
    hfp=VM((8, W), BF16),
    hdp=VM((8, W), BF16),
    hdd=VM((8, D), BF16),
    hdf=VM((8, D), F32),
    hs=DMA((3,)),
    hr=DMA((3,)),
    sib_s=DMA((3,)),
    sib_r=DMA((3,)),
    sm_s=DMA,
    sm_r=DMA,
    own_sem=DMA((12,)),
    s1=DMA,
    r1=DMA((12, 2)),
    s2=DMA,
    r2=DMA((12, 3)),
    s3=DMA,
    r3=DMA((12,)),
    lo=VM((ROWS, D), BF16),
    tg=VM((ROWS, D), F32),
    done=DMA((2,)),
    sloc=VM((8, D), F32),
    dcl=VM((1, FF), F32),
    dx=VM((8, D), F32),
    hfa=VM((32, 8, W), BF16),
    hda=VM((32, 8, W), BF16),
    hgr=VM((32, 8, 128), BF16),
    gdn=VM((96, D), BF16),
    small=VM((8, D), F32),
    dc=VM((8, 128), F32),
    gup=VM((32, 24, 128), BF16),
    gqkv=VM((6, 3, 24, 128), BF16),
    go=VM((2, 24, D), BF16),
    cu=VM((2, 16, 24, 128), BF16),
    zc=VM((24, W), F32),
    zp=VM((3, 8, 24, W), BF16),
    zr=VM((3, 8, 24, W), BF16),
    zs=VM((3, 24, W), BF16),
    c0=VM((16, 24, W), BF16),
    cr=VM((8, 2, 24, W), BF16),
    cs=VM((2, 24, W), BF16),
    ur=VM((8, 4, 24, 128), BF16),
    us=VM((4, 24, 128), BF16),
    sf=VM((96, D), F32),
    s0=VM((12, 8, D), BF16),
    sm1=VM((8, D), BF16),
    sm2=VM((8, D), BF16),
    xr=DMA((8,)),
    xs=DMA((8,)),
    zsr=DMA((3, 2)),
    zss=DMA((3, 2)),
    ks=DMA((4,)),
    kr=DMA((4,)),
    free=pltpu.SemaphoreType.REGULAR,
    mr2=DMA((4, 5)),
    ms2=DMA((3,)),
    **reduce_scratch(8),
    **{("x" + n if n in ("rst", "dd", "de", "cs", "cr") else n): v for n, v in CROSS.items()},
)


def layer_kernel(*refs):
    r = fields(F_IN + list(F_OUT) + list(F_SCR), refs)
    ring = Gather(r)
    cross = CrossGrads(r, r)
    again = types.SimpleNamespace(
        gb=r.ws.at[:, pl.ds(4, 4)],
        r0=r.ws.at[0, pl.ds(8, 4)],
        f2=r.ws.at[1, 8],
        a2=r.ws.at[1, 9],
        b2=r.ws.at[1, 10],
        t1=r.ws.at[1, 11],
        f1=r.stage.at[pl.ds(0, 4)],
        a1=r.stage.at[pl.ds(4, 4)],
        b1=r.stage.at[pl.ds(8, 4)],
        mr=r.mr2,
        ms=r.ms2,
    )
    red, red2 = Reduce(r, r.zp.at[pl.ds(0, 2)]), Reduce(again, r.zp.at[pl.ds(2, 1)])
    me, c, z = ring.me, ring.c, red.z
    is_owner = (c == 0) & (me < 24)
    r.n2, r.de, r.do = r.tg, r.f, r.dd
    r.pcu, r.po_f, r.pu, r.pq, r.po = r.xup, r.wout_f, r.pup, r.xqkv, r.xout
    r.sz, r.sg = r.g46.at[pl.ds(0, 32)], r.g46.at[pl.ds(32, 32)]
    bar = pltpu.get_barrier_semaphore()
    loop(31, lambda i: pl.semaphore_signal(bar, inc=1, device_id={"seg": (me + 1 + i) % 32}, device_id_type=MESH))

    def greet(zz):
        for seg in (me, red.other):
            pl.semaphore_signal(bar, inc=1, device_id={"grp": zz, "seg": seg}, device_id_type=MESH)

    red.peers(greet)
    r.smf[...] = jnp.zeros((16, W), F32)
    r.smf[0:6, 0:24] = r.bias[...].astype(F32)
    r.smf[6:8, 0:24] = r.gains[...].astype(F32)
    r.smf[8:14, 0:24] = r.cbias[...].astype(F32)
    r.smf[14:16, 0:24] = r.cgains[...].astype(F32)
    r.smf[0:1, 128:224] = r.upbias[...].astype(F32)
    table = r.pos[...].astype(F32)
    for t in range(2):
        for i in range(6):
            r.smf[6 * t + i : 6 * t + i + 1, 256:384] = table[t : t + 1, 128 * i : 128 * (i + 1)]
    r.sm[...] = r.smf[...].astype(BF16)
    r.cub[...] = jnp.zeros((8, 128), F32)
    r.cub[0:1, 0:96] = r.cupbias[...].astype(F32)
    pl.semaphore_wait(bar, 45)

    swaps = [(r.qkv, r.sibq), (r.out, r.sibo), (r.up, r.sibu)]
    for i, (src, dst) in enumerate(swaps):
        rcopy(src, dst, r.sib_s.at[i], r.sib_r.at[i], ring.other).start()
    for j in range(4):
        r.stage[8 + j] = r.down[(j % 2) * 48 : (j % 2) * 48 + 48, (j // 2) * W : (j // 2 + 1) * W]

    def compose(k, src, sib, block):
        own = src[:, col(block)].astype(F32)
        oth = sib[:, col(block)].astype(F32)
        lo, hi = jnp.where(c == 0, own, oth), jnp.where(c == 0, oth, own)
        r.stage[k] = jnp.concatenate([lo, hi], axis=0).astype(BF16)
        ring.first(k)

    def arrive(i):
        take(swaps[i][1], r.sib_r.at[i])

    arrive(0)
    loop(3, lambda k: compose(k, r.qkv, r.sibq, 2 * k + c))
    arrive(1)
    compose(3, r.out, r.sibo, c)
    arrive(2)
    loop(8, lambda k: compose(k, r.up, r.sibu, 2 * (k - 4) + c), 4)
    loop(12, ring.first, 8)
    loop(32, lambda t: send_to(me, t, r.sm, r.smg.at[me], r.sm_s, r.sm_r))
    loop(12, ring.first_on)
    loop(6, ring.second)
    cross.reshard()

    take(r.smg, r.sm_r)
    for t in range(32):
        block = r.smg[t].astype(F32)
        r.both[:, 24 * t : 24 * t + 24] = block[:, 0:24]
        r.lub[:, 96 * t : 96 * t + 96] = block[0:1, 128:224]
    r.lb[...] = r.both[0:8, :]
    r.cb[...] = r.both[8:16, :]

    def tick(k):
        ring.second_on(k)

        @pl.when(k < 6)
        def _():
            ring.second(k + 6)

        @pl.when(k >= 3)
        def _():
            ring.last(k - 3)

    def weight(cc, k):
        return r.ws[cc, k].reshape(D, W)

    loop(5, tick)

    def project(k):
        tick(k)
        i = k - 5
        ring.arrived(i)
        shift = jnp.where(i == 0, r.lb[0:1, :], jnp.where(i == 2, r.lb[1:2, :], 0.0))
        for cc in range(2):
            part = slice(cc * W, (cc + 1) * W)
            r.qkvv[i, :, part] = (dot(r.tok[...], weight(cc, i)) + shift[:, part]).astype(BF16)

    loop(8, project, 5)

    def attend(k):
        tick(k)
        s = k - 8
        rows = pl.ds(pl.multiple_of(s * 128, 128), 128)
        for p in range(6):
            part = slice(128 * p, 128 * (p + 1))
            w = softmax(dot_bt(two_heads(r.qkvv[0, rows, part]), r.qkvv[1, rows, part]) * 0.125).astype(BF16)
            r.aw[s, p] = w
            r.mix[rows, part] = side_by_side(dot(w, r.qkvv[2, rows, part])).astype(BF16)

    loop(11, attend, 8)
    tick(11)
    ring.arrived(3)
    for cc in range(2):
        part = slice(cc * W, (cc + 1) * W)
        r.n1[:, part] = dot(r.mix[...], weight(cc, 3)) + (r.tok[:, part].astype(F32) + r.lb[2:3, part])
    ring.last(9)

    row8 = lax.broadcasted_iota(jnp.int32, (8, D), 0)
    r.sloc[...] = jnp.zeros((8, D), F32)

    def heads(ref):
        out = jnp.zeros((8, D), F32)
        for s in range(3):
            top = ref[128 * s : 128 * s + 16, :].astype(F32)[0:1, :]
            out = jnp.where(row8 == s, top, out)
        return out

    def head_norm(i, value):
        n, rstd = norm(value)
        r.hn[i] = n
        r.hrst[i] = jnp.broadcast_to(rstd, (8, 128))
        return n

    hf = head_norm(0, heads(r.n1)) * r.lb[6:7, :] + r.lb[3:4, :]
    r.hf[...] = jnp.where(row8 < 3, hf, 0.0).astype(BF16)

    def head_up(i):
        ring.arrived(i)
        for cc in range(2):
            part = col(2 * (i - 4) + cc)
            g, gp = gelu_both(dot(r.hf[...], weight(cc, i)) + r.lub[0:1, part])
            keep = lax.broadcasted_iota(jnp.int32, (8, W), 0) < 3
            r.hg[:, part] = jnp.where(keep, g, 0.0).astype(BF16)
            r.hgp[:, part] = gp

        @pl.when(i < 6)
        def _():
            ring.last(i + 6)

    loop(8, head_up, 4)

    def down_rows(x, kc):
        pieces = [r.ws[cc, 8 + 2 * kc + j, x, y] for y in range(4) for cc in range(2) for j in range(2)]
        return jnp.concatenate(pieces, axis=0)

    halves = []
    for kc in range(2):
        for j in range(2):
            ring.arrived(8 + 2 * kc + j)
        part = slice(kc * W, (kc + 1) * W)
        acc = r.hf[:, part].astype(F32) + r.lb[4:5, part]
        for x in range(4):
            acc += dot(r.hg[:, D * x : D * (x + 1)], down_rows(x, kc))
        halves.append(acc)
    z0 = head_norm(1, jnp.concatenate(halves, axis=1)) * r.lb[7:8, :] + r.lb[5:6, :]
    cross.reshard_end()
    cross.start(z0, heads(r.cot))

    def blocks(fn):
        loop(ROWS // 64, lambda i: fn(pl.ds(pl.multiple_of(i * 64, 64), 64)))

    def norm_one(rows):
        n, rstd = norm(r.n1[rows, :])
        r.n1[rows, :] = n
        r.rst[rows, :] = jnp.broadcast_to(rstd, (64, 128))
        r.f[rows, :] = (n * r.lb[6:7, :] + r.lb[3:4, :]).astype(BF16)

    def raise_up(i):
        def half(cc):
            part = col(2 * (i - 4) + cc)
            g, gp = gelu_both(dot(r.f[...], weight(cc, i)) + r.lub[0:1, part])
            r.g[:, part] = g.astype(BF16)
            r.gpl[:, part] = gp.astype(BF16)

        loop(2, half)

    def lower(kc):
        part = slice(kc * W, (kc + 1) * W)
        r.n2[:, part] = r.f[:, part].astype(F32) + r.lb[4:5, part]

        def quarter(x):
            r.n2[:, part] += dot(r.g[:, col(x, D)], down_rows(x, kc))

        loop(4, quarter)

    row64 = lax.broadcasted_iota(jnp.int32, (64, D), 0)

    def norm_two(i):
        rows = pl.ds(pl.multiple_of(i * 64, 64), 64)
        n, rstd = norm(r.n2[rows, :])
        r.lo[rows, :] = (n * r.lb[7:8, :] + r.lb[5:6, :]).astype(BF16)
        dy = jnp.where((row64 == 0) & (i % 2 == 0), 0.0, r.cot[rows, :].astype(F32))
        dr2 = norm_back(dy, n, rstd, r.lb[7:8, :])
        dd = dr2.astype(BF16)
        r.n2[rows, :] = dr2
        r.dd[rows, :] = dd
        r.sloc[5:6, :] += sum0(dy)
        r.sloc[7:8, :] += sum0(dy * n)
        r.sloc[4:5, :] += sum0(dd.astype(F32))

    def down_grad(b):
        v = dot_at(r.g[:, col(b)], r.dd[...]).astype(BF16).reshape(2, 2, 2, 48, D)
        for chip in range(2):
            for cc in range(2):
                for j in range(4):
                    v4 = v[chip, cc, j % 2, :, (j // 2) * W : (j // 2 + 1) * W]
                    r.gb[(cc + c) % 2, j, b // 2, 2 * (b % 2) + chip] = v4

    def down_block(b, kc):
        chips = [(b // 2, 2 * (b % 2) + chip) for chip in range(2)]
        pieces = [r.ws[cc, 8 + 2 * kc + j, x, y] for x, y in chips for cc in range(2) for j in range(2)]
        return jnp.concatenate(pieces, axis=0)

    def middle(b):
        part = col(b)
        dg = dot_bt(r.dd[:, 0:W], down_block(b, 0)) + dot_bt(r.dd[:, W:D], down_block(b, 1))
        du = (dg * r.gpl[:, part].astype(F32)).astype(BF16)
        r.dcl[:, part] = sum0(du.astype(F32))
        r.n2[...] += dot_bt(du, r.ws[b % 2, 4 + b // 2].reshape(D, W))
        r.gb[(b + c) % 2, 4 + b // 2] = dot_at(r.f[...], du).astype(BF16).reshape(4, 4, 48, W)

        @pl.when(b % 2 == 1)
        def _():
            red.to_sibling(4 + b // 2)

    def norm_one_back(rows):
        df, n = r.n2[rows, :], r.n1[rows, :]
        dr1 = norm_back(df, n, r.rst[rows, 0:1], r.lb[6:7, :])
        de = dr1.astype(BF16)
        r.n2[rows, :] = dr1
        r.de[rows, :] = de
        r.sloc[3:4, :] += sum0(df)
        r.sloc[6:7, :] += sum0(df * n)
        r.sloc[2:3, :] += sum0(de.astype(F32))

    def out_back(de):
        return dot_bt(de[:, 0:W], weight(0, 3)) + dot_bt(de[:, W:D], weight(1, 3))

    def tick(t):
        red.tick(t, 8)

    blocks(norm_one)
    raise_up(4)
    cross.attention()
    loop(8, raise_up, 5)
    cross.first_norm()
    def pack(value):
        n = value.shape[1] // 2
        row = lax.broadcasted_iota(jnp.int32, (8, n), 0)
        both = jnp.where(row < 3, value[:, :n], pltpu.roll(value[:, n:], 3, 0))
        return jnp.where(row < 6, both, 0.0)

    r.hgs[...] = jnp.zeros((32, 8, 128), BF16)
    hidden, slope = r.hg[...].astype(F32), r.hgp[...]
    for t in range(32):
        part = slice(96 * t, 96 * t + 96)
        both = jnp.concatenate([hidden[:, part], slope[:, part]], axis=1)
        r.hgs[t, :, 0:96] = pack(both).astype(BF16)
    r.hfp[...] = pack(r.hf[...].astype(F32)).astype(BF16)
    loop(32, lambda t: send_to(me, t, r.hgs.at[t], r.hgr.at[me], r.hs.at[0], r.hr.at[0]))
    loop(32, lambda t: send_to(me, t, r.hfp, r.hfa.at[me], r.hs.at[1], r.hr.at[1]))
    lower(0)
    lower(1)
    cross.mlp()
    loop(6, norm_two)
    loop(4, down_grad)
    cross.second_norm()
    loop(8, down_grad, 4)
    loop(4, red.to_sibling)
    middle(0)
    tick(0)
    cross.mlp_back()
    middle(1)
    tick(1)
    middle(2)
    tick(2)
    middle(3)
    tick(3)
    cross.first_norm_back()
    middle(4)
    tick(4)
    middle(5)
    middle(6)
    tick(5)
    middle(7)
    cross.attention_back()
    tick(6)
    blocks(norm_one_back)
    r.do[...] = out_back(r.de[...]).astype(BF16)
    tick(7)
    cross.grads()
    cross.scatter()
    tick(8)
    r.dx[...] = jnp.where(row8 < 3, cross.finish(), 0.0)

    dy0, hn2 = r.dx[...], r.hn[1]
    dr2 = norm_back(dy0, hn2, r.hrst[1, :, 0:1], r.lb[7:8, :])
    r.hdd[...] = dr2.astype(BF16)
    r.hdf[...] = dr2
    r.hdp[...] = pack(dr2).astype(BF16)
    loop(32, lambda t: send_to(me, t, r.hdp, r.hda.at[me], r.hs.at[2], r.hr.at[2]))
    r.sloc[5:6, :] += sum0(dy0)
    r.sloc[7:8, :] += sum0(dy0 * hn2)
    r.sloc[4:5, :] += sum0(r.hdd[...].astype(F32))

    def head_middle(i):
        for cc in range(2):
            b = 2 * i + cc
            part = col(b)
            dg = dot_bt(r.hdd[:, 0:W], down_block(b, 0)) + dot_bt(r.hdd[:, W:D], down_block(b, 1))
            du = (dg * r.hgp[:, part]).astype(BF16)
            r.dcl[:, part] += sum0(du.astype(F32))
            r.hdf[...] += dot_bt(du, weight(cc, 4 + i))

    head_middle(0)
    head_middle(1)
    tick(9)
    head_middle(2)
    head_middle(3)
    ring.drain()
    for t in (ring.other, ring.seg(True, 1), ring.seg(True, 3), ring.seg(False, 1), ring.seg(False, 3)):
        pl.semaphore_signal(r.free, inc=1, device_id={"seg": t}, device_id_type=MESH)
    df, hn1 = r.hdf[...], r.hn[0]
    dr1 = norm_back(df, hn1, r.hrst[0, :, 0:1], r.lb[6:7, :])
    de = dr1.astype(BF16)
    r.sloc[3:4, :] += sum0(df)
    r.sloc[6:7, :] += sum0(df * hn1)
    r.sloc[2:3, :] += sum0(de.astype(F32))
    do = out_back(de)
    y = cross.output_rows()
    row16 = lax.broadcasted_iota(jnp.int32, (16, D), 0)

    def put(ref, s, value):
        rows = slice(128 * s, 128 * s + 16)
        ref[rows, :] = jnp.where(row16 == 0, value[s : s + 1, :], ref[rows, :].astype(F32)).astype(ref.dtype)

    for s in range(3):
        put(r.lo, s, y)
        put(r.n2, s, dr1)
        put(r.de, s, de.astype(F32))
        put(r.do, s, do)
    pltpu.make_async_copy(r.lo, r.lo_h, r.done.at[0]).start()

    def attend_back(s):
        rows = pl.ds(pl.multiple_of(s * 128, 128), 128)
        for p in range(6):
            part = slice(128 * p, 128 * (p + 1))
            q, k, v = r.qkvv[0, rows, part], r.qkvv[1, rows, part], r.qkvv[2, rows, part]
            do = two_heads(r.do[rows, part])
            w = r.aw[s, p]
            ds = softmax_back(w.astype(F32), dot_bt(do, v)).astype(BF16)
            r.qkvv[0, rows, part] = (side_by_side(dot(ds, k)) * 0.125).astype(BF16)
            r.qkvv[1, rows, part] = (dot_at(ds, two_heads(q)) * 0.125).astype(BF16)
            r.qkvv[2, rows, part] = dot_at(w, do).astype(BF16)

    attend_back(0)
    attend_back(1)
    cross.planes(red)
    attend_back(2)
    tick(10)

    def qkv_grad(i):
        for cc in range(2):
            part = slice(cc * W, (cc + 1) * W)
            again.gb[(cc + c) % 2, i + 1] = dot_at(r.tok[...], r.qkvv[i, :, part]).astype(BF16).reshape(4, 4, 48, W)

    pl.semaphore_wait(r.free, 5)

    def qkv_out(i):
        qkv_grad(i)
        red2.to_sibling(i + 1)

    loop(3, qkv_out)
    tick(11)
    for cc in range(2):
        again.gb[(cc + c) % 2, 0] = dot_at(r.mix[...], r.de[:, cc * W : (cc + 1) * W]).astype(BF16).reshape(4, 4, 48, W)
    red2.to_sibling(0)

    def second_round(step):
        loop(4, step, 1)
        step(0)

    sf = r.sf
    sf[...] = jnp.zeros((96, D), F32)
    sf[0:8, :] = r.sloc[...]
    sf[0:1, :] = sum0(r.qkvv[0].astype(F32))
    sf[1:2, :] = sum0(r.qkvv[2].astype(F32))
    sf[8:16, :] = r.small[...]
    for i in range(4):
        sf[16 + i : 17 + i, :] = r.dcl[:, D * i : D * (i + 1)]
    own = jnp.concatenate([r.dc[0:1, :], jnp.zeros((1, D - 128), F32)], axis=1)
    own = pltpu.roll(own, 96 * (me % 8), 1)
    sf[pl.ds(20 + me // 8, 1), :] = own
    line = lax.broadcasted_iota(jnp.int32, (64, D), 0)
    for s in range(3):
        _, place = slot_layout(r.doc, (64, D), jnp.full((64, D), me * 3 + s, jnp.int32))
        sf[24:88, :] += jnp.where(line == place, r.dx[s : s + 1, :], 0.0)
    r.s0[...] = sf[...].reshape(12, 8, D).astype(BF16)
    xs, xr = r.xs, r.xr
    loop(12, lambda k: send_to(me, owner_seg(k), r.s0.at[k], r.sg.at[me], xs.at[0], xr.at[0]))

    tick(12)
    second_round(red2.step_a)
    take(r.hgr, r.hr.at[0])
    take(r.hfa, r.hr.at[1])
    take(r.hda, r.hr.at[2])
    dda, hfa, both = flat8(r.hda[...]).astype(BF16), flat8(r.hfa[...]).astype(BF16), flat8(r.hgr[...])
    line = lax.broadcasted_iota(jnp.int32, (256, 128), 0) % 8

    def low(v):
        return jnp.where(line[:, : v.shape[1]] < 3, v, 0.0)

    left, right = dot_bt(dda, r.down[:, 0:W]), dot_bt(dda, r.down[:, W:D])
    du = low((left + pltpu.roll(right, 253, 0)) * pltpu.roll(both, 253, 0)[:, 0:96])
    share_up = [dot_at(hfa, v.astype(BF16)) for v in (du, pltpu.roll(du, 3, 0))]
    r.pcu[:, :, 0:96] = jnp.concatenate(share_up, axis=0).reshape(32, 24, 96).astype(BF16)
    core = (me // 4) % 2

    def share(t):
        send_to(me, t - t % 2 + core, r.pcu.at[t], r.cu.at[t % 2, (me // 8) * 4 + me % 4], r.ks.at[3], r.kr.at[3])

    loop(32, share)
    tick(13)
    hidden = low(both)
    down_share = [dot_at(v.astype(BF16), dda)[0:96] for v in (hidden, pltpu.roll(hidden, 3, 0))]
    for n in range(8):
        j, h = n // 2, n % 2
        top = (j % 2) * 48 + 24 * h
        piece = down_share[j // 2][top : top + 24]
        r.zp[0, n] = (r.zp[0, n].astype(F32) + piece).astype(BF16)
    red.z_send(0)
    tick(14)
    cross.planes_sum(red)
    second_round(red2.step_b)
    tick(15)

    @pl.when(is_owner)
    def _():
        take(r.sg, xr.at[0])
        r.sm1[...] = jnp.sum(r.sg[...].astype(F32), axis=0).astype(BF16)
        red.peers(lambda zz: zcopy(r.sm1, r.sz.at[z], xs.at[3], xr.at[3], zz, me).start())
        pltpu.make_async_copy(r.sm1, r.sz.at[z], xr.at[3]).start()

    tick(16)
    tick(17)
    second_round(red2.step_c)

    take(r.cu, r.kr.at[3])
    for n in range(8):
        m, h = n // 2, n % 2
        for q in range(4):
            r.zc[:, 96 * q : 96 * q + 96] = r.cu[h, 4 * m + q].astype(F32)[:, 0:96]
        r.zp[1, n] = (r.zp[1, n].astype(F32) + r.zc[...]).astype(BF16)
    red.z_send(1)
    red.z_sum(0)
    second_round(red2.step_d)

    def token_grad(i):
        acc = dot_bt(r.qkvv[i, :, 0:W], weight(0, i))
        r.tg[...] += acc + dot_bt(r.qkvv[i, :, W : 2 * W], weight(1, i))

    token_grad(0)
    second_round(red2.step_e)
    red.z_send(2)
    token_grad(1)

    @pl.when(is_owner)
    def _():
        take(r.sz.at[pl.ds(0, 8)], xr.at[3])
        r.sm2[...] = jnp.sum(r.sz[0:8].astype(F32), axis=0).astype(BF16)
        loop(32, lambda t: send_to(me, t, r.sm2, r.osm.at[me // 2], xs.at[6], xr.at[6]))

    red.z_sum(1)
    token_grad(2)
    pltpu.make_async_copy(r.tg, r.tg_h, r.done.at[1]).start()
    red.z_sum(2)
    for g, ref in ((0, r.fd), (1, r.fa.at[pl.ds(8, 8)]), (2, r.fa.at[pl.ds(0, 8)])):
        take(ref, r.zsr.at[g, 1])
    take(r.osm, xr.at[6])

    take(r.lo, r.done.at[0])
    take(r.tg, r.done.at[1])

    cross.end()
    cross.drain()
    red2.sent(4)
    red.sent(8)
    red.z_sent()
    for i, (src, dst) in enumerate(swaps):
        take(src, r.sib_s.at[i])
    take(r.smg.at[pl.ds(0, 31)], r.sm_s)
    take(r.hgr.at[pl.ds(0, 31)], r.hs.at[0])
    take(r.hfa.at[pl.ds(0, 31)], r.hs.at[1])
    take(r.hda.at[pl.ds(0, 31)], r.hs.at[2])

    @pl.when(core == c)
    def _():
        take(r.pcu.at[pl.ds(0, 30)], r.ks.at[3])

    @pl.when(core != c)
    def _():
        take(r.pcu, r.ks.at[3])

    @pl.when(is_owner)
    def _():
        take(r.sg.at[pl.ds(0, 11)], xs.at[0])
        take(r.sz.at[pl.ds(0, 7)], xs.at[3])
        take(r.sz.at[pl.ds(0, 31)], xs.at[6])

    @pl.when(jnp.logical_not(is_owner))
    def _():
        take(r.sg.at[pl.ds(0, 12)], xs.at[0])


FORMAT_OUT = dict(
    lo_o=((ROWS, D), BF16),
    tg_o=((ROWS, D), F32),
    oq=((24, 3 * D), F32),
    oo=((24, D), F32),
    ou=((24, FF), F32),
    od=((96, D), F32),
    ob=((6, 24), F32),
    ouv=((1, 96), F32),
    og=((2, 24), F32),
    xoq=((24, 3 * D), F32),
    xoo=((24, D), F32),
    xou=((24, FF), F32),
    xod=((96, D), F32),
    xob=((6, 24), F32),
    xouv=((1, 96), F32),
    xog=((2, 24), F32),
    opos=((2, D), F32),
)


def format_kernel(*refs):
    r = fields(list(F_OUT) + list(FORMAT_OUT), refs)
    me = lax.axis_index("seg")
    r.lo_o[...] = r.lo_h[...]
    r.tg_o[...] = r.tg_h[...]
    for p in range(6):
        for j in range(3):
            r.xoq[:, D * j + 128 * p : D * j + 128 * (p + 1)] = r.cf[p // 2, p % 2, :, 128 * j : 128 * (j + 1)].astype(F32)
    for i in range(2):
        r.xoo[:, W * i : W * (i + 1)] = r.cf[3, i].astype(F32)
        for n in range(4):
            m = 8 + 4 * i + n
            r.xod[24 * n : 24 * (n + 1), W * i : W * (i + 1)] = r.cf[m // 2, m % 2].astype(F32)
    for t in range(32):
        r.xou[:, 96 * t : 96 * t + 96] = r.uf[t // 4, t % 4].astype(F32)[:, 0:96]
    for n in range(8):
        j, h = n // 2, n % 2
        top = (j % 2) * 48 + 24 * h
        r.od[top : top + 24, (j // 2) * W : (j // 2 + 1) * W] = r.fd[n].astype(F32)
    for u in range(8, 16):
        r.ou[:, W * (u - 8) : W * (u - 7)] = r.fa[u].astype(F32)
    ours = pltpu.roll(r.osm[0:2].astype(F32).reshape(16, D), (D - 24 * me) % D, 1)
    r.ob[...] = ours[0:6, 0:24]
    r.og[...] = ours[6:8, 0:24]
    r.xob[...] = ours[8:14, 0:24]
    r.xog[...] = ours[14:16, 0:24]
    ups = pltpu.roll(r.osm[2].astype(F32), (D - 96 * (me % 8)) % D, 1)
    line = lax.broadcasted_iota(jnp.int32, (8, D), 0)
    r.ouv[...] = sum0(jnp.where(line == me // 8, ups, 0.0))[:, 0:96]
    r.xouv[...] = sum0(jnp.where(line == 4 + me // 8, ups, 0.0))[:, 0:96]
    r.opos[...] = pltpu.roll(r.osm[3 + me // 4].astype(F32), (8 - 2 * (me % 4)) % 8, 0)[0:2]
    for u in range(8):
        if u < 6:
            r.oq[:, W * u : W * (u + 1)] = r.fa[u].astype(F32)
        else:
            r.oo[:, W * (u - 6) : W * (u - 5)] = r.fa[u].astype(F32)


def call(kernel, name, ins, outs, scratch, cid, args):
    vm, smem = pl.BlockSpec(memory_space=pltpu.VMEM), pl.BlockSpec(memory_space=pltpu.SMEM)
    hbm = pl.BlockSpec(memory_space=pl.ANY)
    return pl.pallas_call(
        kernel,
        out_shape=tuple(jax.ShapeDtypeStruct(s, t) for s, t in outs.values()),
        in_specs=[smem if n == "doc" else vm for n in ins],
        out_specs=tuple(hbm if n in ("lo_h", "tg_h") else vm for n in outs),
        scratch_shapes=list(scratch.values()),
        compiler_params=pltpu.CompilerParams(
            collective_id=cid, has_side_effects=cid is not None, vmem_limit_bytes=63 << 20
        ),
        name=name,
    )(*args)


def shards(tokens, doc, qkv, out, up, down, bias, upbias, gains, cqkv, cout, cup, cdown, cbias, cupbias, cgains, pos, cot):
    made = call(
        layer_kernel, "layer", F_IN, F_OUT, F_SCR, 0,
        (tokens, cot, qkv, out, up, down, bias, upbias.reshape(1, 96), gains, cqkv, cout, cup, cdown, cbias,
         cupbias.reshape(1, 96), cgains, pos, doc),
    )
    out = dict(zip(FORMAT_OUT, call(format_kernel, "format", list(F_OUT), FORMAT_OUT, {}, None, made)))
    out["ouv"], out["xouv"] = out["ouv"].reshape(96), out["xouv"].reshape(96)
    return tuple(out.values())


def solution(mesh):
    both, seg, cols, flat = P(("grp", "seg"), None), P("seg", None), P(None, "seg"), P("seg")
    weights = (seg, seg, seg, seg, cols, flat, cols)
    in_specs = (both, P("grp", None)) + weights + weights + (seg, both)
    out_specs = (both, both) + weights + weights + (seg,)
    return jax.shard_map(shards, mesh=mesh, in_specs=in_specs, out_specs=out_specs, check_vma=False)
```

```python
import functools
import math
import types

import jax
import jax.numpy as jnp
from jax import lax
from jax.experimental import pallas as pl
from jax.experimental.pallas import tpu as pltpu
from jax.sharding import PartitionSpec as P

D = 768
FF = 3072
ROWS = 384
SEG_LEN = 128
W = 384
F32, BF16 = jnp.float32, jnp.bfloat16
MESH = pl.DeviceIdType.MESH
DMA = pltpu.SemaphoreType.DMA
RSQ2 = 1.0 / math.sqrt(2.0)
RS2PI = 1.0 / math.sqrt(2.0 * math.pi)
VM = pltpu.VMEM


def dot(a, b):
    return lax.dot_general(a, b, (((1,), (0,)), ((), ())), preferred_element_type=F32)


def dot_bt(a, b):
    return lax.dot_general(a, b, (((1,), (1,)), ((), ())), preferred_element_type=F32)


def dot_at(a, b):
    return lax.dot_general(a, b, (((0,), (0,)), ((), ())), preferred_element_type=F32)


def rcopy(src, dst, ssem, rsem, seg):
    return pltpu.make_async_remote_copy(
        src_ref=src, dst_ref=dst, send_sem=ssem, recv_sem=rsem, device_id={"seg": seg}, device_id_type=MESH
    )


def zcopy(src, dst, ssem, rsem, z, seg):
    return pltpu.make_async_remote_copy(
        src_ref=src, dst_ref=dst, send_sem=ssem, recv_sem=rsem, device_id={"grp": z, "seg": seg}, device_id_type=MESH
    )


def take(ref, sem):
    pltpu.make_async_copy(ref, ref, sem).wait()


def send_to(me, target, src, dst, ssem, rsem):
    @pl.when(target != me)
    def _():
        rcopy(src, dst, ssem, rsem, target).start()

    @pl.when(target == me)
    def _():
        pltpu.make_async_copy(src, dst, rsem).start()


def loop(n, fn, first=0):
    def body(i, _):
        fn(i)
        return 0

    lax.fori_loop(first, n, body, 0)


def col(u, width=W):
    return pl.ds(pl.multiple_of(u * width, 128), width)


def norm(v):
    center = v - jnp.mean(v, axis=-1, keepdims=True)
    rstd = lax.rsqrt(jnp.mean(center * center, axis=-1, keepdims=True) + 1e-05)
    return center * rstd, rstd


def norm_back(grad, n, rstd, gain):
    dn = grad * gain
    return rstd * (dn - jnp.mean(dn, axis=-1, keepdims=True) - n * jnp.mean(dn * n, axis=-1, keepdims=True))


def gelu_both(u):
    e = jnp.exp(-0.5 * u * u)
    t = 1.0 / (1.0 + (0.3275911 * RSQ2) * jnp.abs(u))
    poly = t * (0.127414796 + t * (-0.142248368 + t * (0.7107068705 + t * (-0.7265760135 + t * 0.5307027145))))
    tail = poly * e
    cdf = jnp.where(u < 0.0, tail, 1.0 - tail)
    return u * cdf, cdf + u * (RS2PI * e)


def two_heads(v):
    lane = lax.broadcasted_iota(jnp.int32, v.shape, 1)
    none = jnp.zeros_like(v)
    return jnp.concatenate([jnp.where(lane < 64, v, none), jnp.where(lane >= 64, v, none)], axis=0)


def side_by_side(v):
    n = v.shape[0] // 2
    lane = lax.broadcasted_iota(jnp.int32, (n, 128), 1)
    return jnp.where(lane < 64, v[:n], v[n:])


def softmax(s):
    e = jnp.exp(s - jnp.max(s, axis=-1, keepdims=True))
    return e / jnp.sum(e, axis=-1, keepdims=True)


def softmax_back(w, dw):
    return w * (dw - jnp.sum(w * dw, axis=-1, keepdims=True))


def rows8(value):
    return value.reshape(value.shape[0] // 8, 8, value.shape[1])


def flat8(value):
    v = value.astype(F32)
    return v.reshape(v.shape[0] * v.shape[1], v.shape[2])


def sum0(v):
    return jnp.sum(v, axis=0, keepdims=True)


def owner_seg(k):
    return 2 * k


def pair_seg(p):
    return 4 * p + 1


def pair_first(p):
    return 5 * (p % 3) + 16 * (p // 3)


def fields(spec, refs):
    return types.SimpleNamespace(**dict(zip(spec, refs)))


CROSS = dict(
    pup=VM((32, 24, 128), BF16),
    xup=VM((32, 24, 128), BF16),
    xqkv=VM((32, 3, 24, 128), BF16),
    xout=VM((6, 24, D), BF16),
    wup=VM((D, 128), BF16),
    wqkv=VM((D, 384), BF16),
    wout=VM((128, D), BF16),
    wout_f=VM((144, D), F32),
    wdn=VM((128, D), BF16),
    msg=VM((8, D), BF16),
    x1=VM((32, 8, D), BF16),
    own=VM((8, 8, D), F32),
    rst=VM((8, 128), F32),
    xall=VM((96, D), BF16),
    q=VM((3, 96, 128), BF16),
    o=VM((96, 128), BF16),
    af=VM((192, 96), F32),
    p2=VM((12, 8, D), BF16),
    g2=VM((6, 8, D), BF16),
    p3=VM((8, D), BF16),
    g3=VM((12, 8, D), BF16),
    p4=VM((12, 8, D), BF16),
    g46=VM((64, 8, D), BF16),
    p5=VM((2, 8, D), BF16),
    g5=VM((12, 8, D), BF16),
    g5y=VM((2, 8, D), BF16),
    y_r=DMA,
    p6=VM((12, 8, D), BF16),
    p7=VM((8, D), BF16),
    g7=VM((12, 8, D), BF16),
    p7f=VM((8, D), F32),
    g7f=VM((2, 8, D), F32),
    p8=VM((32, 8, W), BF16),
    g8=VM((6, 8, W), BF16),
    gp=VM((96, 128), F32),
    gact=VM((96, 128), BF16),
    fall=VM((96, D), BF16),
    dd=VM((96, D), BF16),
    du=VM((96, 128), BF16),
    dq=VM((96, 384), BF16),
    de=VM((96, D), BF16),
    cs=DMA((12,)),
    cr=DMA((12,)),
    c7=DMA,
)


def slot_layout(doc, shape, slots):
    pos = (slots % 3) * 32 + slots // 3
    number = jnp.zeros(shape, jnp.int32)
    begin = jnp.zeros(shape, jnp.int32)
    end = jnp.int32(0)
    for d in range(6):
        begin = jnp.where(pos >= end, end, begin)
        number = jnp.where(pos >= end, d, number)
        end = end + doc[0, d]
    return number, pos - begin


class Cross:
    def __init__(self, r, a):
        self.r, self.a = r, a
        self.me = lax.axis_index("seg")
        self.is_owner = (self.me % 2 == 0) & (self.me < 24)
        self.k = self.me // 2
        self.is_pair = (self.me % 4 == 1) & (self.me < 24)
        self.p = self.me // 4

    def sem(self, e):
        return self.r.xcs.at[e], self.r.xcr.at[e]

    def seams(self):
        m = self.me % 16
        seam = (m == 5) | (m == 10)
        p0 = 3 * (self.me // 16) + jnp.where(m > 10, 2, jnp.where(m > 5, 1, 0))
        return seam, p0

    def reshard(self):
        r, a, me = self.r, self.a, self.me
        s0, r0 = self.sem(0)
        s1, r1 = self.sem(1)
        s2, r2 = self.sem(2)
        r.pup[...] = jnp.zeros((32, 24, 128), BF16)
        up = a.cup[...].astype(F32)
        for t in range(32):
            r.pup[t, :, 0:96] = up[:, 96 * t : 96 * t + 96].astype(BF16)
        loop(32, lambda t: send_to(me, t, r.pup.at[t], r.xup.at[me], s0, r0))

        def to_pair(p):
            for j in range(3):
                part = pl.ds(pl.multiple_of(D * j + 128 * p, 128), 128)
                send_to(me, pair_seg(p), a.cqkv.at[:, part], r.xqkv.at[me, j], s1, r1)
            first = pair_first(p)

            @pl.when((me >= first) & (me < first + 6))
            def _():
                send_to(me, pair_seg(p), a.cout, r.xout.at[me - first], s2, r2)

        loop(6, to_pair)
        r.wdn[0:96, :] = a.cdown[...]
        r.wdn[96:128, :] = jnp.zeros((32, D), BF16)

    def reshard_end(self):
        r = self.r
        take(r.xup, r.xcr.at[0])
        self.reshard_sent()
        r.wup[...] = r.xup[...].astype(F32).reshape(D, 128).astype(BF16)

        @pl.when(self.is_pair)
        def _():
            take(r.xqkv, r.xcr.at[1])
            for j in range(3):
                r.wqkv[:, 128 * j : 128 * (j + 1)] = r.xqkv[:, j].astype(F32).reshape(D, 128).astype(BF16)
            take(r.xout, r.xcr.at[2])
            r.wout_f[...] = r.xout[...].astype(F32).reshape(144, D)
            off = pl.multiple_of(8 * (self.p % 3), 8)
            r.wout[...] = r.wout_f[pl.ds(off, 128), :].astype(BF16)

    def reshard_sent(self):
        r, me = self.r, self.me
        take(r.xup.at[pl.ds(0, 31)], r.xcs.at[0])

        @pl.when(self.is_pair)
        def _():
            take(r.xqkv.at[pl.ds(0, 5)], r.xcs.at[1])

        @pl.when(jnp.logical_not(self.is_pair))
        def _():
            take(r.xqkv.at[pl.ds(0, 6)], r.xcs.at[1])

        seam, p0 = self.seams()
        hits = jnp.where(me == pair_seg(p0), 1, 0) + jnp.where(seam & (me == pair_seg(p0 + 1)), 1, 0)
        count = jnp.where(seam, 2, 1) - hits
        for n in (1, 2):

            @pl.when(count == n)
            def _():
                take(r.xout.at[pl.ds(0, n)], r.xcs.at[2])

    def start(self, z0, dy0):
        r, a, me = self.r, self.a, self.me
        row = lax.broadcasted_iota(jnp.int32, (8, 512), 0)
        lane = lax.broadcasted_iota(jnp.int32, (8, 512), 1)
        _, place = slot_layout(a.doc, (8, 512), jnp.minimum(me * 3 + row, 95))
        table = a.smg[...].astype(F32).reshape(512, 256)[:, 128:256].astype(BF16)
        parts = []
        for i in range(6):
            hot = (lane == (place // 2) * 16 + (place % 2) * 6 + i) & (row < 3)
            parts.append(dot(hot.astype(BF16), table))
        cross_in = z0 + jnp.concatenate(parts, axis=1)
        rowd = lax.broadcasted_iota(jnp.int32, (8, D), 0)
        both = jnp.where(rowd < 3, cross_in, pltpu.roll(dy0, 3, 0))
        r.msg[...] = jnp.where(rowd < 6, both, 0.0).astype(BF16)
        ss, rs = self.sem(3)
        loop(6, lambda p: send_to(me, pair_seg(p), r.msg, r.x1.at[me], ss, rs))
        loop(12, lambda k: send_to(me, owner_seg(k), r.msg, r.x1.at[me], ss, rs))

    def pick(self, n, first, base):
        row = lax.broadcasted_iota(jnp.int32, (n, 256), 0) + first
        lane = lax.broadcasted_iota(jnp.int32, (n, 256), 1)
        return (lane == (row // 3) * 8 + row % 3 + base).astype(BF16)

    def attention(self):
        r, a, me = self.r, self.a, self.me
        ss, rs = self.sem(4)

        @pl.when(self.is_pair)
        def _():
            take(r.x1, r.xcr.at[3])
            msgs = flat8(r.x1[...]).astype(BF16)
            xall = dot(self.pick(96, 0, 0), msgs).astype(BF16)
            r.xall[...] = xall
            part = col(self.p, 128)
            joined = dot(xall, r.wqkv[...])
            q = (joined[:, 0:128] + a.cb[0:1, part]).astype(BF16)
            k = joined[:, 128:256].astype(BF16)
            v = (joined[:, 256:384] + a.cb[1:2, part]).astype(BF16)
            r.q[0], r.q[1], r.q[2] = q, k, v
            line = lax.broadcasted_iota(jnp.int32, (192, 96), 0)
            doc_r, _ = slot_layout(a.doc, (192, 96), jnp.where(line < 96, line, line - 96))
            doc_c, _ = slot_layout(a.doc, (192, 96), lax.broadcasted_iota(jnp.int32, (192, 96), 1))
            w = softmax(jnp.where(doc_r == doc_c, dot_bt(two_heads(q), k) * 0.125, -1e30))
            r.af[...] = w
            o = side_by_side(dot(w.astype(BF16), v)).astype(BF16)
            r.o[...] = o
            r.p2[...] = rows8(dot(o, r.wout[...])).astype(BF16)
            loop(12, lambda k: send_to(me, owner_seg(k), r.p2.at[k], r.g2.at[self.p], ss, rs))

    def first_norm(self):
        r, a, me = self.r, self.a, self.me
        ss, rs = self.sem(5)

        @pl.when(self.is_owner)
        def _():
            take(r.x1, r.xcr.at[3])
            msgs = flat8(r.x1[...]).astype(BF16)
            x = dot(self.pick(8, 8 * self.k, 0), msgs)
            r.own[1] = dot(self.pick(8, 8 * self.k, 3), msgs)
            take(r.g2, r.xcr.at[4])
            total = jnp.sum(r.g2[...].astype(F32), axis=0)
            n, rstd = norm(x + (total + a.cb[2:3, :]))
            r.own[2] = n
            r.xrst[...] = jnp.broadcast_to(rstd, (8, 128))
            r.p3[...] = (n * a.cb[6:7, :] + a.cb[3:4, :]).astype(BF16)
            loop(32, lambda t: send_to(me, t, r.p3, r.g3.at[self.k], ss, rs))

    def mlp(self):
        r, a, me = self.r, self.a, self.me
        ss, rs = self.sem(6)
        take(r.g3, r.xcr.at[5])
        f = flat8(r.g3[...]).astype(BF16)
        r.fall[...] = f
        g, gp = gelu_both(dot(f, r.wup[...]) + a.cub[0:1, :])
        r.gp[...] = gp
        g = g.astype(BF16)
        r.gact[...] = g
        r.p4[...] = rows8(dot(g, r.wdn[...])).astype(BF16)
        loop(12, lambda k: send_to(me, owner_seg(k), r.p4.at[k], r.g46.at[me], ss, rs))

    def second_norm(self):
        r, a, me = self.r, self.a, self.me
        ss, rs = self.sem(7)

        @pl.when(self.is_owner)
        def _():
            take(r.g46.at[pl.ds(0, 32)], r.xcr.at[6])
            total = jnp.sum(r.g46[0:32].astype(F32), axis=0)
            n, rstd = norm(r.p3[...].astype(F32) + (total + a.cb[4:5, :]))
            y = n * a.cb[7:8, :] + a.cb[5:6, :]
            dr2 = norm_back(r.own[1], n, rstd, a.cb[7:8, :])
            r.own[3] = n
            r.own[4] = dr2
            r.p5[0] = dr2.astype(BF16)
            r.p5[1] = y.astype(BF16)
            loop(32, lambda t: send_to(me, t, r.p5.at[0], r.g5.at[self.k], ss, rs))
            self.to_slots(lambda t, i: send_to(me, t, r.p5.at[1], r.g5y.at[i], r.c7, r.y_r))

    def mlp_back(self):
        r, me = self.r, self.me
        ss, rs = self.sem(8)
        take(r.g5, r.xcr.at[7])
        dd = flat8(r.g5[...]).astype(BF16)
        r.xdd[...] = dd
        du = (dot_bt(dd, r.wdn[...]) * r.gp[...]).astype(BF16)
        r.du[...] = du
        r.p6[...] = rows8(dot_bt(du, r.wup[...])).astype(BF16)
        loop(12, lambda k: send_to(me, owner_seg(k), r.p6.at[k], r.g46.at[32 + me], ss, rs))

    def window(self, seg):
        return jnp.minimum((3 * seg) // 8, 10)

    def first_norm_back(self):
        r, a, me = self.r, self.a, self.me
        ss, rs = self.sem(9)
        fr = r.xcr.at[10]

        @pl.when(self.is_owner)
        def _():
            take(r.g46.at[pl.ds(32, 32)], r.xcr.at[8])
            df = jnp.sum(r.g46[32:64].astype(F32), axis=0) + r.own[4]
            r.own[5] = df
            dr1 = norm_back(df, r.own[2], r.xrst[:, 0:1], a.cb[6:7, :])
            r.p7[...] = dr1.astype(BF16)
            loop(6, lambda p: send_to(me, pair_seg(p), r.p7, r.g7.at[self.k], ss, rs))
            r.p7f[...] = dr1

            self.to_slots(lambda t, i: send_to(me, t, r.p7f, r.g7f.at[i], r.c7, fr))

    def to_slots(self, fn):
        def one(t):
            w = self.window(t)

            @pl.when((w == self.k) | (w + 1 == self.k))
            def _():
                fn(t, self.k - w)

        loop(32, one)

    def attention_back(self):
        r, me = self.r, self.me
        ss, rs = self.sem(11)

        @pl.when(self.is_pair)
        def _():
            take(r.g7, r.xcr.at[9])
            de = flat8(r.g7[...]).astype(BF16)
            r.xde[...] = de
            do = dot_bt(de, r.wout[...]).astype(BF16)
            q, k, v = r.q[0], r.q[1], r.q[2]
            do2, w = two_heads(do), r.af[...]
            ds = softmax_back(w, dot_bt(do2, v)).astype(BF16)
            r.dq[:, 0:128] = (side_by_side(dot(ds, k)) * 0.125).astype(BF16)
            r.dq[:, 128:256] = (dot_at(ds, two_heads(q)) * 0.125).astype(BF16)
            r.dq[:, 256:384] = dot_at(w.astype(BF16), do2).astype(BF16)
            dx = dot_bt(r.dq[...], r.wqkv[...]).astype(BF16)
            line = lax.broadcasted_iota(jnp.int32, (256, 96), 0)
            place = (line // 8) * 3 + line % 8 - lax.broadcasted_iota(jnp.int32, (256, 96), 1)
            left = ((line % 8 < 3) & (place == 0)).astype(BF16)
            right = ((line % 8 >= 3) & (line % 8 < 6) & (place == 3)).astype(BF16)
            r.p8[...] = rows8(dot(left, dx[:, 0:W]) + dot(right, dx[:, W:D])).astype(BF16)
            loop(32, lambda t: send_to(me, t, r.p8.at[t], r.g8.at[self.p], ss, rs))

    def finish(self):
        r = self.r
        take(r.g7f, r.xcr.at[10])
        take(r.g8, r.xcr.at[11])
        total = jnp.sum(r.g8[...].astype(F32), axis=0)
        shift = 3 * self.me - 8 * self.window(self.me)
        rest = pltpu.roll(r.g7f[...].reshape(16, D), 16 - shift, 0)[0:8]
        return rest + jnp.concatenate([total, pltpu.roll(total, 5, 0)], axis=1)

    def output_rows(self):
        take(self.r.g5y, self.r.y_r)
        y = self.r.g5y[...].astype(F32).reshape(16, D)
        return pltpu.roll(y, 16 - (3 * self.me - 8 * self.window(self.me)), 0)[0:8]

    def grads(self):
        r, a = self.r, self.a
        a.pu[...] = dot_at(r.fall[...], r.du[...]).reshape(32, 24, 128).astype(BF16)
        a.gdn[...] = dot_at(r.gact[...], r.xdd[...])[0:96].astype(BF16)

        @pl.when(self.is_pair)
        def _():
            for j in range(3):
                part = dot_at(r.xall[...], r.dq[:, 128 * j : 128 * (j + 1)])
                a.pq[:, j] = part.reshape(32, 24, 128).astype(BF16)
            r.po_f[...] = jnp.zeros((144, D), F32)
            off = pl.multiple_of(8 * (self.p % 3), 8)
            r.po_f[pl.ds(off, 128), :] = dot_at(r.o[...], r.xde[...])
            a.po[...] = r.po_f[...].reshape(6, 24, D).astype(BF16)

        a.small[...] = jnp.zeros((8, D), F32)

        @pl.when(self.is_owner)
        def _():
            dr1, df, dr2, dy = r.p7[...].astype(F32), r.own[5], r.own[4], r.own[1]
            dd = r.p5[0].astype(F32)
            for row, v in ((2, dr1), (3, df), (4, dd), (5, dy), (6, df * r.own[2]), (7, dy * r.own[3])):
                a.small[row : row + 1, :] = sum0(v)

        @pl.when(self.is_pair)
        def _():
            part = col(self.p, 128)
            a.small[0:1, part] = sum0(r.dq[:, 0:128].astype(F32))
            a.small[1:2, part] = sum0(r.dq[:, 256:384].astype(F32))

        a.dc[...] = jnp.broadcast_to(sum0(r.du[...].astype(F32)), (8, 128))

    def drain(self):
        r, me = self.r, self.me
        cs = r.xcs

        def some(e, ref, count, fewer):
            @pl.when(fewer)
            def _():
                take(ref.at[pl.ds(0, count - 1)], cs.at[e])

            @pl.when(jnp.logical_not(fewer))
            def _():
                take(ref.at[pl.ds(0, count)], cs.at[e])

        some(3, r.g46, 18, self.is_pair | self.is_owner)
        some(6, r.g46, 12, self.is_owner)
        some(8, r.g46, 12, self.is_owner)

        @pl.when(self.is_pair)
        def _():
            take(r.g46.at[pl.ds(0, 12)], cs.at[4])
            take(r.p8.at[pl.ds(0, 31)], cs.at[11])

        @pl.when(self.is_owner)
        def _():
            take(r.g46.at[pl.ds(0, 31)], cs.at[5])
            take(r.g46.at[pl.ds(0, 31)], cs.at[7])
            take(r.g46.at[pl.ds(0, 6)], cs.at[9])

            count = jnp.int32(0)
            for t in range(32):
                w = min(3 * t // 8, 10)
                count += jnp.where(((self.k == w) | (self.k == w + 1)) & (me != t), 1, 0)
            for n in range(1, 10):

                @pl.when(count == n)
                def _():
                    take(r.g46.at[pl.ds(0, 3 * n)], r.c7)


class CrossGrads(Cross):
    def scatter(self):
        r, a, me = self.r, self.a, self.me
        loop(32, lambda t: send_to(me, t, a.pu.at[t], r.gup.at[me], r.ks.at[0], r.kr.at[0]))

        @pl.when(self.is_pair)
        def _():
            loop(32, lambda t: send_to(me, t, a.pq.at[t], r.gqkv.at[self.p], r.ks.at[1], r.kr.at[1]))
            loop(
                6,
                lambda i: send_to(
                    me, pair_first(self.p) + i, a.po.at[i], r.go.at[self.p % 2], r.ks.at[2], r.kr.at[2]
                ),
            )

    def planes(self, red):
        r, a, me, z = self.r, self.a, self.me, red.z
        take(r.gup, r.kr.at[0])
        take(r.gqkv, r.kr.at[1])
        for i in range(6):
            for j in range(3):
                r.c0[i, :, 128 * j : 128 * (j + 1)] = r.gqkv[i, j]
        seam, p0 = self.seams()

        @pl.when(seam)
        def _():
            take(r.go, r.kr.at[2])
            both = (r.go[0].astype(F32) + r.go[1].astype(F32)).astype(BF16)
            for i in range(2):
                r.c0[6 + i] = both[:, W * i : W * (i + 1)]

        @pl.when(jnp.logical_not(seam))
        def _():
            take(r.go.at[0], r.kr.at[2])
            for i in range(2):
                r.c0[6 + i] = r.go[p0 % 2, :, W * i : W * (i + 1)]

        gdn = a.gdn[...].astype(F32).reshape(4, 24, D)
        for i in range(2):
            for n in range(4):
                r.c0[8 + 4 * i + n] = gdn[n, :, W * i : W * (i + 1)].astype(BF16)

        def out(zz):
            zcopy(r.c0.at[pl.ds(2 * zz, 2)], r.cr.at[z], r.xs.at[1], r.xr.at[1], zz, me).start()
            zcopy(r.gup.at[pl.ds(4 * zz, 4)], r.ur.at[z], r.xs.at[2], r.xr.at[2], zz, me).start()

        red.peers(out)
        pltpu.make_async_copy(r.c0.at[pl.ds(2 * z, 2)], r.cr.at[z], r.xr.at[1]).start()
        pltpu.make_async_copy(r.gup.at[pl.ds(4 * z, 4)], r.ur.at[z], r.xr.at[2]).start()

    def planes_sum(self, red):
        r, me, z = self.r, self.me, red.z
        take(r.cr, r.xr.at[1])
        r.cs[...] = jnp.sum(r.cr[...].astype(F32), axis=0).astype(BF16)
        take(r.ur, r.xr.at[2])
        r.us[...] = jnp.sum(r.ur[...].astype(F32), axis=0).astype(BF16)

        def back(zz):
            zcopy(r.cs, r.cf.at[z], r.xs.at[4], r.xr.at[4], zz, me).start()
            zcopy(r.us, r.uf.at[z], r.xs.at[5], r.xr.at[5], zz, me).start()

        red.peers(back)
        pltpu.make_async_copy(r.cs, r.cf.at[z], r.xr.at[4]).start()
        pltpu.make_async_copy(r.us, r.uf.at[z], r.xr.at[5]).start()

    def end(self):
        r, me = self.r, self.me
        take(r.cf, r.xr.at[4])
        take(r.uf, r.xr.at[5])
        take(r.gup.at[pl.ds(0, 31)], r.ks.at[0])

        @pl.when(self.is_pair)
        def _():
            take(r.pq.at[pl.ds(0, 31)], r.ks.at[1])
            first = pair_first(self.p)
            inside = (me >= first) & (me < first + 6)

            @pl.when(inside)
            def _():
                take(r.po.at[pl.ds(0, 5)], r.ks.at[2])

            @pl.when(jnp.logical_not(inside))
            def _():
                take(r.po, r.ks.at[2])

        for n, buf in ((1, r.cr), (2, r.ur), (4, r.cr), (5, r.ur)):
            take(buf.at[pl.ds(0, 7)], r.xs.at[n])


class Plane:
    def __init__(self):
        self.me = lax.axis_index("seg")
        self.x, self.y, self.c = self.me // 8, (self.me // 2) % 4, self.me % 2
        self.other = self.me + 1 - 2 * self.c

    def seg(self, on_x, step):
        if on_x:
            return (((self.x + step) % 4) * 4 + self.y) * 2 + self.c
        return (self.x * 4 + (self.y + step) % 4) * 2 + self.c

    def ring(self, part, which, step):
        return self.seg((part == 0) == (which == 1), step)

    def pos(self, part, which):
        return self.x if (part == 0) == (which == 1) else self.y

    def by_part(self, k, fn):
        for part in range(2):
            pl.when(k % 2 == part)(functools.partial(fn, part))

    @staticmethod
    def ahead(k):
        return 1 + 2 * ((k // 2) % 2)


class Gather(Plane):
    def __init__(self, r):
        super().__init__()
        self.r = r
        self.z = lax.axis_index("grp")
        self.mine, self.others = 4 + 2 * (self.z % 2), 6 - 2 * (self.z % 2)

    def unit(self, i):
        return jnp.where(i < 3, i, jnp.where(i < 5, self.mine + i - 3, jnp.where(i == 5, 3, i + 2)))

    def to_plane(self, k, row):
        @pl.when((k >= 4) & (k < 8))
        def _():
            z = (self.z + 1 + 6 * (k % 2)) % 8
            zcopy(row, row, self.r.up_s, self.r.up_r.at[k - 4], z, self.me).start()

    def from_planes(self):
        r = self.r
        for j in range(2):
            k = self.others + j
            unit = r.ws.at[self.c, k]
            take(unit, r.up_r.at[k - 4])
            rcopy(unit, unit, r.s3, r.r3.at[k], self.other).start()

    def v1(self, k, part, off):
        mine = self.r.ws.at[self.c, k]
        return mine.at[(self.x + off) % 4, self.y] if part == 0 else mine.at[self.x, (self.y + off) % 4]

    def v2(self, k, part, off):
        mine = self.r.ws.at[self.c, k]
        return mine.at[:, (self.y + off) % 4] if part == 0 else mine.at[(self.x + off) % 4]

    def first(self, k):
        r = self.r

        def go(part):
            own = self.v1(k, part, 0)
            src = r.stage.at[k]
            pltpu.make_async_copy(src, own, r.own_sem.at[k]).start()
            rcopy(src, own, r.s1, r.r1.at[k, 0], self.ring(part, 1, 1)).start()
            rcopy(src, own, r.s1, r.r1.at[k, 1], self.ring(part, 1, 3)).start()

        @pl.when((k < 4) | (k >= 8) | (k // 2 == self.mine // 2))
        def _():
            self.by_part(k, go)

    def first_on(self, k):
        r, ahead = self.r, self.ahead(k)

        def go(part):
            block = self.v1(k, part, 4 - ahead)
            take(block, r.r1.at[k, ahead // 2])
            rcopy(block, block, r.s1, r.r1.at[k, 1 - ahead // 2], self.ring(part, 1, ahead)).start()

        self.by_part(k, go)

    def second(self, k):
        r, ahead = self.r, self.ahead(k)

        def go(part):
            take(r.ws.at[0, 0, 0, pl.ds(0, 2)], r.r1.at[k, 1 - ahead // 2])
            own = self.v1(k, part, 0)
            take(own, r.own_sem.at[k])
            row = self.v2(k, part, 0)
            rcopy(row, row, r.s2, r.r2.at[k, 0], self.ring(part, 2, 1)).start()
            rcopy(row, row, r.s2, r.r2.at[k, 1], self.ring(part, 2, 3)).start()
            rcopy(row, row, r.s3, r.r3.at[k], self.other).start()
            self.to_plane(k, row)

        self.by_part(k, go)

    def second_on(self, k):
        r, ahead = self.r, self.ahead(k)

        def go(part):
            row = self.v2(k, part, 4 - ahead)
            take(row, r.r2.at[k, ahead // 2])
            rcopy(row, row, r.s2, r.r2.at[k, 2], self.ring(part, 2, ahead)).start()
            rcopy(row, row, r.s3, r.r3.at[k], self.other).start()
            self.to_plane(k, row)
            row = self.v2(k, part, ahead)
            take(row, r.r2.at[k, 1 - ahead // 2])
            rcopy(row, row, r.s3, r.r3.at[k], self.other).start()
            self.to_plane(k, row)

        self.by_part(k, go)

    def last(self, k):
        r = self.r

        def go(part):
            row = self.v2(k, part, 2)
            take(row, r.r2.at[k, 2])
            rcopy(row, row, r.s3, r.r3.at[k], self.other).start()
            self.to_plane(k, row)

        self.by_part(k, go)

    def arrived(self, k):
        r = self.r
        take(r.ws.at[1 - self.c, k], r.r3.at[k])

    def drain(self):
        r = self.r

        take(r.ws.at[0, pl.ds(0, 10), 0, pl.ds(0, 3)], r.s1)
        take(r.ws.at[0, pl.ds(0, 10), pl.ds(0, 3)], r.s2)
        take(r.ws.at[0, pl.ds(0, 2)], r.up_s)
        take(r.ws.at[0], r.s3)


class Reduce(Plane):
    def __init__(self, r, pieces):
        super().__init__()
        self.r, self.pieces = r, pieces
        self.z = lax.axis_index("grp")

    def peers(self, fn):
        loop(7, lambda i: fn((self.z + 1 + i) % 8))

    def to_sibling(self, k):
        r = self.r
        rcopy(r.gb.at[1, k], r.r0.at[k], r.ms.at[0], r.mr.at[k, 0], self.other).start()

    def msg(self, k, part, q):
        return self.r.gb.at[0, k, :, q] if part == 0 else self.r.gb.at[0, k, q]

    def step_a(self, k):
        r, ahead = self.r, self.ahead(k)
        take(r.r0.at[k], r.mr.at[k, 0])

        def add(i):
            px, py = i // 4, i % 4
            r.gb[0, k, px, py] = (r.gb[0, k, px, py].astype(F32) + r.r0[k, px, py].astype(F32)).astype(BF16)

        loop(16, add)

        def go(part):
            q = self.pos(part, 2)
            far, back = self.msg(k, part, (q + 2) % 4), self.msg(k, part, (q + 4 - ahead) % 4)
            rcopy(far, r.f2.at[k], r.ms.at[1], r.mr.at[k, 1], self.ring(part, 2, ahead)).start()
            rcopy(back, r.b2.at[k], r.ms.at[1], r.mr.at[k, 2], self.ring(part, 2, 4 - ahead)).start()

        self.by_part(k, go)

    def step_b(self, k):
        r, ahead = self.r, self.ahead(k)
        take(r.f2.at[k], r.mr.at[k, 1])

        def go(part):
            block = self.msg(k, part, (self.pos(part, 2) + ahead) % 4)

            def add(i):
                block[i] = (block[i].astype(F32) + r.f2[k, i].astype(F32)).astype(BF16)

            loop(4, add)
            rcopy(block, r.a2.at[k], r.ms.at[1], r.mr.at[k, 2], self.ring(part, 2, ahead)).start()

        self.by_part(k, go)

    def step_c(self, k):
        r = self.r
        take(r.r0.at[0, pl.ds(0, 2)], r.mr.at[k, 2])

        def go(part):
            block = self.msg(k, part, self.pos(part, 2))

            def add(i):
                r.t1[k, i] = (block[i].astype(F32) + r.a2[k, i].astype(F32) + r.b2[k, i].astype(F32)).astype(BF16)

            loop(4, add)
            q = self.pos(part, 1)
            for step, dst in ((1, r.a1), (2, r.f1), (3, r.b1)):
                block = r.t1.at[k, (q + step) % 4]
                rcopy(block, dst.at[k], r.ms.at[2], r.mr.at[k, 3], self.ring(part, 1, step)).start()

        self.by_part(k, go)

    def step_d(self, k):
        r = self.r
        take(r.r0.at[0, 0, pl.ds(0, 3)], r.mr.at[k, 3])

        def go(part):
            t = r.t1[k, self.pos(part, 1)].astype(F32) + r.f1[k].astype(F32)
            t += r.a1[k].astype(F32) + r.b1[k].astype(F32)
            self.pieces[k // 4, pl.ds(2 * (k % 4), 2)] = t.reshape(2, 24, W).astype(BF16)

        self.by_part(k, go)

    def sent(self, slots):
        r = self.r
        some = pl.ds(0, slots * 3 // 4)
        take(r.r0, r.ms.at[0])
        take(r.r0.at[some], r.ms.at[1])
        take(r.r0.at[some, 0], r.ms.at[2])

    def z_send(self, g):
        r, z, me = self.r, self.z, self.me
        self.peers(lambda zz: zcopy(r.zp.at[g, zz], r.zr.at[g, z], r.zss.at[g, 0], r.zsr.at[g, 0], zz, me).start())
        pltpu.make_async_copy(r.zp.at[g, z], r.zr.at[g, z], r.zsr.at[g, 0]).start()

    def z_sum(self, g):
        r, z, me, c = self.r, self.z, self.me, self.c
        take(r.zr.at[g], r.zsr.at[g, 0])
        r.zs[g] = jnp.sum(r.zr[g].astype(F32), axis=0).astype(BF16)
        m, h = z // 2, z % 2

        def out(dst, sem, seg):
            def one(zz):
                here = (zz == z) & (seg == me)

                @pl.when(here)
                def _():
                    pltpu.make_async_copy(r.zs.at[g], dst, sem).start()

                @pl.when(jnp.logical_not(here))
                def _():
                    zcopy(r.zs.at[g], dst, r.zss.at[g, 1], sem, zz, seg).start()

            loop(8, one)

        if g == 0:
            out(r.fd.at[z], r.zsr.at[0, 1], me)
        elif g == 1:
            out(r.fa.at[8 + 2 * m + c], r.zsr.at[1, 1], me - c + h)
        else:
            out(r.fa.at[2 * ((m + 3) % 4) + c], r.zsr.at[2, 1], me - c + h)

    def z_sent(self):
        r, z, c = self.r, self.z, self.c
        for g in range(3):
            take(r.zr.at[g, pl.ds(0, 7)], r.zss.at[g, 0])
            stays = (z % 2 == c) if g > 0 else (z >= 0)

            @pl.when(stays)
            def _():
                take(r.zr.at[g, pl.ds(0, 7)], r.zss.at[g, 1])

            @pl.when(jnp.logical_not(stays))
            def _():
                take(r.zr.at[g], r.zss.at[g, 1])


F_IN = list(dict(tok=0, cot=0, qkv=0, out=0, up=0, down=0, bias=0, upbias=0, gains=0, cqkv=0, cout=0, cup=0, cdown=0, cbias=0, cupbias=0, cgains=0, pos=0, doc=0))
F_OUT = dict(
    lo_h=((ROWS, D), BF16),
    tg_h=((ROWS, D), F32),
    fa=((16, 24, W), BF16),
    fd=((8, 24, W), BF16),
    cf=((8, 2, 24, W), BF16),
    uf=((8, 4, 24, 128), BF16),
    osm=((12, 8, D), BF16),
)


def reduce_scratch(n):
    unit, line = (4, 4, 48, W), (n, 4, 48, W)
    return dict(
        gb=VM((2, n) + unit, BF16),
        r0=VM((n,) + unit, BF16),
        f2=VM(line, BF16),
        a2=VM(line, BF16),
        b2=VM(line, BF16),
        t1=VM(line, BF16),
        f1=VM((n, 48, W), BF16),
        a1=VM((n, 48, W), BF16),
        b1=VM((n, 48, W), BF16),
        mr=DMA((n, 4)),
        ms=DMA((3,)),
    )


F_SCR = dict(
    ws=VM((2, 12, 4, 4, 48, W), BF16),
    stage=VM((12, 48, W), BF16),
    sibq=VM((24, 3 * D), BF16),
    sibo=VM((24, D), BF16),
    sibu=VM((24, FF), BF16),
    smf=VM((16, 256), F32),
    sm=VM((16, 256), BF16),
    smg=VM((16, 2, 16, 256), BF16),
    both=VM((16, D), F32),
    lb=VM((8, D), F32),
    lub=VM((1, FF), F32),
    cub=VM((8, 128), F32),
    cb=VM((8, D), F32),
    qkvv=VM((3, ROWS, D), BF16),
    mix=VM((ROWS, D), BF16),
    aw=VM((3, 6, 256, 128), BF16),
    n1=VM((ROWS, D), F32),
    f=VM((ROWS, D), BF16),
    g=VM((ROWS, FF), BF16),
    gpl=VM((ROWS, FF), BF16),
    rst=VM((ROWS, 128), F32),
    dd=VM((ROWS, D), BF16),
    hf=VM((8, D), BF16),
    hg=VM((8, FF), BF16),
    hgp=VM((8, FF), F32),
    hn=VM((2, 8, D), F32),
    hrst=VM((2, 8, 128), F32),
    hgs=VM((32, 8, 128), BF16),
    hfp=VM((8, W), BF16),
    hdp=VM((8, W), BF16),
    hdd=VM((8, D), BF16),
    hdf=VM((8, D), F32),
    hs=DMA((3,)),
    hr=DMA((3,)),
    sib_s=DMA((3,)),
    sib_r=DMA((3,)),
    sm_s=DMA((2,)),
    sm_r=DMA((2,)),
    own_sem=DMA((12,)),
    s1=DMA,
    r1=DMA((12, 2)),
    s2=DMA,
    r2=DMA((12, 3)),
    s3=DMA,
    r3=DMA((12,)),
    up_s=DMA,
    up_r=DMA((4,)),
    lo=VM((ROWS, D), BF16),
    tg=VM((ROWS, D), F32),
    done=DMA((2,)),
    sloc=VM((8, D), F32),
    dcl=VM((1, FF), F32),
    dx=VM((8, D), F32),
    hfd=VM((2, 16, 2, 8, W), BF16),
    hgr=VM((32, 8, 128), BF16),
    gdn=VM((96, D), BF16),
    small=VM((8, D), F32),
    dc=VM((8, 128), F32),
    gup=VM((32, 24, 128), BF16),
    gqkv=VM((6, 3, 24, 128), BF16),
    go=VM((2, 24, D), BF16),
    cu=VM((2, 16, 24, 128), BF16),
    zc=VM((24, W), F32),
    zp=VM((3, 8, 24, W), BF16),
    zr=VM((3, 8, 24, W), BF16),
    zs=VM((3, 24, W), BF16),
    c0=VM((16, 24, W), BF16),
    cr=VM((8, 2, 24, W), BF16),
    cs=VM((2, 24, W), BF16),
    ur=VM((8, 4, 24, 128), BF16),
    us=VM((4, 24, 128), BF16),
    sf=VM((96, D), F32),
    s0=VM((12, 8, D), BF16),
    sm1=VM((8, D), BF16),
    sm2=VM((8, D), BF16),
    xr=DMA((8,)),
    xs=DMA((8,)),
    zsr=DMA((3, 2)),
    zss=DMA((3, 2)),
    ks=DMA((4,)),
    kr=DMA((4,)),
    free=pltpu.SemaphoreType.REGULAR,
    mr2=DMA((4, 4)),
    ms2=DMA((3,)),
    **reduce_scratch(8),
    **{("x" + n if n in ("rst", "dd", "de", "cs", "cr") else n): v for n, v in CROSS.items()},
)


def layer_kernel(*refs):
    r = fields(F_IN + list(F_OUT) + list(F_SCR), refs)
    ring = Gather(r)
    cross = CrossGrads(r, r)
    again = types.SimpleNamespace(
        gb=r.ws.at[:, pl.ds(4, 4)],
        r0=r.ws.at[0, pl.ds(8, 4)],
        f2=r.ws.at[1, 8],
        a2=r.ws.at[1, 9],
        b2=r.ws.at[1, 10],
        t1=r.ws.at[1, 11],
        f1=r.stage.at[pl.ds(0, 4)],
        a1=r.stage.at[pl.ds(4, 4)],
        b1=r.stage.at[pl.ds(8, 4)],
        mr=r.mr2,
        ms=r.ms2,
    )
    red, red2 = Reduce(r, r.zp.at[pl.ds(0, 2)]), Reduce(again, r.zp.at[pl.ds(2, 1)])
    me, c, z = ring.me, ring.c, red.z
    is_owner = (c == 0) & (me < 24)
    r.n2, r.de, r.do = r.tg, r.f, r.dd
    r.pcu, r.po_f, r.pu, r.pq, r.po = r.xup, r.wout_f, r.pup, r.xqkv, r.xout
    r.sz, r.sg = r.g46.at[pl.ds(0, 32)], r.g46.at[pl.ds(32, 32)]
    bar = pltpu.get_barrier_semaphore()
    loop(31, lambda i: pl.semaphore_signal(bar, inc=1, device_id={"seg": (me + 1 + i) % 32}, device_id_type=MESH))

    def greet(zz):
        for seg in (me, red.other):
            pl.semaphore_signal(bar, inc=1, device_id={"grp": zz, "seg": seg}, device_id_type=MESH)

    red.peers(greet)
    r.smf[...] = jnp.zeros((16, 256), F32)
    r.smf[0:6, 0:24] = r.bias[...].astype(F32)
    r.smf[6:8, 0:24] = r.gains[...].astype(F32)
    r.smf[8:14, 0:24] = r.cbias[...].astype(F32)
    r.smf[14:16, 0:24] = r.cgains[...].astype(F32)
    r.smf[0:1, 32:128] = r.upbias[...].astype(F32)
    table = r.pos[...].astype(F32)
    for t in range(2):
        for i in range(6):
            r.smf[6 * t + i : 6 * t + i + 1, 128:256] = table[t : t + 1, 128 * i : 128 * (i + 1)]
    r.sm[...] = r.smf[...].astype(BF16)
    r.cub[...] = jnp.zeros((8, 128), F32)
    r.cub[0:1, 0:96] = r.cupbias[...].astype(F32)
    pl.semaphore_wait(bar, 45)

    swaps = [(r.qkv, r.sibq), (r.out, r.sibo), (r.up, r.sibu)]
    for i, (src, dst) in enumerate(swaps):
        rcopy(src, dst, r.sib_s.at[i], r.sib_r.at[i], ring.other).start()
    for j in range(4):
        r.stage[8 + j] = r.down[(j % 2) * 48 : (j % 2) * 48 + 48, (j // 2) * W : (j // 2 + 1) * W]

    def compose(k, src, sib, block):
        own = src[:, col(block)].astype(F32)
        oth = sib[:, col(block)].astype(F32)
        lo, hi = jnp.where(c == 0, own, oth), jnp.where(c == 0, oth, own)
        r.stage[k] = jnp.concatenate([lo, hi], axis=0).astype(BF16)
        ring.first(k)

    def arrive(i):
        take(swaps[i][1], r.sib_r.at[i])

    arrive(0)
    loop(3, lambda k: compose(k, r.qkv, r.sibq, 2 * k + c))
    arrive(1)
    compose(3, r.out, r.sibo, c)
    arrive(2)
    loop(8, lambda k: compose(k, r.up, r.sibu, 2 * (k - 4) + c), 4)
    loop(12, ring.first, 8)
    loop(16, lambda t: send_to(me, 2 * t + c, r.sm, r.smg.at[me // 2, c], r.sm_s.at[0], r.sm_r.at[0]))
    loop(10, lambda i: ring.first_on(ring.unit(i)))
    loop(6, lambda i: ring.second(ring.unit(i)))
    take(r.smg.at[:, 0], r.sm_r.at[0])
    rcopy(r.smg.at[:, c], r.smg.at[:, c], r.sm_s.at[1], r.sm_r.at[1], ring.other).start()

    def tick(i):
        ring.second_on(ring.unit(i))

        @pl.when(i < 4)
        def _():
            ring.second(ring.unit(i + 6))

        @pl.when(i >= 3)
        def _():
            ring.last(ring.unit(i - 3))

    def weight(cc, k):
        return r.ws[cc, k].reshape(D, W)

    loop(3, tick)
    take(r.smg.at[:, 0], r.sm_r.at[1])
    for t in range(32):
        block = r.smg[t // 2, t % 2].astype(F32)
        r.both[:, 24 * t : 24 * t + 24] = block[:, 0:24]
        r.lub[:, 96 * t : 96 * t + 96] = block[0:1, 32:128]
    r.lb[...] = r.both[0:8, :]
    r.cb[...] = r.both[8:16, :]
    tick(3)

    def project(k):
        tick(k)
        i = k - 4
        ring.arrived(i)
        shift = jnp.where(i == 0, r.lb[0:1, :], jnp.where(i == 2, r.lb[1:2, :], 0.0))
        for cc in range(2):
            part = slice(cc * W, (cc + 1) * W)
            r.qkvv[i, :, part] = (dot(r.tok[...], weight(cc, i)) + shift[:, part]).astype(BF16)

    loop(7, project, 4)
    cross.reshard()

    def attend(k):
        tick(k)
        s = k - 7
        rows = pl.ds(pl.multiple_of(s * 128, 128), 128)
        for p in range(6):
            part = slice(128 * p, 128 * (p + 1))
            w = softmax(dot_bt(two_heads(r.qkvv[0, rows, part]), r.qkvv[1, rows, part]) * 0.125).astype(BF16)
            r.aw[s, p] = w
            r.mix[rows, part] = side_by_side(dot(w, r.qkvv[2, rows, part])).astype(BF16)

    loop(10, attend, 7)
    ring.arrived(3)
    for cc in range(2):
        part = slice(cc * W, (cc + 1) * W)
        r.n1[:, part] = dot(r.mix[...], weight(cc, 3)) + (r.tok[:, part].astype(F32) + r.lb[2:3, part])
    row8 = lax.broadcasted_iota(jnp.int32, (8, D), 0)
    r.sloc[...] = jnp.zeros((8, D), F32)

    def heads(ref):
        out = jnp.zeros((8, D), F32)
        for s in range(3):
            top = ref[128 * s : 128 * s + 16, :].astype(F32)[0:1, :]
            out = jnp.where(row8 == s, top, out)
        return out

    def head_norm(i, value):
        n, rstd = norm(value)
        r.hn[i] = n
        r.hrst[i] = jnp.broadcast_to(rstd, (8, 128))
        return n

    hf = head_norm(0, heads(r.n1)) * r.lb[6:7, :] + r.lb[3:4, :]
    r.hf[...] = jnp.where(row8 < 3, hf, 0.0).astype(BF16)

    def head_up(i):
        ring.arrived(i)
        for cc in range(2):
            part = col(2 * (i - 4) + cc)
            g, gp = gelu_both(dot(r.hf[...], weight(cc, i)) + r.lub[0:1, part])
            keep = lax.broadcasted_iota(jnp.int32, (8, W), 0) < 3
            r.hg[:, part] = jnp.where(keep, g, 0.0).astype(BF16)
            r.hgp[:, part] = gp

    head_up(ring.mine)
    head_up(ring.mine + 1)
    ring.last(ring.unit(7))
    ring.from_planes()
    ring.last(ring.unit(8))
    ring.last(ring.unit(9))
    head_up(ring.others)
    head_up(ring.others + 1)

    def down_rows(x, kc):
        pieces = [r.ws[cc, 8 + 2 * kc + j, x, y] for y in range(4) for cc in range(2) for j in range(2)]
        return jnp.concatenate(pieces, axis=0)

    halves = []
    for kc in range(2):
        for j in range(2):
            ring.arrived(8 + 2 * kc + j)
        part = slice(kc * W, (kc + 1) * W)
        acc = r.hf[:, part].astype(F32) + r.lb[4:5, part]
        for x in range(4):
            acc += dot(r.hg[:, D * x : D * (x + 1)], down_rows(x, kc))
        halves.append(acc)
    z0 = head_norm(1, jnp.concatenate(halves, axis=1)) * r.lb[7:8, :] + r.lb[5:6, :]
    cross.reshard_end()
    cross.start(z0, heads(r.cot))

    def blocks(fn):
        loop(ROWS // 64, lambda i: fn(pl.ds(pl.multiple_of(i * 64, 64), 64)))

    def norm_one(rows):
        n, rstd = norm(r.n1[rows, :])
        r.n1[rows, :] = n
        r.rst[rows, :] = jnp.broadcast_to(rstd, (64, 128))
        r.f[rows, :] = (n * r.lb[6:7, :] + r.lb[3:4, :]).astype(BF16)

    def raise_up(i):
        def half(cc):
            part = col(2 * (i - 4) + cc)
            g, gp = gelu_both(dot(r.f[...], weight(cc, i)) + r.lub[0:1, part])
            r.g[:, part] = g.astype(BF16)
            r.gpl[:, part] = gp.astype(BF16)

        loop(2, half)

    def lower(kc):
        part = slice(kc * W, (kc + 1) * W)
        r.n2[:, part] = r.f[:, part].astype(F32) + r.lb[4:5, part]

        def quarter(x):
            r.n2[:, part] += dot(r.g[:, col(x, D)], down_rows(x, kc))

        loop(4, quarter)

    row64 = lax.broadcasted_iota(jnp.int32, (64, D), 0)

    def norm_two(i):
        rows = pl.ds(pl.multiple_of(i * 64, 64), 64)
        n, rstd = norm(r.n2[rows, :])
        r.lo[rows, :] = (n * r.lb[7:8, :] + r.lb[5:6, :]).astype(BF16)
        dy = jnp.where((row64 == 0) & (i % 2 == 0), 0.0, r.cot[rows, :].astype(F32))
        dr2 = norm_back(dy, n, rstd, r.lb[7:8, :])
        dd = dr2.astype(BF16)
        r.n2[rows, :] = dr2
        r.dd[rows, :] = dd
        r.sloc[5:6, :] += sum0(dy)
        r.sloc[7:8, :] += sum0(dy * n)
        r.sloc[4:5, :] += sum0(dd.astype(F32))

    def down_grad(b):
        v = dot_at(r.g[:, col(b)], r.dd[...]).astype(BF16).reshape(2, 2, 2, 48, D)
        for chip in range(2):
            for cc in range(2):
                for j in range(4):
                    v4 = v[chip, cc, j % 2, :, (j // 2) * W : (j // 2 + 1) * W]
                    r.gb[(cc + c) % 2, j, b // 2, 2 * (b % 2) + chip] = v4

    def down_block(b, kc):
        chips = [(b // 2, 2 * (b % 2) + chip) for chip in range(2)]
        pieces = [r.ws[cc, 8 + 2 * kc + j, x, y] for x, y in chips for cc in range(2) for j in range(2)]
        return jnp.concatenate(pieces, axis=0)

    def middle(b):
        part = col(b)
        dg = dot_bt(r.dd[:, 0:W], down_block(b, 0)) + dot_bt(r.dd[:, W:D], down_block(b, 1))
        du = (dg * r.gpl[:, part].astype(F32)).astype(BF16)
        r.dcl[:, part] = sum0(du.astype(F32))
        r.n2[...] += dot_bt(du, r.ws[b % 2, 4 + b // 2].reshape(D, W))
        r.gb[(b + c) % 2, 4 + b // 2] = dot_at(r.f[...], du).astype(BF16).reshape(4, 4, 48, W)

        @pl.when(b % 2 == 1)
        def _():
            red.to_sibling(4 + b // 2)

    def norm_one_back(rows):
        df, n = r.n2[rows, :], r.n1[rows, :]
        dr1 = norm_back(df, n, r.rst[rows, 0:1], r.lb[6:7, :])
        de = dr1.astype(BF16)
        r.n2[rows, :] = dr1
        r.de[rows, :] = de
        r.sloc[3:4, :] += sum0(df)
        r.sloc[6:7, :] += sum0(df * n)
        r.sloc[2:3, :] += sum0(de.astype(F32))

    def out_back(de):
        return dot_bt(de[:, 0:W], weight(0, 3)) + dot_bt(de[:, W:D], weight(1, 3))

    blocks(norm_one)
    loop(6, raise_up, 4)
    cross.attention()
    loop(8, raise_up, 6)
    def pack(value):
        n = value.shape[1] // 2
        row = lax.broadcasted_iota(jnp.int32, (8, n), 0)
        both = jnp.where(row < 3, value[:, :n], pltpu.roll(value[:, n:], 3, 0))
        return jnp.where(row < 6, both, 0.0)

    r.hgs[...] = jnp.zeros((32, 8, 128), BF16)
    hidden, slope = r.hg[...].astype(F32), r.hgp[...]
    for t in range(32):
        part = slice(96 * t, 96 * t + 96)
        both = jnp.concatenate([hidden[:, part], slope[:, part]], axis=1)
        r.hgs[t, :, 0:96] = pack(both).astype(BF16)
    r.hfp[...] = pack(r.hf[...].astype(F32)).astype(BF16)
    cross.first_norm()
    lower(0)
    lower(1)
    cross.mlp()
    loop(6, norm_two)
    loop(4, down_grad)
    cross.second_norm()
    loop(8, down_grad, 4)
    loop(4, red.to_sibling)
    loop(2, middle)
    cross.mlp_back()
    middle(2)
    loop(4, red.step_a)
    loop(5, middle, 3)
    cross.first_norm_back()
    loop(8, middle, 5)
    cross.attention_back()
    loop(4, red.step_b)
    blocks(norm_one_back)
    r.do[...] = out_back(r.de[...]).astype(BF16)
    loop(6, red.step_a, 4)
    cross.grads()
    cross.scatter()
    r.dx[...] = jnp.where(row8 < 3, cross.finish(), 0.0)

    dy0, hn2 = r.dx[...], r.hn[1]
    dr2 = norm_back(dy0, hn2, r.hrst[1, :, 0:1], r.lb[7:8, :])
    r.hdd[...] = dr2.astype(BF16)
    r.hdf[...] = dr2
    r.hdp[...] = pack(dr2).astype(BF16)
    loop(16, lambda t: send_to(me, 2 * t + c, r.hdp, r.hfd.at[1, me // 2, c], r.hs.at[1], r.hr.at[1]))
    loop(32, lambda t: send_to(me, t, r.hgs.at[t], r.hgr.at[me], r.hs.at[0], r.hr.at[0]))
    loop(16, lambda t: send_to(me, 2 * t + c, r.hfp, r.hfd.at[0, me // 2, c], r.hs.at[1], r.hr.at[1]))
    loop(8, red.step_a, 6)
    r.sloc[5:6, :] += sum0(dy0)
    r.sloc[7:8, :] += sum0(dy0 * hn2)
    r.sloc[4:5, :] += sum0(r.hdd[...].astype(F32))

    def head_middle(i):
        for cc in range(2):
            b = 2 * i + cc
            part = col(b)
            dg = dot_bt(r.hdd[:, 0:W], down_block(b, 0)) + dot_bt(r.hdd[:, W:D], down_block(b, 1))
            du = (dg * r.hgp[:, part]).astype(BF16)
            r.dcl[:, part] += sum0(du.astype(F32))
            r.hdf[...] += dot_bt(du, weight(cc, 4 + i))

    loop(4, head_middle)
    ring.drain()
    for t in (ring.other, ring.seg(True, 1), ring.seg(True, 3), ring.seg(False, 1), ring.seg(False, 3)):
        pl.semaphore_signal(r.free, inc=1, device_id={"seg": t}, device_id_type=MESH)
    df, hn1 = r.hdf[...], r.hn[0]
    dr1 = norm_back(df, hn1, r.hrst[0, :, 0:1], r.lb[6:7, :])
    de = dr1.astype(BF16)
    r.sloc[3:4, :] += sum0(df)
    r.sloc[6:7, :] += sum0(df * hn1)
    r.sloc[2:3, :] += sum0(de.astype(F32))
    do = out_back(de)
    y = cross.output_rows()
    row16 = lax.broadcasted_iota(jnp.int32, (16, D), 0)

    def put(ref, s, value):
        rows = slice(128 * s, 128 * s + 16)
        ref[rows, :] = jnp.where(row16 == 0, value[s : s + 1, :], ref[rows, :].astype(F32)).astype(ref.dtype)

    for s in range(3):
        put(r.lo, s, y)
        put(r.n2, s, dr1)
        put(r.de, s, de.astype(F32))
        put(r.do, s, do)
    pltpu.make_async_copy(r.lo, r.lo_h, r.done.at[0]).start()

    def attend_back(s):
        rows = pl.ds(pl.multiple_of(s * 128, 128), 128)
        for p in range(6):
            part = slice(128 * p, 128 * (p + 1))
            q, k, v = r.qkvv[0, rows, part], r.qkvv[1, rows, part], r.qkvv[2, rows, part]
            do = two_heads(r.do[rows, part])
            w = r.aw[s, p]
            ds = softmax_back(w.astype(F32), dot_bt(do, v)).astype(BF16)
            r.qkvv[0, rows, part] = (side_by_side(dot(ds, k)) * 0.125).astype(BF16)
            r.qkvv[1, rows, part] = (dot_at(ds, two_heads(q)) * 0.125).astype(BF16)
            r.qkvv[2, rows, part] = dot_at(w, do).astype(BF16)

    attend_back(0)
    loop(6, red.step_b, 4)
    pl.semaphore_wait(r.free, 5)
    for cc in range(2):
        again.gb[(cc + c) % 2, 0] = dot_at(r.mix[...], r.de[:, cc * W : (cc + 1) * W]).astype(BF16).reshape(4, 4, 48, W)
    red2.to_sibling(0)
    attend_back(1)
    cross.planes(red)
    attend_back(2)
    loop(8, red.step_b, 6)

    def qkv_grad(i):
        for cc in range(2):
            part = slice(cc * W, (cc + 1) * W)
            again.gb[(cc + c) % 2, i + 1] = dot_at(r.tok[...], r.qkvv[i, :, part]).astype(BF16).reshape(4, 4, 48, W)

    def qkv_out(i):
        qkv_grad(i)
        red2.to_sibling(i + 1)

    loop(3, qkv_out)
    take(r.hfd.at[:, :, 0], r.hr.at[1])
    rcopy(r.hfd.at[:, :, c], r.hfd.at[:, :, c], r.hs.at[2], r.hr.at[2], ring.other).start()
    loop(4, red.step_c)
    red2.step_a(0)

    def second_round(step):
        loop(4, step)

    sf = r.sf
    sf[...] = jnp.zeros((96, D), F32)
    sf[0:8, :] = r.sloc[...]
    sf[0:1, :] = sum0(r.qkvv[0].astype(F32))
    sf[1:2, :] = sum0(r.qkvv[2].astype(F32))
    sf[8:16, :] = r.small[...]
    for i in range(4):
        sf[16 + i : 17 + i, :] = r.dcl[:, D * i : D * (i + 1)]
    own = jnp.concatenate([r.dc[0:1, :], jnp.zeros((1, D - 128), F32)], axis=1)
    own = pltpu.roll(own, 96 * (me % 8), 1)
    sf[pl.ds(20 + me // 8, 1), :] = own
    line = lax.broadcasted_iota(jnp.int32, (64, D), 0)
    for s in range(3):
        _, place = slot_layout(r.doc, (64, D), jnp.full((64, D), me * 3 + s, jnp.int32))
        sf[24:88, :] += jnp.where(line == place, r.dx[s : s + 1, :], 0.0)
    r.s0[...] = sf[...].reshape(12, 8, D).astype(BF16)
    xs, xr = r.xs, r.xr
    loop(12, lambda k: send_to(me, owner_seg(k), r.s0.at[k], r.sg.at[me], xs.at[0], xr.at[0]))

    loop(4, red2.step_a, 1)
    loop(8, red.step_c, 4)
    take(r.hgr, r.hr.at[0])
    take(r.hfd.at[:, :, 0], r.hr.at[2])
    hfa, dda = [r.hfd[i].astype(F32).reshape(256, W).astype(BF16) for i in range(2)]
    both = flat8(r.hgr[...])
    line = lax.broadcasted_iota(jnp.int32, (256, 128), 0) % 8

    def low(v):
        return jnp.where(line[:, : v.shape[1]] < 3, v, 0.0)

    left, right = dot_bt(dda, r.down[:, 0:W]), dot_bt(dda, r.down[:, W:D])
    du = low((left + pltpu.roll(right, 253, 0)) * pltpu.roll(both, 253, 0)[:, 0:96])
    share_up = [dot_at(hfa, v.astype(BF16)) for v in (du, pltpu.roll(du, 3, 0))]
    r.pcu[:, :, 0:96] = jnp.concatenate(share_up, axis=0).reshape(32, 24, 96).astype(BF16)
    core = (me // 4) % 2

    def share(t):
        send_to(me, t - t % 2 + core, r.pcu.at[t], r.cu.at[t % 2, (me // 8) * 4 + me % 4], r.ks.at[3], r.kr.at[3])

    loop(32, share)
    loop(4, red.step_d)
    hidden = low(both)
    down_share = [dot_at(v.astype(BF16), dda)[0:96] for v in (hidden, pltpu.roll(hidden, 3, 0))]
    for n in range(8):
        j, h = n // 2, n % 2
        top = (j % 2) * 48 + 24 * h
        piece = down_share[j // 2][top : top + 24]
        r.zp[0, n] = (r.zp[0, n].astype(F32) + piece).astype(BF16)
    red.z_send(0)
    cross.planes_sum(red)
    second_round(red2.step_b)
    loop(8, red.step_d, 4)

    @pl.when(is_owner)
    def _():
        take(r.sg, xr.at[0])
        r.sm1[...] = jnp.sum(r.sg[...].astype(F32), axis=0).astype(BF16)
        red.peers(lambda zz: zcopy(r.sm1, r.sz.at[z], xs.at[3], xr.at[3], zz, me).start())
        pltpu.make_async_copy(r.sm1, r.sz.at[z], xr.at[3]).start()

    take(r.cu, r.kr.at[3])
    for n in range(8):
        m, h = n // 2, n % 2
        for q in range(4):
            r.zc[:, 96 * q : 96 * q + 96] = r.cu[h, 4 * m + q].astype(F32)[:, 0:96]
        r.zp[1, n] = (r.zp[1, n].astype(F32) + r.zc[...]).astype(BF16)
    red.z_send(1)
    second_round(red2.step_c)
    red.z_sum(0)

    def token_grad(i):
        acc = dot_bt(r.qkvv[i, :, 0:W], weight(0, i))
        r.tg[...] += acc + dot_bt(r.qkvv[i, :, W : 2 * W], weight(1, i))

    token_grad(0)
    second_round(red2.step_d)
    red.z_send(2)
    token_grad(1)

    @pl.when(is_owner)
    def _():
        take(r.sz.at[pl.ds(0, 8)], xr.at[3])
        r.sm2[...] = jnp.sum(r.sz[0:8].astype(F32), axis=0).astype(BF16)
        loop(32, lambda t: send_to(me, t, r.sm2, r.osm.at[me // 2], xs.at[6], xr.at[6]))

    red.z_sum(1)
    token_grad(2)
    pltpu.make_async_copy(r.tg, r.tg_h, r.done.at[1]).start()
    red.z_sum(2)
    for g, ref in ((0, r.fd), (1, r.fa.at[pl.ds(8, 8)]), (2, r.fa.at[pl.ds(0, 8)])):
        take(ref, r.zsr.at[g, 1])
    take(r.osm, xr.at[6])

    take(r.lo, r.done.at[0])
    take(r.tg, r.done.at[1])

    cross.end()
    cross.drain()
    red2.sent(4)
    red.sent(8)
    red.z_sent()
    for i, (src, dst) in enumerate(swaps):
        take(src, r.sib_s.at[i])
    take(r.smg.at[pl.ds(0, 15), 0], r.sm_s.at[0])
    take(r.smg.at[:, 0], r.sm_s.at[1])
    take(r.hgr.at[pl.ds(0, 31)], r.hs.at[0])
    take(r.hfd.at[:, pl.ds(0, 15), 0], r.hs.at[1])
    take(r.hfd.at[:, :, 0], r.hs.at[2])

    @pl.when(core == c)
    def _():
        take(r.pcu.at[pl.ds(0, 30)], r.ks.at[3])

    @pl.when(core != c)
    def _():
        take(r.pcu, r.ks.at[3])

    @pl.when(is_owner)
    def _():
        take(r.sg.at[pl.ds(0, 11)], xs.at[0])
        take(r.sz.at[pl.ds(0, 7)], xs.at[3])
        take(r.sz.at[pl.ds(0, 31)], xs.at[6])

    @pl.when(jnp.logical_not(is_owner))
    def _():
        take(r.sg.at[pl.ds(0, 12)], xs.at[0])


FORMAT_OUT = dict(
    lo_o=((ROWS, D), BF16),
    tg_o=((ROWS, D), F32),
    oq=((24, 3 * D), F32),
    oo=((24, D), F32),
    ou=((24, FF), F32),
    od=((96, D), F32),
    ob=((6, 24), F32),
    ouv=((1, 96), F32),
    og=((2, 24), F32),
    xoq=((24, 3 * D), F32),
    xoo=((24, D), F32),
    xou=((24, FF), F32),
    xod=((96, D), F32),
    xob=((6, 24), F32),
    xouv=((1, 96), F32),
    xog=((2, 24), F32),
    opos=((2, D), F32),
)


def format_kernel(*refs):
    r = fields(list(F_OUT) + list(FORMAT_OUT), refs)
    me = lax.axis_index("seg")
    r.lo_o[...] = r.lo_h[...]
    r.tg_o[...] = r.tg_h[...]
    for p in range(6):
        for j in range(3):
            r.xoq[:, D * j + 128 * p : D * j + 128 * (p + 1)] = r.cf[p // 2, p % 2, :, 128 * j : 128 * (j + 1)].astype(F32)
    for i in range(2):
        r.xoo[:, W * i : W * (i + 1)] = r.cf[3, i].astype(F32)
        for n in range(4):
            m = 8 + 4 * i + n
            r.xod[24 * n : 24 * (n + 1), W * i : W * (i + 1)] = r.cf[m // 2, m % 2].astype(F32)
    for t in range(32):
        r.xou[:, 96 * t : 96 * t + 96] = r.uf[t // 4, t % 4].astype(F32)[:, 0:96]
    for n in range(8):
        j, h = n // 2, n % 2
        top = (j % 2) * 48 + 24 * h
        r.od[top : top + 24, (j // 2) * W : (j // 2 + 1) * W] = r.fd[n].astype(F32)
    for u in range(8, 16):
        r.ou[:, W * (u - 8) : W * (u - 7)] = r.fa[u].astype(F32)
    ours = pltpu.roll(r.osm[0:2].astype(F32).reshape(16, D), (D - 24 * me) % D, 1)
    r.ob[...] = ours[0:6, 0:24]
    r.og[...] = ours[6:8, 0:24]
    r.xob[...] = ours[8:14, 0:24]
    r.xog[...] = ours[14:16, 0:24]
    ups = pltpu.roll(r.osm[2].astype(F32), (D - 96 * (me % 8)) % D, 1)
    line = lax.broadcasted_iota(jnp.int32, (8, D), 0)
    r.ouv[...] = sum0(jnp.where(line == me // 8, ups, 0.0))[:, 0:96]
    r.xouv[...] = sum0(jnp.where(line == 4 + me // 8, ups, 0.0))[:, 0:96]
    r.opos[...] = pltpu.roll(r.osm[3 + me // 4].astype(F32), (8 - 2 * (me % 4)) % 8, 0)[0:2]
    for u in range(8):
        if u < 6:
            r.oq[:, W * u : W * (u + 1)] = r.fa[u].astype(F32)
        else:
            r.oo[:, W * (u - 6) : W * (u - 5)] = r.fa[u].astype(F32)


def call(kernel, name, ins, outs, scratch, cid, args):
    vm, smem = pl.BlockSpec(memory_space=pltpu.VMEM), pl.BlockSpec(memory_space=pltpu.SMEM)
    hbm = pl.BlockSpec(memory_space=pl.ANY)
    return pl.pallas_call(
        kernel,
        out_shape=tuple(jax.ShapeDtypeStruct(s, t) for s, t in outs.values()),
        in_specs=[smem if n == "doc" else vm for n in ins],
        out_specs=tuple(hbm if n in ("lo_h", "tg_h") else vm for n in outs),
        scratch_shapes=list(scratch.values()),
        compiler_params=pltpu.CompilerParams(
            collective_id=cid, has_side_effects=cid is not None, vmem_limit_bytes=63 << 20
        ),
        name=name,
    )(*args)


def shards(tokens, doc, qkv, out, up, down, bias, upbias, gains, cqkv, cout, cup, cdown, cbias, cupbias, cgains, pos, cot):
    made = call(
        layer_kernel, "layer", F_IN, F_OUT, F_SCR, 0,
        (tokens, cot, qkv, out, up, down, bias, upbias.reshape(1, 96), gains, cqkv, cout, cup, cdown, cbias,
         cupbias.reshape(1, 96), cgains, pos, doc),
    )
    out = dict(zip(FORMAT_OUT, call(format_kernel, "format", list(F_OUT), FORMAT_OUT, {}, None, made)))
    out["ouv"], out["xouv"] = out["ouv"].reshape(96), out["xouv"].reshape(96)
    return tuple(out.values())


def solution(mesh):
    both, seg, cols, flat = P(("grp", "seg"), None), P("seg", None), P(None, "seg"), P("seg")
    weights = (seg, seg, seg, seg, cols, flat, cols)
    in_specs = (both, P("grp", None)) + weights + weights + (seg, both)
    out_specs = (both, both) + weights + weights + (seg,)
    return jax.shard_map(shards, mesh=mesh, in_specs=in_specs, out_specs=out_specs, check_vma=False)
```

```python
import functools
import math
import types

import jax
import jax.numpy as jnp
from jax import lax
from jax.experimental import pallas as pl
from jax.experimental.pallas import tpu as pltpu
from jax.sharding import PartitionSpec as P

D = 768
FF = 3072
ROWS = 384
SEG_LEN = 128
W = 384
F32, BF16 = jnp.float32, jnp.bfloat16
MESH = pl.DeviceIdType.MESH
DMA = pltpu.SemaphoreType.DMA
RSQ2 = 1.0 / math.sqrt(2.0)
RS2PI = 1.0 / math.sqrt(2.0 * math.pi)
VM = pltpu.VMEM


def dot(a, b):
    return lax.dot_general(a, b, (((1,), (0,)), ((), ())), preferred_element_type=F32)


def dot_bt(a, b):
    return lax.dot_general(a, b, (((1,), (1,)), ((), ())), preferred_element_type=F32)


def dot_at(a, b):
    return lax.dot_general(a, b, (((0,), (0,)), ((), ())), preferred_element_type=F32)


def rcopy(src, dst, ssem, rsem, seg):
    return pltpu.make_async_remote_copy(
        src_ref=src, dst_ref=dst, send_sem=ssem, recv_sem=rsem, device_id={"seg": seg}, device_id_type=MESH
    )


def zcopy(src, dst, ssem, rsem, z, seg):
    return pltpu.make_async_remote_copy(
        src_ref=src, dst_ref=dst, send_sem=ssem, recv_sem=rsem, device_id={"grp": z, "seg": seg}, device_id_type=MESH
    )


def take(ref, sem):
    pltpu.make_async_copy(ref, ref, sem).wait()


def send_to(me, target, src, dst, ssem, rsem):
    @pl.when(target != me)
    def _():
        rcopy(src, dst, ssem, rsem, target).start()

    @pl.when(target == me)
    def _():
        pltpu.make_async_copy(src, dst, rsem).start()


def loop(n, fn, first=0):
    def body(i, _):
        fn(i)
        return 0

    lax.fori_loop(first, n, body, 0)


def col(u, width=W):
    return pl.ds(pl.multiple_of(u * width, 128), width)


def norm(v):
    center = v - jnp.mean(v, axis=-1, keepdims=True)
    rstd = lax.rsqrt(jnp.mean(center * center, axis=-1, keepdims=True) + 1e-05)
    return center * rstd, rstd


def norm_back(grad, n, rstd, gain):
    dn = grad * gain
    return rstd * (dn - jnp.mean(dn, axis=-1, keepdims=True) - n * jnp.mean(dn * n, axis=-1, keepdims=True))


def gelu_both(u):
    e = jnp.exp(-0.5 * u * u)
    t = 1.0 / (1.0 + (0.3275911 * RSQ2) * jnp.abs(u))
    poly = t * (0.127414796 + t * (-0.142248368 + t * (0.7107068705 + t * (-0.7265760135 + t * 0.5307027145))))
    tail = poly * e
    cdf = jnp.where(u < 0.0, tail, 1.0 - tail)
    return u * cdf, cdf + u * (RS2PI * e)


def two_heads(v):
    lane = lax.broadcasted_iota(jnp.int32, v.shape, 1)
    none = jnp.zeros_like(v)
    return jnp.concatenate([jnp.where(lane < 64, v, none), jnp.where(lane >= 64, v, none)], axis=0)


def side_by_side(v):
    n = v.shape[0] // 2
    lane = lax.broadcasted_iota(jnp.int32, (n, 128), 1)
    return jnp.where(lane < 64, v[:n], v[n:])


def softmax(s):
    e = jnp.exp(s - jnp.max(s, axis=-1, keepdims=True))
    return e / jnp.sum(e, axis=-1, keepdims=True)


def softmax_back(w, dw):
    return w * (dw - jnp.sum(w * dw, axis=-1, keepdims=True))


def rows8(value):
    return value.reshape(value.shape[0] // 8, 8, value.shape[1])


def flat8(value):
    v = value.astype(F32)
    return v.reshape(v.shape[0] * v.shape[1], v.shape[2])


def sum0(v):
    return jnp.sum(v, axis=0, keepdims=True)


def owner_seg(k):
    return 2 * k


def pair_seg(p):
    return 4 * p + 1


def pair_first(p):
    return 5 * (p % 3) + 16 * (p // 3)


def fields(spec, refs):
    return types.SimpleNamespace(**dict(zip(spec, refs)))


CROSS = dict(
    pup=VM((32, 24, 128), BF16),
    xup=VM((32, 24, 128), BF16),
    xqkv=VM((32, 3, 24, 128), BF16),
    xout=VM((6, 24, D), BF16),
    wup=VM((D, 128), BF16),
    wqkv=VM((D, 384), BF16),
    wout=VM((128, D), BF16),
    wout_f=VM((144, D), F32),
    wdn=VM((128, D), BF16),
    msg=VM((8, D), BF16),
    x1=VM((32, 8, D), BF16),
    own=VM((8, 8, D), F32),
    rst=VM((8, 128), F32),
    xall=VM((96, D), BF16),
    q=VM((3, 96, 128), BF16),
    o=VM((96, 128), BF16),
    af=VM((192, 96), F32),
    p2=VM((12, 8, D), BF16),
    g2=VM((6, 8, D), BF16),
    p3=VM((8, D), BF16),
    g3=VM((12, 8, D), BF16),
    p4=VM((12, 8, D), BF16),
    g46=VM((64, 8, D), BF16),
    p5=VM((2, 8, D), BF16),
    g5=VM((12, 8, D), BF16),
    g5y=VM((2, 8, D), BF16),
    y_r=DMA,
    p6=VM((12, 8, D), BF16),
    p7=VM((8, D), BF16),
    g7=VM((12, 8, D), BF16),
    p7f=VM((8, D), F32),
    g7f=VM((2, 8, D), F32),
    p8=VM((32, 8, W), BF16),
    g8=VM((6, 8, W), BF16),
    gp=VM((96, 128), F32),
    gact=VM((96, 128), BF16),
    fall=VM((96, D), BF16),
    dd=VM((96, D), BF16),
    du=VM((96, 128), BF16),
    dq=VM((96, 384), BF16),
    de=VM((96, D), BF16),
    cs=DMA((12,)),
    cr=DMA((12,)),
    c7=DMA,
)


def slot_layout(doc, shape, slots):
    pos = (slots % 3) * 32 + slots // 3
    number = jnp.zeros(shape, jnp.int32)
    begin = jnp.zeros(shape, jnp.int32)
    end = jnp.int32(0)
    for d in range(6):
        begin = jnp.where(pos >= end, end, begin)
        number = jnp.where(pos >= end, d, number)
        end = end + doc[0, d]
    return number, pos - begin


class Cross:
    def __init__(self, r, a):
        self.r, self.a = r, a
        self.me = lax.axis_index("seg")
        self.is_owner = (self.me % 2 == 0) & (self.me < 24)
        self.k = self.me // 2
        self.is_pair = (self.me % 4 == 1) & (self.me < 24)
        self.p = self.me // 4

    def sem(self, e):
        return self.r.xcs.at[e], self.r.xcr.at[e]

    def seams(self):
        m = self.me % 16
        seam = (m == 5) | (m == 10)
        p0 = 3 * (self.me // 16) + jnp.where(m > 10, 2, jnp.where(m > 5, 1, 0))
        return seam, p0

    def reshard(self):
        r, a, me = self.r, self.a, self.me
        s0, r0 = self.sem(0)
        s1, r1 = self.sem(1)
        s2, r2 = self.sem(2)
        r.pup[...] = jnp.zeros((32, 24, 128), BF16)
        up = a.cup[...].astype(F32)
        for t in range(32):
            r.pup[t, :, 0:96] = up[:, 96 * t : 96 * t + 96].astype(BF16)
        loop(32, lambda t: send_to(me, t, r.pup.at[t], r.xup.at[me], s0, r0))

        def to_pair(p):
            for j in range(3):
                part = pl.ds(pl.multiple_of(D * j + 128 * p, 128), 128)
                send_to(me, pair_seg(p), a.cqkv.at[:, part], r.xqkv.at[me, j], s1, r1)
            first = pair_first(p)

            @pl.when((me >= first) & (me < first + 6))
            def _():
                send_to(me, pair_seg(p), a.cout, r.xout.at[me - first], s2, r2)

        loop(6, to_pair)
        r.wdn[0:96, :] = a.cdown[...]
        r.wdn[96:128, :] = jnp.zeros((32, D), BF16)

    def reshard_end(self):
        r = self.r
        take(r.xup, r.xcr.at[0])
        self.reshard_sent()
        r.wup[...] = r.xup[...].astype(F32).reshape(D, 128).astype(BF16)

        @pl.when(self.is_pair)
        def _():
            take(r.xqkv, r.xcr.at[1])
            for j in range(3):
                r.wqkv[:, 128 * j : 128 * (j + 1)] = r.xqkv[:, j].astype(F32).reshape(D, 128).astype(BF16)
            take(r.xout, r.xcr.at[2])
            r.wout_f[...] = r.xout[...].astype(F32).reshape(144, D)
            off = pl.multiple_of(8 * (self.p % 3), 8)
            r.wout[...] = r.wout_f[pl.ds(off, 128), :].astype(BF16)

    def reshard_sent(self):
        r, me = self.r, self.me
        take(r.xup.at[pl.ds(0, 31)], r.xcs.at[0])

        @pl.when(self.is_pair)
        def _():
            take(r.xqkv.at[pl.ds(0, 5)], r.xcs.at[1])

        @pl.when(jnp.logical_not(self.is_pair))
        def _():
            take(r.xqkv.at[pl.ds(0, 6)], r.xcs.at[1])

        seam, p0 = self.seams()
        hits = jnp.where(me == pair_seg(p0), 1, 0) + jnp.where(seam & (me == pair_seg(p0 + 1)), 1, 0)
        count = jnp.where(seam, 2, 1) - hits
        for n in (1, 2):

            @pl.when(count == n)
            def _():
                take(r.xout.at[pl.ds(0, n)], r.xcs.at[2])

    def start(self, z0, dy0):
        r, a, me = self.r, self.a, self.me
        row = lax.broadcasted_iota(jnp.int32, (8, 512), 0)
        lane = lax.broadcasted_iota(jnp.int32, (8, 512), 1)
        _, place = slot_layout(a.doc, (8, 512), jnp.minimum(me * 3 + row, 95))
        table = a.smg[...].astype(F32).reshape(512, 256)[:, 128:256].astype(BF16)
        parts = []
        for i in range(6):
            hot = (lane == (place // 2) * 16 + (place % 2) * 6 + i) & (row < 3)
            parts.append(dot(hot.astype(BF16), table))
        cross_in = z0 + jnp.concatenate(parts, axis=1)
        rowd = lax.broadcasted_iota(jnp.int32, (8, D), 0)
        both = jnp.where(rowd < 3, cross_in, pltpu.roll(dy0, 3, 0))
        r.msg[...] = jnp.where(rowd < 6, both, 0.0).astype(BF16)
        ss, rs = self.sem(3)
        loop(6, lambda p: send_to(me, pair_seg(p), r.msg, r.x1.at[me], ss, rs))
        loop(12, lambda k: send_to(me, owner_seg(k), r.msg, r.x1.at[me], ss, rs))

    def pick(self, n, first, base):
        row = lax.broadcasted_iota(jnp.int32, (n, 256), 0) + first
        lane = lax.broadcasted_iota(jnp.int32, (n, 256), 1)
        return (lane == (row // 3) * 8 + row % 3 + base).astype(BF16)

    def attention(self):
        r, a, me = self.r, self.a, self.me
        ss, rs = self.sem(4)

        @pl.when(self.is_pair)
        def _():
            take(r.x1, r.xcr.at[3])
            msgs = flat8(r.x1[...]).astype(BF16)
            xall = dot(self.pick(96, 0, 0), msgs).astype(BF16)
            r.xall[...] = xall
            part = col(self.p, 128)
            joined = dot(xall, r.wqkv[...])
            q = (joined[:, 0:128] + a.cb[0:1, part]).astype(BF16)
            k = joined[:, 128:256].astype(BF16)
            v = (joined[:, 256:384] + a.cb[1:2, part]).astype(BF16)
            r.q[0], r.q[1], r.q[2] = q, k, v
            line = lax.broadcasted_iota(jnp.int32, (192, 96), 0)
            doc_r, _ = slot_layout(a.doc, (192, 96), jnp.where(line < 96, line, line - 96))
            doc_c, _ = slot_layout(a.doc, (192, 96), lax.broadcasted_iota(jnp.int32, (192, 96), 1))
            w = softmax(jnp.where(doc_r == doc_c, dot_bt(two_heads(q), k) * 0.125, -1e30))
            r.af[...] = w
            o = side_by_side(dot(w.astype(BF16), v)).astype(BF16)
            r.o[...] = o
            r.p2[...] = rows8(dot(o, r.wout[...])).astype(BF16)
            loop(12, lambda k: send_to(me, owner_seg(k), r.p2.at[k], r.g2.at[self.p], ss, rs))

    def first_norm(self):
        r, a, me = self.r, self.a, self.me
        ss, rs = self.sem(5)

        @pl.when(self.is_owner)
        def _():
            take(r.x1, r.xcr.at[3])
            msgs = flat8(r.x1[...]).astype(BF16)
            x = dot(self.pick(8, 8 * self.k, 0), msgs)
            r.own[1] = dot(self.pick(8, 8 * self.k, 3), msgs)
            take(r.g2, r.xcr.at[4])
            total = jnp.sum(r.g2[...].astype(F32), axis=0)
            n, rstd = norm(x + (total + a.cb[2:3, :]))
            r.own[2] = n
            r.xrst[...] = jnp.broadcast_to(rstd, (8, 128))
            r.p3[...] = (n * a.cb[6:7, :] + a.cb[3:4, :]).astype(BF16)
            loop(32, lambda t: send_to(me, t, r.p3, r.g3.at[self.k], ss, rs))

    def mlp(self):
        r, a, me = self.r, self.a, self.me
        ss, rs = self.sem(6)
        take(r.g3, r.xcr.at[5])
        f = flat8(r.g3[...]).astype(BF16)
        r.fall[...] = f
        g, gp = gelu_both(dot(f, r.wup[...]) + a.cub[0:1, :])
        r.gp[...] = gp
        g = g.astype(BF16)
        r.gact[...] = g
        r.p4[...] = rows8(dot(g, r.wdn[...])).astype(BF16)
        loop(12, lambda k: send_to(me, owner_seg(k), r.p4.at[k], r.g46.at[me], ss, rs))

    def second_norm(self):
        r, a, me = self.r, self.a, self.me
        ss, rs = self.sem(7)

        @pl.when(self.is_owner)
        def _():
            take(r.g46.at[pl.ds(0, 32)], r.xcr.at[6])
            total = jnp.sum(r.g46[0:32].astype(F32), axis=0)
            n, rstd = norm(r.p3[...].astype(F32) + (total + a.cb[4:5, :]))
            y = n * a.cb[7:8, :] + a.cb[5:6, :]
            dr2 = norm_back(r.own[1], n, rstd, a.cb[7:8, :])
            r.own[3] = n
            r.own[4] = dr2
            r.p5[0] = dr2.astype(BF16)
            r.p5[1] = y.astype(BF16)
            loop(32, lambda t: send_to(me, t, r.p5.at[0], r.g5.at[self.k], ss, rs))
            self.to_slots(lambda t, i: send_to(me, t, r.p5.at[1], r.g5y.at[i], r.c7, r.y_r))

    def mlp_back(self):
        r, me = self.r, self.me
        ss, rs = self.sem(8)
        take(r.g5, r.xcr.at[7])
        dd = flat8(r.g5[...]).astype(BF16)
        r.xdd[...] = dd
        du = (dot_bt(dd, r.wdn[...]) * r.gp[...]).astype(BF16)
        r.du[...] = du
        r.p6[...] = rows8(dot_bt(du, r.wup[...])).astype(BF16)
        loop(12, lambda k: send_to(me, owner_seg(k), r.p6.at[k], r.g46.at[32 + me], ss, rs))

    def window(self, seg):
        return jnp.minimum((3 * seg) // 8, 10)

    def first_norm_back(self):
        r, a, me = self.r, self.a, self.me
        ss, rs = self.sem(9)
        fr = r.xcr.at[10]

        @pl.when(self.is_owner)
        def _():
            take(r.g46.at[pl.ds(32, 32)], r.xcr.at[8])
            df = jnp.sum(r.g46[32:64].astype(F32), axis=0) + r.own[4]
            r.own[5] = df
            dr1 = norm_back(df, r.own[2], r.xrst[:, 0:1], a.cb[6:7, :])
            r.p7[...] = dr1.astype(BF16)
            loop(6, lambda p: send_to(me, pair_seg(p), r.p7, r.g7.at[self.k], ss, rs))
            r.p7f[...] = dr1

            self.to_slots(lambda t, i: send_to(me, t, r.p7f, r.g7f.at[i], r.c7, fr))

    def to_slots(self, fn):
        def one(t):
            w = self.window(t)

            @pl.when((w == self.k) | (w + 1 == self.k))
            def _():
                fn(t, self.k - w)

        loop(32, one)

    def attention_back(self):
        r, me = self.r, self.me
        ss, rs = self.sem(11)

        @pl.when(self.is_pair)
        def _():
            take(r.g7, r.xcr.at[9])
            de = flat8(r.g7[...]).astype(BF16)
            r.xde[...] = de
            do = dot_bt(de, r.wout[...]).astype(BF16)
            q, k, v = r.q[0], r.q[1], r.q[2]
            do2, w = two_heads(do), r.af[...]
            ds = softmax_back(w, dot_bt(do2, v)).astype(BF16)
            r.dq[:, 0:128] = (side_by_side(dot(ds, k)) * 0.125).astype(BF16)
            r.dq[:, 128:256] = (dot_at(ds, two_heads(q)) * 0.125).astype(BF16)
            r.dq[:, 256:384] = dot_at(w.astype(BF16), do2).astype(BF16)
            dx = dot_bt(r.dq[...], r.wqkv[...]).astype(BF16)
            line = lax.broadcasted_iota(jnp.int32, (256, 96), 0)
            place = (line // 8) * 3 + line % 8 - lax.broadcasted_iota(jnp.int32, (256, 96), 1)
            left = ((line % 8 < 3) & (place == 0)).astype(BF16)
            right = ((line % 8 >= 3) & (line % 8 < 6) & (place == 3)).astype(BF16)
            r.p8[...] = rows8(dot(left, dx[:, 0:W]) + dot(right, dx[:, W:D])).astype(BF16)
            loop(32, lambda t: send_to(me, t, r.p8.at[t], r.g8.at[self.p], ss, rs))

    def finish(self):
        r = self.r
        take(r.g7f, r.xcr.at[10])
        take(r.g8, r.xcr.at[11])
        total = jnp.sum(r.g8[...].astype(F32), axis=0)
        shift = 3 * self.me - 8 * self.window(self.me)
        rest = pltpu.roll(r.g7f[...].reshape(16, D), 16 - shift, 0)[0:8]
        return rest + jnp.concatenate([total, pltpu.roll(total, 5, 0)], axis=1)

    def output_rows(self):
        take(self.r.g5y, self.r.y_r)
        y = self.r.g5y[...].astype(F32).reshape(16, D)
        return pltpu.roll(y, 16 - (3 * self.me - 8 * self.window(self.me)), 0)[0:8]

    def grads(self):
        r, a = self.r, self.a
        a.pu[...] = dot_at(r.fall[...], r.du[...]).reshape(32, 24, 128).astype(BF16)
        a.gdn[...] = dot_at(r.gact[...], r.xdd[...])[0:96].astype(BF16)

        @pl.when(self.is_pair)
        def _():
            for j in range(3):
                part = dot_at(r.xall[...], r.dq[:, 128 * j : 128 * (j + 1)])
                a.pq[:, j] = part.reshape(32, 24, 128).astype(BF16)
            r.po_f[...] = jnp.zeros((144, D), F32)
            off = pl.multiple_of(8 * (self.p % 3), 8)
            r.po_f[pl.ds(off, 128), :] = dot_at(r.o[...], r.xde[...])
            a.po[...] = r.po_f[...].reshape(6, 24, D).astype(BF16)

        a.small[...] = jnp.zeros((8, D), F32)

        @pl.when(self.is_owner)
        def _():
            dr1, df, dr2, dy = r.p7[...].astype(F32), r.own[5], r.own[4], r.own[1]
            dd = r.p5[0].astype(F32)
            for row, v in ((2, dr1), (3, df), (4, dd), (5, dy), (6, df * r.own[2]), (7, dy * r.own[3])):
                a.small[row : row + 1, :] = sum0(v)

        @pl.when(self.is_pair)
        def _():
            part = col(self.p, 128)
            a.small[0:1, part] = sum0(r.dq[:, 0:128].astype(F32))
            a.small[1:2, part] = sum0(r.dq[:, 256:384].astype(F32))

        a.dc[...] = jnp.broadcast_to(sum0(r.du[...].astype(F32)), (8, 128))

    def drain(self):
        r, me = self.r, self.me
        cs = r.xcs

        def some(e, ref, count, fewer):
            @pl.when(fewer)
            def _():
                take(ref.at[pl.ds(0, count - 1)], cs.at[e])

            @pl.when(jnp.logical_not(fewer))
            def _():
                take(ref.at[pl.ds(0, count)], cs.at[e])

        some(3, r.g46, 18, self.is_pair | self.is_owner)
        some(6, r.g46, 12, self.is_owner)
        some(8, r.g46, 12, self.is_owner)

        @pl.when(self.is_pair)
        def _():
            take(r.g46.at[pl.ds(0, 12)], cs.at[4])
            take(r.p8.at[pl.ds(0, 31)], cs.at[11])

        @pl.when(self.is_owner)
        def _():
            take(r.g46.at[pl.ds(0, 31)], cs.at[5])
            take(r.g46.at[pl.ds(0, 31)], cs.at[7])
            take(r.g46.at[pl.ds(0, 6)], cs.at[9])

            count = jnp.int32(0)
            for t in range(32):
                w = min(3 * t // 8, 10)
                count += jnp.where(((self.k == w) | (self.k == w + 1)) & (me != t), 1, 0)
            for n in range(1, 10):

                @pl.when(count == n)
                def _():
                    take(r.g46.at[pl.ds(0, 3 * n)], r.c7)


class CrossGrads(Cross):
    def scatter(self):
        r, a, me = self.r, self.a, self.me
        loop(32, lambda t: send_to(me, t, a.pu.at[t], r.gup.at[me], r.ks.at[0], r.kr.at[0]))

        @pl.when(self.is_pair)
        def _():
            loop(32, lambda t: send_to(me, t, a.pq.at[t], r.gqkv.at[self.p], r.ks.at[1], r.kr.at[1]))
            loop(
                6,
                lambda i: send_to(
                    me, pair_first(self.p) + i, a.po.at[i], r.go.at[self.p % 2], r.ks.at[2], r.kr.at[2]
                ),
            )

    def planes(self, red):
        r, a, me, z = self.r, self.a, self.me, red.z
        take(r.gup, r.kr.at[0])
        take(r.gqkv, r.kr.at[1])
        for i in range(6):
            for j in range(3):
                r.c0[i, :, 128 * j : 128 * (j + 1)] = r.gqkv[i, j]
        seam, p0 = self.seams()

        @pl.when(seam)
        def _():
            take(r.go, r.kr.at[2])
            both = (r.go[0].astype(F32) + r.go[1].astype(F32)).astype(BF16)
            for i in range(2):
                r.c0[6 + i] = both[:, W * i : W * (i + 1)]

        @pl.when(jnp.logical_not(seam))
        def _():
            take(r.go.at[0], r.kr.at[2])
            for i in range(2):
                r.c0[6 + i] = r.go[p0 % 2, :, W * i : W * (i + 1)]

        gdn = a.gdn[...].astype(F32).reshape(4, 24, D)
        for i in range(2):
            for n in range(4):
                r.c0[8 + 4 * i + n] = gdn[n, :, W * i : W * (i + 1)].astype(BF16)

        def out(zz):
            zcopy(r.c0.at[pl.ds(2 * zz, 2)], r.cr.at[z], r.xs.at[1], r.xr.at[1], zz, me).start()
            zcopy(r.gup.at[pl.ds(4 * zz, 4)], r.ur.at[z], r.xs.at[2], r.xr.at[2], zz, me).start()

        red.peers(out)
        pltpu.make_async_copy(r.c0.at[pl.ds(2 * z, 2)], r.cr.at[z], r.xr.at[1]).start()
        pltpu.make_async_copy(r.gup.at[pl.ds(4 * z, 4)], r.ur.at[z], r.xr.at[2]).start()

    def planes_sum(self, red):
        r, me, z = self.r, self.me, red.z
        take(r.cr, r.xr.at[1])
        r.cs[...] = jnp.sum(r.cr[...].astype(F32), axis=0).astype(BF16)
        take(r.ur, r.xr.at[2])
        r.us[...] = jnp.sum(r.ur[...].astype(F32), axis=0).astype(BF16)

        def back(zz):
            zcopy(r.cs, r.cf.at[z], r.xs.at[4], r.xr.at[4], zz, me).start()
            zcopy(r.us, r.uf.at[z], r.xs.at[5], r.xr.at[5], zz, me).start()

        red.peers(back)
        pltpu.make_async_copy(r.cs, r.cf.at[z], r.xr.at[4]).start()
        pltpu.make_async_copy(r.us, r.uf.at[z], r.xr.at[5]).start()

    def end(self):
        r, me = self.r, self.me
        take(r.cf, r.xr.at[4])
        take(r.uf, r.xr.at[5])
        take(r.gup.at[pl.ds(0, 31)], r.ks.at[0])

        @pl.when(self.is_pair)
        def _():
            take(r.pq.at[pl.ds(0, 31)], r.ks.at[1])
            first = pair_first(self.p)
            inside = (me >= first) & (me < first + 6)

            @pl.when(inside)
            def _():
                take(r.po.at[pl.ds(0, 5)], r.ks.at[2])

            @pl.when(jnp.logical_not(inside))
            def _():
                take(r.po, r.ks.at[2])

        for n, buf in ((1, r.cr), (2, r.ur), (4, r.cr), (5, r.ur)):
            take(buf.at[pl.ds(0, 7)], r.xs.at[n])


class Plane:
    def __init__(self):
        self.me = lax.axis_index("seg")
        self.x, self.y, self.c = self.me // 8, (self.me // 2) % 4, self.me % 2
        self.other = self.me + 1 - 2 * self.c

    def seg(self, on_x, step):
        if on_x:
            return (((self.x + step) % 4) * 4 + self.y) * 2 + self.c
        return (self.x * 4 + (self.y + step) % 4) * 2 + self.c

    def ring(self, part, which, step):
        return self.seg((part == 0) == (which == 1), step)

    def pos(self, part, which):
        return self.x if (part == 0) == (which == 1) else self.y

    def by_part(self, k, fn):
        for part in range(2):
            pl.when(k % 2 == part)(functools.partial(fn, part))

    @staticmethod
    def ahead(k):
        return 1 + 2 * ((k // 2) % 2)


class Gather(Plane):
    def __init__(self, r):
        super().__init__()
        self.r = r
        self.z = lax.axis_index("grp")
        self.mine, self.others = 4 + 2 * (self.z % 2), 6 - 2 * (self.z % 2)

    def unit(self, i):
        return jnp.where(i < 3, i, jnp.where(i < 5, self.mine + i - 3, jnp.where(i == 5, 3, i + 2)))

    def to_plane(self, k, row):
        @pl.when((k >= 4) & (k < 8))
        def _():
            z = (self.z + 1 + 6 * (k % 2)) % 8
            zcopy(row, row, self.r.up_s, self.r.up_r.at[k - 4], z, self.me).start()

    def from_planes(self):
        r = self.r
        for j in range(2):
            k = self.others + j
            unit = r.ws.at[self.c, k]
            take(unit, r.up_r.at[k - 4])
            rcopy(unit, unit, r.s3, r.r3.at[k], self.other).start()

    def v1(self, k, part, off):
        mine = self.r.ws.at[self.c, k]
        return mine.at[(self.x + off) % 4, self.y] if part == 0 else mine.at[self.x, (self.y + off) % 4]

    def v2(self, k, part, off):
        mine = self.r.ws.at[self.c, k]
        return mine.at[:, (self.y + off) % 4] if part == 0 else mine.at[(self.x + off) % 4]

    def first(self, k):
        r = self.r

        def go(part):
            own = self.v1(k, part, 0)
            src = r.stage.at[k]
            pltpu.make_async_copy(src, own, r.own_sem.at[k]).start()
            rcopy(src, own, r.s1, r.r1.at[k, 0], self.ring(part, 1, 1)).start()
            rcopy(src, own, r.s1, r.r1.at[k, 1], self.ring(part, 1, 3)).start()

        @pl.when((k < 4) | (k >= 8) | (k // 2 == self.mine // 2))
        def _():
            self.by_part(k, go)

    def first_on(self, k):
        r, ahead = self.r, self.ahead(k)

        def go(part):
            block = self.v1(k, part, 4 - ahead)
            take(block, r.r1.at[k, ahead // 2])
            rcopy(block, block, r.s1, r.r1.at[k, 1 - ahead // 2], self.ring(part, 1, ahead)).start()

        self.by_part(k, go)

    def second(self, k):
        r, ahead = self.r, self.ahead(k)

        def go(part):
            take(r.ws.at[0, 0, 0, pl.ds(0, 2)], r.r1.at[k, 1 - ahead // 2])
            own = self.v1(k, part, 0)
            take(own, r.own_sem.at[k])
            row = self.v2(k, part, 0)
            rcopy(row, row, r.s2, r.r2.at[k, 0], self.ring(part, 2, 1)).start()
            rcopy(row, row, r.s2, r.r2.at[k, 1], self.ring(part, 2, 3)).start()
            rcopy(row, row, r.s3, r.r3.at[k], self.other).start()
            self.to_plane(k, row)

        self.by_part(k, go)

    def second_on(self, k):
        r, ahead = self.r, self.ahead(k)

        def go(part):
            row = self.v2(k, part, 4 - ahead)
            take(row, r.r2.at[k, ahead // 2])
            rcopy(row, row, r.s2, r.r2.at[k, 2], self.ring(part, 2, ahead)).start()
            rcopy(row, row, r.s3, r.r3.at[k], self.other).start()
            self.to_plane(k, row)
            row = self.v2(k, part, ahead)
            take(row, r.r2.at[k, 1 - ahead // 2])
            rcopy(row, row, r.s3, r.r3.at[k], self.other).start()
            self.to_plane(k, row)

        self.by_part(k, go)

    def last(self, k):
        r = self.r

        def go(part):
            row = self.v2(k, part, 2)
            take(row, r.r2.at[k, 2])
            rcopy(row, row, r.s3, r.r3.at[k], self.other).start()
            self.to_plane(k, row)

        self.by_part(k, go)

    def arrived(self, k):
        r = self.r
        take(r.ws.at[1 - self.c, k], r.r3.at[k])

    def drain(self):
        r = self.r

        take(r.ws.at[0, pl.ds(0, 10), 0, pl.ds(0, 3)], r.s1)
        take(r.ws.at[0, pl.ds(0, 10), pl.ds(0, 3)], r.s2)
        take(r.ws.at[0, pl.ds(0, 2)], r.up_s)
        take(r.ws.at[0], r.s3)


class Reduce(Plane):
    def __init__(self, r, pieces):
        super().__init__()
        self.r, self.pieces = r, pieces
        self.z = lax.axis_index("grp")

    def peers(self, fn):
        loop(7, lambda i: fn((self.z + 1 + i) % 8))

    def to_sibling(self, k):
        r = self.r
        rcopy(r.gb.at[1, k], r.r0.at[k], r.ms.at[0], r.mr.at[k, 0], self.other).start()

    def msg(self, k, part, q):
        return self.r.gb.at[0, k, :, q] if part == 0 else self.r.gb.at[0, k, q]

    def step_a(self, k):
        r, ahead = self.r, self.ahead(k)
        take(r.r0.at[k], r.mr.at[k, 0])

        def add(i):
            px, py = i // 4, i % 4
            r.gb[0, k, px, py] = (r.gb[0, k, px, py].astype(F32) + r.r0[k, px, py].astype(F32)).astype(BF16)

        loop(16, add)

        def go(part):
            q = self.pos(part, 2)
            far, back = self.msg(k, part, (q + 2) % 4), self.msg(k, part, (q + 4 - ahead) % 4)
            rcopy(far, r.f2.at[k], r.ms.at[1], r.mr.at[k, 1], self.ring(part, 2, ahead)).start()
            rcopy(back, r.b2.at[k], r.ms.at[1], r.mr.at[k, 2], self.ring(part, 2, 4 - ahead)).start()

        self.by_part(k, go)

    def step_b(self, k):
        r, ahead = self.r, self.ahead(k)
        take(r.f2.at[k], r.mr.at[k, 1])

        def go(part):
            block = self.msg(k, part, (self.pos(part, 2) + ahead) % 4)

            def add(i):
                block[i] = (block[i].astype(F32) + r.f2[k, i].astype(F32)).astype(BF16)

            loop(4, add)
            rcopy(block, r.a2.at[k], r.ms.at[1], r.mr.at[k, 2], self.ring(part, 2, ahead)).start()

        self.by_part(k, go)

    def step_c(self, k):
        r = self.r
        take(r.r0.at[0, pl.ds(0, 2)], r.mr.at[k, 2])

        def go(part):
            block = self.msg(k, part, self.pos(part, 2))

            def add(i):
                r.t1[k, i] = (block[i].astype(F32) + r.a2[k, i].astype(F32) + r.b2[k, i].astype(F32)).astype(BF16)

            loop(4, add)
            q = self.pos(part, 1)
            for step, dst in ((1, r.a1), (2, r.f1), (3, r.b1)):
                block = r.t1.at[k, (q + step) % 4]
                rcopy(block, dst.at[k], r.ms.at[2], r.mr.at[k, 3], self.ring(part, 1, step)).start()

        self.by_part(k, go)

    def step_d(self, k):
        r = self.r
        take(r.r0.at[0, 0, pl.ds(0, 3)], r.mr.at[k, 3])

        def go(part):
            t = r.t1[k, self.pos(part, 1)].astype(F32) + r.f1[k].astype(F32)
            t += r.a1[k].astype(F32) + r.b1[k].astype(F32)
            self.pieces[k // 4, pl.ds(2 * (k % 4), 2)] = t.reshape(2, 24, W).astype(BF16)

        self.by_part(k, go)

    def sent(self, slots):
        r = self.r
        some = pl.ds(0, slots * 3 // 4)
        take(r.r0, r.ms.at[0])
        take(r.r0.at[some], r.ms.at[1])
        take(r.r0.at[some, 0], r.ms.at[2])

    def z_send(self, g):
        r, z, me = self.r, self.z, self.me
        self.peers(lambda zz: zcopy(r.zp.at[g, zz], r.zr.at[g, z], r.zss.at[g, 0], r.zsr.at[g, 0], zz, me).start())
        pltpu.make_async_copy(r.zp.at[g, z], r.zr.at[g, z], r.zsr.at[g, 0]).start()

    def z_sum(self, g):
        r, z, me, c = self.r, self.z, self.me, self.c
        take(r.zr.at[g], r.zsr.at[g, 0])
        r.zs[g] = jnp.sum(r.zr[g].astype(F32), axis=0).astype(BF16)
        m, h = z // 2, z % 2

        def out(dst, sem, seg):
            def one(zz):
                here = (zz == z) & (seg == me)

                @pl.when(here)
                def _():
                    pltpu.make_async_copy(r.zs.at[g], dst, sem).start()

                @pl.when(jnp.logical_not(here))
                def _():
                    zcopy(r.zs.at[g], dst, r.zss.at[g, 1], sem, zz, seg).start()

            loop(8, one)

        if g == 0:
            out(r.fd.at[z], r.zsr.at[0, 1], me)
        elif g == 1:
            out(r.fa.at[8 + 2 * m + c], r.zsr.at[1, 1], me - c + h)
        else:
            out(r.fa.at[2 * ((m + 3) % 4) + c], r.zsr.at[2, 1], me - c + h)

    def z_sent(self):
        r, z, c = self.r, self.z, self.c
        for g in range(3):
            take(r.zr.at[g, pl.ds(0, 7)], r.zss.at[g, 0])
            stays = (z % 2 == c) if g > 0 else (z >= 0)

            @pl.when(stays)
            def _():
                take(r.zr.at[g, pl.ds(0, 7)], r.zss.at[g, 1])

            @pl.when(jnp.logical_not(stays))
            def _():
                take(r.zr.at[g], r.zss.at[g, 1])


F_IN = list(dict(tok=0, cot=0, qkv=0, out=0, up=0, down=0, bias=0, upbias=0, gains=0, cqkv=0, cout=0, cup=0, cdown=0, cbias=0, cupbias=0, cgains=0, pos=0, doc=0))
F_OUT = dict(
    lo_h=((ROWS, D), BF16),
    tg_h=((ROWS, D), F32),
    fa=((16, 24, W), BF16),
    fd=((8, 24, W), BF16),
    cf=((8, 2, 24, W), BF16),
    uf=((8, 4, 24, 128), BF16),
    osm=((12, 8, D), BF16),
)


def reduce_scratch(n):
    unit, line = (4, 4, 48, W), (n, 4, 48, W)
    return dict(
        gb=VM((2, n) + unit, BF16),
        r0=VM((n,) + unit, BF16),
        f2=VM(line, BF16),
        a2=VM(line, BF16),
        b2=VM(line, BF16),
        t1=VM(line, BF16),
        f1=VM((n, 48, W), BF16),
        a1=VM((n, 48, W), BF16),
        b1=VM((n, 48, W), BF16),
        mr=DMA((n, 4)),
        ms=DMA((3,)),
    )


F_SCR = dict(
    ws=VM((2, 12, 4, 4, 48, W), BF16),
    stage=VM((12, 48, W), BF16),
    sibq=VM((24, 3 * D), BF16),
    sibo=VM((24, D), BF16),
    sibu=VM((24, FF), BF16),
    smf=VM((16, 256), F32),
    sm=VM((16, 256), BF16),
    smg=VM((16, 2, 16, 256), BF16),
    both=VM((16, D), F32),
    lb=VM((8, D), F32),
    lub=VM((1, FF), F32),
    cub=VM((8, 128), F32),
    cb=VM((8, D), F32),
    qkvv=VM((3, ROWS, D), BF16),
    mix=VM((ROWS, D), BF16),
    aw=VM((3, 6, 256, 128), BF16),
    n1=VM((ROWS, D), F32),
    f=VM((ROWS, D), BF16),
    g=VM((ROWS, FF), BF16),
    gpl=VM((ROWS, FF), BF16),
    rst=VM((ROWS, 128), F32),
    dd=VM((ROWS, D), BF16),
    hf=VM((8, D), BF16),
    hg=VM((8, FF), BF16),
    hgp=VM((8, FF), F32),
    hn=VM((2, 8, D), F32),
    hrst=VM((2, 8, 128), F32),
    hgs=VM((32, 8, 128), BF16),
    hfp=VM((8, W), BF16),
    hdp=VM((8, W), BF16),
    hdd=VM((8, D), BF16),
    hdf=VM((8, D), F32),
    hs=DMA((3,)),
    hr=DMA((3,)),
    sib_s=DMA((3,)),
    sib_r=DMA((3,)),
    sm_s=DMA((2,)),
    sm_r=DMA((2,)),
    own_sem=DMA((12,)),
    s1=DMA,
    r1=DMA((12, 2)),
    s2=DMA,
    r2=DMA((12, 3)),
    s3=DMA,
    r3=DMA((12,)),
    up_s=DMA,
    up_r=DMA((4,)),
    lo=VM((ROWS, D), BF16),
    tg=VM((ROWS, D), F32),
    done=DMA((2,)),
    sloc=VM((8, D), F32),
    dcl=VM((1, FF), F32),
    dx=VM((8, D), F32),
    hfd=VM((2, 16, 2, 8, W), BF16),
    hgr=VM((32, 8, 128), BF16),
    gdn=VM((96, D), BF16),
    small=VM((8, D), F32),
    dc=VM((8, 128), F32),
    gup=VM((32, 24, 128), BF16),
    gqkv=VM((6, 3, 24, 128), BF16),
    go=VM((2, 24, D), BF16),
    cu=VM((2, 16, 24, 128), BF16),
    zc=VM((24, W), F32),
    zp=VM((3, 8, 24, W), BF16),
    zr=VM((3, 8, 24, W), BF16),
    zs=VM((3, 24, W), BF16),
    c0=VM((16, 24, W), BF16),
    cr=VM((8, 2, 24, W), BF16),
    cs=VM((2, 24, W), BF16),
    ur=VM((8, 4, 24, 128), BF16),
    us=VM((4, 24, 128), BF16),
    sf=VM((96, D), F32),
    s0=VM((12, 8, D), BF16),
    sm1=VM((8, D), BF16),
    sm2=VM((8, D), BF16),
    xr=DMA((8,)),
    xs=DMA((8,)),
    zsr=DMA((3, 2)),
    zss=DMA((3, 2)),
    ks=DMA((4,)),
    kr=DMA((4,)),
    free=pltpu.SemaphoreType.REGULAR,
    mr2=DMA((4, 4)),
    ms2=DMA((3,)),
    **reduce_scratch(8),
    **{("x" + n if n in ("rst", "dd", "de", "cs", "cr") else n): v for n, v in CROSS.items()},
)


def layer_kernel(*refs):
    r = fields(F_IN + list(F_OUT) + list(F_SCR), refs)
    ring = Gather(r)
    cross = CrossGrads(r, r)
    again = types.SimpleNamespace(
        gb=r.ws.at[:, pl.ds(4, 4)],
        r0=r.ws.at[0, pl.ds(8, 4)],
        f2=r.ws.at[1, 8],
        a2=r.ws.at[1, 9],
        b2=r.ws.at[1, 10],
        t1=r.ws.at[1, 11],
        f1=r.stage.at[pl.ds(0, 4)],
        a1=r.stage.at[pl.ds(4, 4)],
        b1=r.stage.at[pl.ds(8, 4)],
        mr=r.mr2,
        ms=r.ms2,
    )
    red, red2 = Reduce(r, r.zp.at[pl.ds(0, 2)]), Reduce(again, r.zp.at[pl.ds(2, 1)])
    me, c, z = ring.me, ring.c, red.z
    is_owner = (c == 0) & (me < 24)
    r.n2, r.de, r.do = r.tg, r.f, r.dd
    r.pcu, r.po_f, r.pu, r.pq, r.po = r.xup, r.wout_f, r.pup, r.xqkv, r.xout
    r.sz, r.sg = r.g46.at[pl.ds(0, 32)], r.g46.at[pl.ds(32, 32)]
    bar = pltpu.get_barrier_semaphore()
    loop(31, lambda i: pl.semaphore_signal(bar, inc=1, device_id={"seg": (me + 1 + i) % 32}, device_id_type=MESH))

    def greet(zz):
        for seg in (me, red.other):
            pl.semaphore_signal(bar, inc=1, device_id={"grp": zz, "seg": seg}, device_id_type=MESH)

    red.peers(greet)
    r.smf[...] = jnp.zeros((16, 256), F32)
    r.smf[0:6, 0:24] = r.bias[...].astype(F32)
    r.smf[6:8, 0:24] = r.gains[...].astype(F32)
    r.smf[8:14, 0:24] = r.cbias[...].astype(F32)
    r.smf[14:16, 0:24] = r.cgains[...].astype(F32)
    r.smf[0:1, 32:128] = r.upbias[...].astype(F32)
    table = r.pos[...].astype(F32)
    for t in range(2):
        for i in range(6):
            r.smf[6 * t + i : 6 * t + i + 1, 128:256] = table[t : t + 1, 128 * i : 128 * (i + 1)]
    r.sm[...] = r.smf[...].astype(BF16)
    r.cub[...] = jnp.zeros((8, 128), F32)
    r.cub[0:1, 0:96] = r.cupbias[...].astype(F32)
    pl.semaphore_wait(bar, 45)

    swaps = [(r.qkv, r.sibq), (r.out, r.sibo), (r.up, r.sibu)]
    for i, (src, dst) in enumerate(swaps):
        rcopy(src, dst, r.sib_s.at[i], r.sib_r.at[i], ring.other).start()
    for j in range(4):
        r.stage[8 + j] = r.down[(j % 2) * 48 : (j % 2) * 48 + 48, (j // 2) * W : (j // 2 + 1) * W]

    def compose(k, src, sib, block):
        own = src[:, col(block)].astype(F32)
        oth = sib[:, col(block)].astype(F32)
        lo, hi = jnp.where(c == 0, own, oth), jnp.where(c == 0, oth, own)
        r.stage[k] = jnp.concatenate([lo, hi], axis=0).astype(BF16)
        ring.first(k)

    def arrive(i):
        take(swaps[i][1], r.sib_r.at[i])

    arrive(0)
    loop(3, lambda k: compose(k, r.qkv, r.sibq, 2 * k + c))
    arrive(1)
    compose(3, r.out, r.sibo, c)
    arrive(2)
    loop(8, lambda k: compose(k, r.up, r.sibu, 2 * (k - 4) + c), 4)
    loop(12, ring.first, 8)
    loop(16, lambda t: send_to(me, 2 * t + c, r.sm, r.smg.at[me // 2, c], r.sm_s.at[0], r.sm_r.at[0]))
    loop(10, lambda i: ring.first_on(ring.unit(i)))
    loop(6, lambda i: ring.second(ring.unit(i)))
    take(r.smg.at[:, 0], r.sm_r.at[0])
    rcopy(r.smg.at[:, c], r.smg.at[:, c], r.sm_s.at[1], r.sm_r.at[1], ring.other).start()

    def tick(i):
        ring.second_on(ring.unit(i))

        @pl.when(i < 4)
        def _():
            ring.second(ring.unit(i + 6))

        @pl.when(i >= 3)
        def _():
            ring.last(ring.unit(i - 3))

    def weight(cc, k):
        return r.ws[cc, k].reshape(D, W)

    loop(3, tick)
    take(r.smg.at[:, 0], r.sm_r.at[1])
    for t in range(32):
        block = r.smg[t // 2, t % 2].astype(F32)
        r.both[:, 24 * t : 24 * t + 24] = block[:, 0:24]
        r.lub[:, 96 * t : 96 * t + 96] = block[0:1, 32:128]
    r.lb[...] = r.both[0:8, :]
    r.cb[...] = r.both[8:16, :]
    tick(3)

    def project(k):
        tick(k)
        i = k - 4
        ring.arrived(i)
        shift = jnp.where(i == 0, r.lb[0:1, :], jnp.where(i == 2, r.lb[1:2, :], 0.0))
        for cc in range(2):
            part = slice(cc * W, (cc + 1) * W)
            r.qkvv[i, :, part] = (dot(r.tok[...], weight(cc, i)) + shift[:, part]).astype(BF16)

    loop(7, project, 4)
    cross.reshard()

    def attend(k):
        tick(k)
        s = k - 7
        rows = pl.ds(pl.multiple_of(s * 128, 128), 128)
        for p in range(6):
            part = slice(128 * p, 128 * (p + 1))
            w = softmax(dot_bt(two_heads(r.qkvv[0, rows, part]), r.qkvv[1, rows, part]) * 0.125).astype(BF16)
            r.aw[s, p] = w
            r.mix[rows, part] = side_by_side(dot(w, r.qkvv[2, rows, part])).astype(BF16)

    loop(10, attend, 7)
    ring.arrived(3)
    for cc in range(2):
        part = slice(cc * W, (cc + 1) * W)
        r.n1[:, part] = dot(r.mix[...], weight(cc, 3)) + (r.tok[:, part].astype(F32) + r.lb[2:3, part])
    row8 = lax.broadcasted_iota(jnp.int32, (8, D), 0)
    r.sloc[...] = jnp.zeros((8, D), F32)

    def heads(ref):
        out = jnp.zeros((8, D), F32)
        for s in range(3):
            top = ref[128 * s : 128 * s + 16, :].astype(F32)[0:1, :]
            out = jnp.where(row8 == s, top, out)
        return out

    def head_norm(i, value):
        n, rstd = norm(value)
        r.hn[i] = n
        r.hrst[i] = jnp.broadcast_to(rstd, (8, 128))
        return n

    hf = head_norm(0, heads(r.n1)) * r.lb[6:7, :] + r.lb[3:4, :]
    r.hf[...] = jnp.where(row8 < 3, hf, 0.0).astype(BF16)

    def head_up(i):
        ring.arrived(i)
        for cc in range(2):
            part = col(2 * (i - 4) + cc)
            g, gp = gelu_both(dot(r.hf[...], weight(cc, i)) + r.lub[0:1, part])
            keep = lax.broadcasted_iota(jnp.int32, (8, W), 0) < 3
            r.hg[:, part] = jnp.where(keep, g, 0.0).astype(BF16)
            r.hgp[:, part] = gp

    head_up(ring.mine)
    head_up(ring.mine + 1)
    ring.last(ring.unit(7))
    ring.from_planes()
    ring.last(ring.unit(8))
    ring.last(ring.unit(9))
    head_up(ring.others)
    head_up(ring.others + 1)

    def down_rows(x, kc):
        pieces = [r.ws[cc, 8 + 2 * kc + j, x, y] for y in range(4) for cc in range(2) for j in range(2)]
        return jnp.concatenate(pieces, axis=0)

    halves = []
    for kc in range(2):
        for j in range(2):
            ring.arrived(8 + 2 * kc + j)
        part = slice(kc * W, (kc + 1) * W)
        acc = r.hf[:, part].astype(F32) + r.lb[4:5, part]
        for x in range(4):
            acc += dot(r.hg[:, D * x : D * (x + 1)], down_rows(x, kc))
        halves.append(acc)
    z0 = head_norm(1, jnp.concatenate(halves, axis=1)) * r.lb[7:8, :] + r.lb[5:6, :]
    cross.reshard_end()
    cross.start(z0, heads(r.cot))

    def blocks(fn):
        loop(ROWS // 64, lambda i: fn(pl.ds(pl.multiple_of(i * 64, 64), 64)))

    def norm_one(rows):
        n, rstd = norm(r.n1[rows, :])
        r.n1[rows, :] = n
        r.rst[rows, :] = jnp.broadcast_to(rstd, (64, 128))
        r.f[rows, :] = (n * r.lb[6:7, :] + r.lb[3:4, :]).astype(BF16)

    def raise_up(i):
        def half(cc):
            part = col(2 * (i - 4) + cc)
            g, gp = gelu_both(dot(r.f[...], weight(cc, i)) + r.lub[0:1, part])
            r.g[:, part] = g.astype(BF16)
            r.gpl[:, part] = gp.astype(BF16)

        loop(2, half)

    def lower(kc):
        part = slice(kc * W, (kc + 1) * W)
        r.n2[:, part] = r.f[:, part].astype(F32) + r.lb[4:5, part]

        def quarter(x):
            r.n2[:, part] += dot(r.g[:, col(x, D)], down_rows(x, kc))

        loop(4, quarter)

    row64 = lax.broadcasted_iota(jnp.int32, (64, D), 0)

    def norm_two(i):
        rows = pl.ds(pl.multiple_of(i * 64, 64), 64)
        n, rstd = norm(r.n2[rows, :])
        r.lo[rows, :] = (n * r.lb[7:8, :] + r.lb[5:6, :]).astype(BF16)
        dy = jnp.where((row64 == 0) & (i % 2 == 0), 0.0, r.cot[rows, :].astype(F32))
        dr2 = norm_back(dy, n, rstd, r.lb[7:8, :])
        dd = dr2.astype(BF16)
        r.n2[rows, :] = dr2
        r.dd[rows, :] = dd
        r.sloc[5:6, :] += sum0(dy)
        r.sloc[7:8, :] += sum0(dy * n)
        r.sloc[4:5, :] += sum0(dd.astype(F32))

    def down_grad(b):
        v = dot_at(r.g[:, col(b)], r.dd[...]).astype(BF16).reshape(2, 2, 2, 48, D)
        for chip in range(2):
            for cc in range(2):
                for j in range(4):
                    v4 = v[chip, cc, j % 2, :, (j // 2) * W : (j // 2 + 1) * W]
                    r.gb[(cc + c) % 2, j, b // 2, 2 * (b % 2) + chip] = v4

    def down_block(b, kc):
        chips = [(b // 2, 2 * (b % 2) + chip) for chip in range(2)]
        pieces = [r.ws[cc, 8 + 2 * kc + j, x, y] for x, y in chips for cc in range(2) for j in range(2)]
        return jnp.concatenate(pieces, axis=0)

    def middle(b):
        part = col(b)
        dg = dot_bt(r.dd[:, 0:W], down_block(b, 0)) + dot_bt(r.dd[:, W:D], down_block(b, 1))
        du = (dg * r.gpl[:, part].astype(F32)).astype(BF16)
        r.dcl[:, part] = sum0(du.astype(F32))
        r.n2[...] += dot_bt(du, r.ws[b % 2, 4 + b // 2].reshape(D, W))
        r.gb[(b + c) % 2, 4 + b // 2] = dot_at(r.f[...], du).astype(BF16).reshape(4, 4, 48, W)

        @pl.when(b % 2 == 1)
        def _():
            red.to_sibling(4 + b // 2)

    def norm_one_back(rows):
        df, n = r.n2[rows, :], r.n1[rows, :]
        dr1 = norm_back(df, n, r.rst[rows, 0:1], r.lb[6:7, :])
        de = dr1.astype(BF16)
        r.n2[rows, :] = dr1
        r.de[rows, :] = de
        r.sloc[3:4, :] += sum0(df)
        r.sloc[6:7, :] += sum0(df * n)
        r.sloc[2:3, :] += sum0(de.astype(F32))

    def out_back(de):
        return dot_bt(de[:, 0:W], weight(0, 3)) + dot_bt(de[:, W:D], weight(1, 3))

    blocks(norm_one)
    loop(6, raise_up, 4)
    cross.attention()
    loop(8, raise_up, 6)
    def pack(value):
        n = value.shape[1] // 2
        row = lax.broadcasted_iota(jnp.int32, (8, n), 0)
        both = jnp.where(row < 3, value[:, :n], pltpu.roll(value[:, n:], 3, 0))
        return jnp.where(row < 6, both, 0.0)

    r.hgs[...] = jnp.zeros((32, 8, 128), BF16)
    hidden, slope = r.hg[...].astype(F32), r.hgp[...]
    for t in range(32):
        part = slice(96 * t, 96 * t + 96)
        both = jnp.concatenate([hidden[:, part], slope[:, part]], axis=1)
        r.hgs[t, :, 0:96] = pack(both).astype(BF16)
    r.hfp[...] = pack(r.hf[...].astype(F32)).astype(BF16)
    cross.first_norm()
    lower(0)
    lower(1)
    cross.mlp()
    loop(6, norm_two)
    loop(4, down_grad)
    cross.second_norm()
    loop(8, down_grad, 4)
    loop(4, red.to_sibling)
    loop(2, middle)
    cross.mlp_back()
    middle(2)
    loop(4, red.step_a)
    loop(5, middle, 3)
    cross.first_norm_back()
    loop(8, middle, 5)
    cross.attention_back()
    loop(4, red.step_b)
    blocks(norm_one_back)
    r.do[...] = out_back(r.de[...]).astype(BF16)
    loop(6, red.step_a, 4)
    cross.grads()
    cross.scatter()
    r.dx[...] = jnp.where(row8 < 3, cross.finish(), 0.0)

    dy0, hn2 = r.dx[...], r.hn[1]
    dr2 = norm_back(dy0, hn2, r.hrst[1, :, 0:1], r.lb[7:8, :])
    r.hdd[...] = dr2.astype(BF16)
    r.hdf[...] = dr2
    r.hdp[...] = pack(dr2).astype(BF16)
    loop(16, lambda t: send_to(me, 2 * t + c, r.hdp, r.hfd.at[1, me // 2, c], r.hs.at[1], r.hr.at[1]))
    loop(32, lambda t: send_to(me, t, r.hgs.at[t], r.hgr.at[me], r.hs.at[0], r.hr.at[0]))
    loop(16, lambda t: send_to(me, 2 * t + c, r.hfp, r.hfd.at[0, me // 2, c], r.hs.at[1], r.hr.at[1]))
    loop(8, red.step_a, 6)
    r.sloc[5:6, :] += sum0(dy0)
    r.sloc[7:8, :] += sum0(dy0 * hn2)
    r.sloc[4:5, :] += sum0(r.hdd[...].astype(F32))

    def head_middle(i):
        for cc in range(2):
            b = 2 * i + cc
            part = col(b)
            dg = dot_bt(r.hdd[:, 0:W], down_block(b, 0)) + dot_bt(r.hdd[:, W:D], down_block(b, 1))
            du = (dg * r.hgp[:, part]).astype(BF16)
            r.dcl[:, part] += sum0(du.astype(F32))
            r.hdf[...] += dot_bt(du, weight(cc, 4 + i))

    loop(4, head_middle)
    ring.drain()
    for t in (ring.other, ring.seg(True, 1), ring.seg(True, 3), ring.seg(False, 1), ring.seg(False, 3)):
        pl.semaphore_signal(r.free, inc=1, device_id={"seg": t}, device_id_type=MESH)
    df, hn1 = r.hdf[...], r.hn[0]
    dr1 = norm_back(df, hn1, r.hrst[0, :, 0:1], r.lb[6:7, :])
    de = dr1.astype(BF16)
    r.sloc[3:4, :] += sum0(df)
    r.sloc[6:7, :] += sum0(df * hn1)
    r.sloc[2:3, :] += sum0(de.astype(F32))
    do = out_back(de)
    y = cross.output_rows()
    row16 = lax.broadcasted_iota(jnp.int32, (16, D), 0)

    def put(ref, s, value):
        rows = slice(128 * s, 128 * s + 16)
        ref[rows, :] = jnp.where(row16 == 0, value[s : s + 1, :], ref[rows, :].astype(F32)).astype(ref.dtype)

    for s in range(3):
        put(r.lo, s, y)
        put(r.n2, s, dr1)
        put(r.de, s, de.astype(F32))
        put(r.do, s, do)
    pltpu.make_async_copy(r.lo, r.lo_h, r.done.at[0]).start()

    def attend_back(s):
        rows = pl.ds(pl.multiple_of(s * 128, 128), 128)
        for p in range(6):
            part = slice(128 * p, 128 * (p + 1))
            q, k, v = r.qkvv[0, rows, part], r.qkvv[1, rows, part], r.qkvv[2, rows, part]
            do = two_heads(r.do[rows, part])
            w = r.aw[s, p]
            ds = softmax_back(w.astype(F32), dot_bt(do, v)).astype(BF16)
            r.qkvv[0, rows, part] = (side_by_side(dot(ds, k)) * 0.125).astype(BF16)
            r.qkvv[1, rows, part] = (dot_at(ds, two_heads(q)) * 0.125).astype(BF16)
            r.qkvv[2, rows, part] = dot_at(w, do).astype(BF16)

    attend_back(0)
    loop(6, red.step_b, 4)
    pl.semaphore_wait(r.free, 5)
    for cc in range(2):
        again.gb[(cc + c) % 2, 0] = dot_at(r.mix[...], r.de[:, cc * W : (cc + 1) * W]).astype(BF16).reshape(4, 4, 48, W)
    red2.to_sibling(0)
    attend_back(1)
    cross.planes(red)
    attend_back(2)
    loop(8, red.step_b, 6)

    def qkv_grad(i):
        for cc in range(2):
            part = slice(cc * W, (cc + 1) * W)
            again.gb[(cc + c) % 2, i + 1] = dot_at(r.tok[...], r.qkvv[i, :, part]).astype(BF16).reshape(4, 4, 48, W)

    def qkv_out(i):
        qkv_grad(i)
        red2.to_sibling(i + 1)

    loop(3, qkv_out)
    loop(4, red2.step_a)
    take(r.hfd.at[:, :, 0], r.hr.at[1])
    rcopy(r.hfd.at[:, :, c], r.hfd.at[:, :, c], r.hs.at[2], r.hr.at[2], ring.other).start()
    loop(4, red.step_c)

    def second_round(step):
        loop(4, step)

    sf = r.sf
    sf[...] = jnp.zeros((96, D), F32)
    sf[0:8, :] = r.sloc[...]
    sf[0:1, :] = sum0(r.qkvv[0].astype(F32))
    sf[1:2, :] = sum0(r.qkvv[2].astype(F32))
    sf[8:16, :] = r.small[...]
    for i in range(4):
        sf[16 + i : 17 + i, :] = r.dcl[:, D * i : D * (i + 1)]
    own = jnp.concatenate([r.dc[0:1, :], jnp.zeros((1, D - 128), F32)], axis=1)
    own = pltpu.roll(own, 96 * (me % 8), 1)
    sf[pl.ds(20 + me // 8, 1), :] = own
    line = lax.broadcasted_iota(jnp.int32, (64, D), 0)
    for s in range(3):
        _, place = slot_layout(r.doc, (64, D), jnp.full((64, D), me * 3 + s, jnp.int32))
        sf[24:88, :] += jnp.where(line == place, r.dx[s : s + 1, :], 0.0)
    r.s0[...] = sf[...].reshape(12, 8, D).astype(BF16)
    xs, xr = r.xs, r.xr
    loop(12, lambda k: send_to(me, owner_seg(k), r.s0.at[k], r.sg.at[me], xs.at[0], xr.at[0]))

    loop(8, red.step_c, 4)
    take(r.hgr, r.hr.at[0])
    take(r.hfd.at[:, :, 0], r.hr.at[2])
    hfa, dda = [r.hfd[i].astype(F32).reshape(256, W).astype(BF16) for i in range(2)]
    both = flat8(r.hgr[...])
    line = lax.broadcasted_iota(jnp.int32, (256, 128), 0) % 8

    def low(v):
        return jnp.where(line[:, : v.shape[1]] < 3, v, 0.0)

    left, right = dot_bt(dda, r.down[:, 0:W]), dot_bt(dda, r.down[:, W:D])
    du = low((left + pltpu.roll(right, 253, 0)) * pltpu.roll(both, 253, 0)[:, 0:96])
    share_up = [dot_at(hfa, v.astype(BF16)) for v in (du, pltpu.roll(du, 3, 0))]
    r.pcu[:, :, 0:96] = jnp.concatenate(share_up, axis=0).reshape(32, 24, 96).astype(BF16)
    core = (me // 4) % 2

    def share(t):
        send_to(me, t - t % 2 + core, r.pcu.at[t], r.cu.at[t % 2, (me // 8) * 4 + me % 4], r.ks.at[3], r.kr.at[3])

    loop(32, share)
    loop(4, red.step_d)
    hidden = low(both)
    down_share = [dot_at(v.astype(BF16), dda)[0:96] for v in (hidden, pltpu.roll(hidden, 3, 0))]
    for n in range(8):
        j, h = n // 2, n % 2
        top = (j % 2) * 48 + 24 * h
        piece = down_share[j // 2][top : top + 24]
        r.zp[0, n] = (r.zp[0, n].astype(F32) + piece).astype(BF16)
    red.z_send(0)
    cross.planes_sum(red)
    second_round(red2.step_b)
    loop(8, red.step_d, 4)

    @pl.when(is_owner)
    def _():
        take(r.sg, xr.at[0])
        r.sm1[...] = jnp.sum(r.sg[...].astype(F32), axis=0).astype(BF16)
        red.peers(lambda zz: zcopy(r.sm1, r.sz.at[z], xs.at[3], xr.at[3], zz, me).start())
        pltpu.make_async_copy(r.sm1, r.sz.at[z], xr.at[3]).start()

    take(r.cu, r.kr.at[3])
    for n in range(8):
        m, h = n // 2, n % 2
        for q in range(4):
            r.zc[:, 96 * q : 96 * q + 96] = r.cu[h, 4 * m + q].astype(F32)[:, 0:96]
        r.zp[1, n] = (r.zp[1, n].astype(F32) + r.zc[...]).astype(BF16)
    red.z_send(1)
    second_round(red2.step_c)
    red.z_sum(0)

    def token_grad(i):
        acc = dot_bt(r.qkvv[i, :, 0:W], weight(0, i))
        r.tg[...] += acc + dot_bt(r.qkvv[i, :, W : 2 * W], weight(1, i))

    token_grad(0)
    second_round(red2.step_d)
    red.z_send(2)
    token_grad(1)

    @pl.when(is_owner)
    def _():
        take(r.sz.at[pl.ds(0, 8)], xr.at[3])
        r.sm2[...] = jnp.sum(r.sz[0:8].astype(F32), axis=0).astype(BF16)
        loop(32, lambda t: send_to(me, t, r.sm2, r.osm.at[me // 2], xs.at[6], xr.at[6]))

    red.z_sum(1)
    token_grad(2)
    pltpu.make_async_copy(r.tg, r.tg_h, r.done.at[1]).start()
    red.z_sum(2)
    for g, ref in ((0, r.fd), (1, r.fa.at[pl.ds(8, 8)]), (2, r.fa.at[pl.ds(0, 8)])):
        take(ref, r.zsr.at[g, 1])
    take(r.osm, xr.at[6])

    take(r.lo, r.done.at[0])
    take(r.tg, r.done.at[1])

    cross.end()
    cross.drain()
    red2.sent(4)
    red.sent(8)
    red.z_sent()
    for i, (src, dst) in enumerate(swaps):
        take(src, r.sib_s.at[i])
    take(r.smg.at[pl.ds(0, 15), 0], r.sm_s.at[0])
    take(r.smg.at[:, 0], r.sm_s.at[1])
    take(r.hgr.at[pl.ds(0, 31)], r.hs.at[0])
    take(r.hfd.at[:, pl.ds(0, 15), 0], r.hs.at[1])
    take(r.hfd.at[:, :, 0], r.hs.at[2])

    @pl.when(core == c)
    def _():
        take(r.pcu.at[pl.ds(0, 30)], r.ks.at[3])

    @pl.when(core != c)
    def _():
        take(r.pcu, r.ks.at[3])

    @pl.when(is_owner)
    def _():
        take(r.sg.at[pl.ds(0, 11)], xs.at[0])
        take(r.sz.at[pl.ds(0, 7)], xs.at[3])
        take(r.sz.at[pl.ds(0, 31)], xs.at[6])

    @pl.when(jnp.logical_not(is_owner))
    def _():
        take(r.sg.at[pl.ds(0, 12)], xs.at[0])


FORMAT_OUT = dict(
    lo_o=((ROWS, D), BF16),
    tg_o=((ROWS, D), F32),
    oq=((24, 3 * D), F32),
    oo=((24, D), F32),
    ou=((24, FF), F32),
    od=((96, D), F32),
    ob=((6, 24), F32),
    ouv=((1, 96), F32),
    og=((2, 24), F32),
    xoq=((24, 3 * D), F32),
    xoo=((24, D), F32),
    xou=((24, FF), F32),
    xod=((96, D), F32),
    xob=((6, 24), F32),
    xouv=((1, 96), F32),
    xog=((2, 24), F32),
    opos=((2, D), F32),
)


def format_kernel(*refs):
    r = fields(list(F_OUT) + list(FORMAT_OUT), refs)
    me = lax.axis_index("seg")
    r.lo_o[...] = r.lo_h[...]
    r.tg_o[...] = r.tg_h[...]
    for p in range(6):
        for j in range(3):
            r.xoq[:, D * j + 128 * p : D * j + 128 * (p + 1)] = r.cf[p // 2, p % 2, :, 128 * j : 128 * (j + 1)].astype(F32)
    for i in range(2):
        r.xoo[:, W * i : W * (i + 1)] = r.cf[3, i].astype(F32)
        for n in range(4):
            m = 8 + 4 * i + n
            r.xod[24 * n : 24 * (n + 1), W * i : W * (i + 1)] = r.cf[m // 2, m % 2].astype(F32)
    for t in range(32):
        r.xou[:, 96 * t : 96 * t + 96] = r.uf[t // 4, t % 4].astype(F32)[:, 0:96]
    for n in range(8):
        j, h = n // 2, n % 2
        top = (j % 2) * 48 + 24 * h
        r.od[top : top + 24, (j // 2) * W : (j // 2 + 1) * W] = r.fd[n].astype(F32)
    for u in range(8, 16):
        r.ou[:, W * (u - 8) : W * (u - 7)] = r.fa[u].astype(F32)
    ours = pltpu.roll(r.osm[0:2].astype(F32).reshape(16, D), (D - 24 * me) % D, 1)
    r.ob[...] = ours[0:6, 0:24]
    r.og[...] = ours[6:8, 0:24]
    r.xob[...] = ours[8:14, 0:24]
    r.xog[...] = ours[14:16, 0:24]
    ups = pltpu.roll(r.osm[2].astype(F32), (D - 96 * (me % 8)) % D, 1)
    line = lax.broadcasted_iota(jnp.int32, (8, D), 0)
    r.ouv[...] = sum0(jnp.where(line == me // 8, ups, 0.0))[:, 0:96]
    r.xouv[...] = sum0(jnp.where(line == 4 + me // 8, ups, 0.0))[:, 0:96]
    r.opos[...] = pltpu.roll(r.osm[3 + me // 4].astype(F32), (8 - 2 * (me % 4)) % 8, 0)[0:2]
    for u in range(8):
        if u < 6:
            r.oq[:, W * u : W * (u + 1)] = r.fa[u].astype(F32)
        else:
            r.oo[:, W * (u - 6) : W * (u - 5)] = r.fa[u].astype(F32)


def call(kernel, name, ins, outs, scratch, cid, args):
    vm, smem = pl.BlockSpec(memory_space=pltpu.VMEM), pl.BlockSpec(memory_space=pltpu.SMEM)
    hbm = pl.BlockSpec(memory_space=pl.ANY)
    return pl.pallas_call(
        kernel,
        out_shape=tuple(jax.ShapeDtypeStruct(s, t) for s, t in outs.values()),
        in_specs=[smem if n == "doc" else vm for n in ins],
        out_specs=tuple(hbm if n in ("lo_h", "tg_h") else vm for n in outs),
        scratch_shapes=list(scratch.values()),
        compiler_params=pltpu.CompilerParams(
            collective_id=cid, has_side_effects=cid is not None, vmem_limit_bytes=63 << 20
        ),
        name=name,
    )(*args)


def shards(tokens, doc, qkv, out, up, down, bias, upbias, gains, cqkv, cout, cup, cdown, cbias, cupbias, cgains, pos, cot):
    made = call(
        layer_kernel, "layer", F_IN, F_OUT, F_SCR, 0,
        (tokens, cot, qkv, out, up, down, bias, upbias.reshape(1, 96), gains, cqkv, cout, cup, cdown, cbias,
         cupbias.reshape(1, 96), cgains, pos, doc),
    )
    out = dict(zip(FORMAT_OUT, call(format_kernel, "format", list(F_OUT), FORMAT_OUT, {}, None, made)))
    out["ouv"], out["xouv"] = out["ouv"].reshape(96), out["xouv"].reshape(96)
    return tuple(out.values())


def solution(mesh):
    both, seg, cols, flat = P(("grp", "seg"), None), P("seg", None), P(None, "seg"), P("seg")
    weights = (seg, seg, seg, seg, cols, flat, cols)
    in_specs = (both, P("grp", None)) + weights + weights + (seg, both)
    out_specs = (both, both) + weights + weights + (seg,)
    return jax.shard_map(shards, mesh=mesh, in_specs=in_specs, out_specs=out_specs, check_vma=False)
```
